32 devices in a mesh: dp: 8 (over z, y), tp: 4 (over x, core).
Axes of the slice: x: 2, y: 2, z: 4, core: 2. Of those that a mesh axis runs over, the one named last changes fastest.
Arguments:
- layer_input: bfloat16 [16384, 768], P('dp'), may hold values from -6 to 6
- lengths: int32 [32], P('dp'), may hold values from 1 to 512, as said below
- query_weight: bfloat16 [768, 768], P(None, 'tp'), may hold values from -0.21875 to 0.21875
- query_bias: float32 [768], P('tp'), may hold values from -3 to 3
- key_weight: bfloat16 [768, 768], P(None, 'tp'), may hold values from -0.21875 to 0.21875
- value_weight: bfloat16 [768, 768], P(None, 'tp'), may hold values from -0.21875 to 0.21875
- value_bias: float32 [768], P('tp'), may hold values from -3 to 3
- out_weight: bfloat16 [768, 768], P('tp'), may hold values from -1.5 to 1.5
- out_bias: float32 [768], replicated, may hold values from -3 to 3
- first_gain: float32 [768], replicated, may hold values from 0.25 to 1.75
- first_shift: float32 [768], replicated, may hold values from -3 to 3
- inner_weight: bfloat16 [768, 3072], P(None, 'tp'), may hold values from -0.21875 to 0.21875
- inner_bias: float32 [3072], P('tp'), may hold values from -3 to 3
- outer_weight: bfloat16 [3072, 768], P('tp'), may hold values from -0.109375 to 0.109375
- outer_bias: float32 [768], replicated, may hold values from -3 to 3
- second_gain: float32 [768], replicated, may hold values from 0.25 to 1.75
- second_shift: float32 [768], replicated, may hold values from -3 to 3
- cotangent: bfloat16 [16384, 768], P('dp'), may hold values from -6 to 6
Outputs:
- layer_output: bfloat16 [16384, 768], P(('dp', 'tp'))
- input_grad: float32 [16384, 768], P(('dp', 'tp'))
- query_weight_grad: float32 [768, 768], P(None, 'tp')
- query_bias_grad: float32 [768], P('tp')
- key_weight_grad: float32 [768, 768], P(None, 'tp')
- value_weight_grad: float32 [768, 768], P(None, 'tp')
- value_bias_grad: float32 [768], P('tp')
- out_weight_grad: float32 [768, 768], P('tp')
- out_bias_grad: float32 [768], replicated
- first_gain_grad: float32 [768], replicated
- first_shift_grad: float32 [768], replicated
- inner_weight_grad: float32 [768, 3072], P(None, 'tp')
- inner_bias_grad: float32 [3072], P('tp')
- outer_weight_grad: float32 [3072, 768], P('tp')
- outer_bias_grad: float32 [768], replicated
- second_gain_grad: float32 [768], replicated
- second_shift_grad: float32 [768], replicated
The draws below stay inside these ranges and needn't reach their ends.
Inputs may be any that keep to these rules, and one draw needn't show every extreme that they name: lengths[s] is the number of real tokens of sequence s, which fill its first slots; most sequences are short, and some sequence fills all 512 slots.
All inputs are finite; a program needn't handle non-finite values.
Results may differ from the reference program's by a relative error of at most 0.013.
Values may be sent and summed in bfloat16 or wider, within the bound.
No kernel may reach another device: no remote copies, remote signals or barrier semaphores. Data moves between devices by JAX's collectives and lax.ppermute only.
A program may use at most 128 MiB of HBM per device.

```python
import math
import jax
import jax.numpy as jnp
from jax import lax

D = 768
HEADS = 12
HD = 64
FF = 3072
SEQ_LEN = 512
SEQS = 32
TOKENS = 16384


def draw_lengths(key, part):
    key = jax.random.fold_in(key, 7)
    first, second, third, fourth = jax.random.split(key, 4)
    short_cap = min(150, SEQ_LEN)
    short_len = jax.random.randint(first, (SEQS,), 1, short_cap + 1)
    long_len = jax.random.randint(second, (SEQS,), short_cap, SEQ_LEN + 1)
    picked = jax.random.randint(third, (SEQS,), 0, 8) == 0
    drawn = jnp.where(picked, long_len, short_len)
    chosen = jax.random.randint(fourth, (), 0, SEQS)
    return drawn.at[chosen].set(SEQ_LEN).astype(jnp.int32)


def levels(key, extent, cuts, smallest, top_value):
    level = 1.0
    for dim, blocks in cuts:
        heights = jax.random.uniform(jax.random.fold_in(jax.random.fold_in(key, 6), dim), (blocks,), jnp.float32, smallest / len(cuts), top_value / len(cuts))
        level = level * jnp.repeat(jnp.exp(heights), extent[dim] // blocks).reshape((-1,) + (1,) * (len(extent) - 1 - dim))
    return level


def centred(stream_key, dims, scale, bound, cuts=(), kind=jnp.bfloat16):
    array = jax.random.normal(stream_key, dims, jnp.float32) * scale
    if len(cuts) > 0:
        array = levels(stream_key, dims, cuts, -0.22, 0.18) * array
    return jnp.clip(array, min=-bound, max=bound).astype(kind)


def setup_inputs(seed: int = 0) -> dict:
    key_of = jax.random.split(jax.random.key(seed), 19)
    return {
        "layer_input": centred(key_of[0], (TOKENS, D), 1.0, 6.0, ((0, 8),)),
        "lengths": draw_lengths(jax.random.fold_in(key_of[18], 71), 0),
        "query_weight": centred(key_of[2], (D, D), D ** -0.5, 0.21875, ((1, 4),)),
        "query_bias": centred(key_of[3], (D,), 0.5, 3.0, ((0, 4),), jnp.float32),
        "key_weight": centred(key_of[4], (D, D), D ** -0.5, 0.21875, ((1, 4),)),
        "value_weight": centred(key_of[5], (D, D), D ** -0.5, 0.21875, ((1, 4),)),
        "value_bias": centred(key_of[6], (D,), 0.5, 3.0, ((0, 4),), jnp.float32),
        "out_weight": centred(key_of[7], (D, D), (D // 48) ** -0.5, 1.5, ((0, 4),)),
        "out_bias": centred(key_of[8], (D,), 0.5, 3.0, (), jnp.float32),
        "first_gain": jnp.clip(1.0 + 0.15 * jax.random.normal(key_of[9], (D,), jnp.float32), 0.25, 1.75),
        "first_shift": centred(key_of[10], (D,), 0.5, 3.0, (), jnp.float32),
        "inner_weight": centred(key_of[11], (D, FF), D ** -0.5, 0.21875, ((1, 4),)),
        "inner_bias": centred(key_of[12], (FF,), 0.5, 3.0, ((0, 4),), jnp.float32),
        "outer_weight": centred(key_of[13], (FF, D), FF ** -0.5, 0.109375, ((0, 4),)),
        "outer_bias": centred(key_of[14], (D,), 0.5, 3.0, (), jnp.float32),
        "second_gain": jnp.clip(1.0 + 0.15 * jax.random.normal(key_of[15], (D,), jnp.float32), 0.25, 1.75),
        "second_shift": centred(key_of[16], (D,), 0.5, 3.0, (), jnp.float32),
        "cotangent": centred(key_of[17], (TOKENS, D), 1.0, 6.0, ((0, 8),)),
    }


@jax.custom_vjp
def low(v):
    return lax.optimization_barrier(v.astype(jnp.bfloat16)).astype(jnp.float32)

@jax.custom_vjp
def low_back(v):
    return v

def low_keep(v):
    return (low(v), None)

def low_pass(kept, grad):
    return (grad,)

def back_keep(v):
    return (v, None)

def back_low(kept, grad):
    return (low(grad),)
low.defvjp(low_keep, low_pass)
low_back.defvjp(back_keep, back_low)
epsilon = 1e-05

def product(left, right):
    return jnp.dot(left, right, precision=lax.Precision.HIGHEST)

def layer_norm(values, scaling, offset):
    average = lax.optimization_barrier(jnp.mean(values, axis=-1, keepdims=True))
    centered = values - average
    spread = lax.optimization_barrier(jnp.mean(centered * centered, axis=-1, keepdims=True))
    return centered * lax.rsqrt(spread + epsilon) * scaling + offset

def attend(pieces):
    queries, keys, values, length = pieces
    factor = HD ** (-0.5)
    scores = low_back(factor * jnp.einsum('qhd,khd->hqk', queries, keys, precision=lax.Precision.HIGHEST))
    visible = jnp.arange(SEQ_LEN, dtype=jnp.int32) < length
    scores = jnp.where(visible[None, None, :], scores, -1e+30)
    row_max = lax.optimization_barrier(jnp.max(scores, axis=-1, keepdims=True))
    log_total = row_max + jnp.log(lax.optimization_barrier(jnp.sum(jnp.exp(scores - row_max), axis=-1, keepdims=True)))
    attn_probs = jnp.exp(scores - log_total)
    context = jnp.einsum('hqk,khd->qhd', low(attn_probs), values, precision=lax.Precision.HIGHEST)
    return low_back(low(context))

def forward(params, inputs, block_lengths):
    query_weight, query_bias, key_weight, value_weight, value_bias, out_weight, out_bias, first_gain, first_shift, inner_weight, inner_bias, outer_weight, outer_bias, second_gain, second_shift = params
    row_count = inputs.shape[0]
    block_shape = (row_count // SEQ_LEN, SEQ_LEN, HEADS, HD)
    queries = low_back(low(product(inputs, query_weight) + query_bias))
    keys = low_back(low(product(inputs, key_weight)))
    values = low_back(low(product(inputs, value_weight) + value_bias))
    context = lax.map(jax.checkpoint(attend), (queries.reshape(block_shape), keys.reshape(block_shape), values.reshape(block_shape), block_lengths))
    context = context.reshape(row_count, D)
    branch = low_back(product(context, out_weight))
    normed = layer_norm(inputs + branch + out_bias, first_gain, first_shift)
    hidden = low_back(product(low(normed), inner_weight) + inner_bias)
    active = low(jax.nn.gelu(hidden, approximate=False))
    result = low_back(product(active, outer_weight))
    return layer_norm(normed + result + outer_bias, second_gain, second_shift)

def reference(layer_input, lengths, query_weight, query_bias, key_weight, value_weight, value_bias, out_weight, out_bias, first_gain, first_shift, inner_weight, inner_bias, outer_weight, outer_bias, second_gain, second_shift, cotangent):
    params = tuple((p.astype(jnp.float32) for p in (query_weight, query_bias, key_weight, value_weight, value_bias, out_weight, out_bias, first_gain, first_shift, inner_weight, inner_bias, outer_weight, outer_bias, second_gain, second_shift)))
    group = math.gcd(SEQS, max(1, 4096 // SEQ_LEN))
    blocks = SEQS // group
    input_blocks = layer_input.astype(jnp.float32).reshape(blocks, group * SEQ_LEN, D)
    grad_blocks = cotangent.astype(jnp.float32).reshape(blocks, group * SEQ_LEN, D)
    length_blocks = lengths.reshape(blocks, group)

    def scan_step(accumulated, pieces):
        inputs, grads_out, block_lengths = pieces
        outcome, pullback = jax.vjp(lambda p, v: forward(p, v, block_lengths), params, inputs)
        param_grads, input_grads = pullback(grads_out)
        accumulated = jax.tree.map(lambda a, b: a + b, accumulated, param_grads)
        return (accumulated, (outcome.astype(jnp.bfloat16), input_grads))
    start_sums = jax.tree.map(jnp.zeros_like, params)
    totals, (outputs, input_grads) = lax.scan(scan_step, start_sums, (input_blocks, grad_blocks, length_blocks))
    layer_output = outputs.reshape(TOKENS, D)
    input_grad = input_grads.reshape(TOKENS, D)
    return (layer_output, input_grad, totals[0], totals[1], totals[2], totals[3], totals[4], totals[5], totals[6], totals[7], totals[8], totals[9], totals[10], totals[11], totals[12], totals[13], totals[14])
```

```python
import jax
import jax.numpy as jnp
from jax import lax
from jax.sharding import PartitionSpec as P

HD = 64
EPSILON = 1e-05
BF16 = jnp.bfloat16
F32 = jnp.float32


def dot(left, right, left_dim=1, right_dim=0):
    return lax.dot_general(
        left, right, (((left_dim,), (right_dim,)), ((), ())), preferred_element_type=F32
    )


def exchange(array, dp_bits, tp_bits):
    dp_size, tp_size = lax.axis_size("dp"), lax.axis_size("tp")
    pairs = [
        (d * tp_size + t, (d ^ dp_bits) * tp_size + (t ^ tp_bits))
        for d in range(dp_size)
        for t in range(tp_size)
    ]
    return lax.ppermute(array, ("dp", "tp"), pairs)


def norm_forward(values, gain, shift):
    average = jnp.mean(values, axis=-1, keepdims=True)
    centered = values - average
    spread = jnp.mean(centered * centered, axis=-1, keepdims=True)
    scale = lax.rsqrt(spread + EPSILON)
    rows = centered * scale
    return rows * gain + shift, rows, scale


def norm_backward(grad, rows, scale, gain):
    e = grad * gain
    first = jnp.mean(e, axis=-1, keepdims=True)
    second = jnp.mean(e * rows, axis=-1, keepdims=True)
    return scale * (e - first - rows * second)


def pick(flag, first, second):
    return jnp.where(flag, first, second)


def attention_forward(queries, keys, values, length):
    rows, width = queries.shape
    heads = width // HD
    q, k, v = (a.reshape(rows, heads, HD) for a in (queries, keys, values))
    raw = jnp.einsum("qhd,khd->hqk", q, k, preferred_element_type=F32) * HD**-0.5
    position = jnp.arange(rows, dtype=jnp.int32)
    scores = jnp.where((position < length)[None, None, :], raw, -1e30)
    row_max = jnp.max(scores, axis=-1, keepdims=True)
    log_total = row_max + jnp.log(jnp.sum(jnp.exp(scores - row_max), axis=-1, keepdims=True))
    probs = jnp.exp(scores - log_total)
    context = jnp.einsum("hqk,khd->qhd", probs.astype(BF16), v, preferred_element_type=F32)
    return context.astype(BF16).reshape(rows, width), log_total


def attention_backward(queries, keys, values, context_grad, length, log_total):
    rows, width = queries.shape
    heads = width // HD
    q, k, v, g = (a.reshape(rows, heads, HD) for a in (queries, keys, values, context_grad))
    raw = jnp.einsum("qhd,khd->hqk", q, k, preferred_element_type=F32) * HD**-0.5
    position = jnp.arange(rows, dtype=jnp.int32)
    scores = jnp.where((position < length)[None, None, :], raw, -1e30)
    probs = jnp.exp(scores - log_total)
    v_grad = jnp.einsum("hqk,qhd->khd", probs.astype(BF16), g, preferred_element_type=F32)
    prob_grad = jnp.einsum("qhd,khd->hqk", g, v, preferred_element_type=F32)
    inner = jnp.sum(probs * prob_grad, axis=-1, keepdims=True)
    score_grad = (probs * (prob_grad - inner)).astype(BF16)
    q_grad = jnp.einsum("hqk,khd->qhd", score_grad, k, preferred_element_type=F32) * HD**-0.5
    k_grad = jnp.einsum("hqk,qhd->khd", score_grad, q, preferred_element_type=F32) * HD**-0.5
    return tuple(a.astype(BF16).reshape(rows, width) for a in (q_grad, k_grad, v_grad))


def add(*terms):
    total = terms[0].astype(F32)
    for term in terms[1:]:
        total = total + term.astype(F32)
    return total


def reduce_grad(parts, odd, z):
    rows, columns = parts[0].shape
    dp_size = lax.axis_size("dp")
    got1 = exchange(parts[1], 0, 1)
    got3 = exchange(parts[3], 0, 1)
    across = add(parts[2], got3).astype(BF16)
    got2 = exchange(across, 0, 2)
    half = rows // 2
    quarter = half // 4

    def side(first):
        cut = lambda a: lax.dynamic_slice_in_dim(a, first, half, 0)
        return add(cut(parts[0]), cut(got1), cut(got2)).astype(BF16)

    keep, send = side(odd * half), side((1 - odd) * half)
    gathered = exchange(send, 1, 0)
    kept = add(keep, gathered).astype(BF16)
    cut = lambda a, k: lax.dynamic_slice_in_dim(a, k * quarter, quarter, 0)
    got = [exchange(cut(kept, z ^ k), 2 * k, 0) for k in (1, 2, 3)]
    mine = add(cut(kept, z), *got).astype(BF16)
    bit = 8
    while bit < dp_size:
        mine = add(mine, exchange(mine, bit, 0)).astype(BF16)
        bit *= 2
    whole = jnp.zeros((half, columns), BF16)
    whole = lax.dynamic_update_slice_in_dim(whole, mine, z * quarter, 0)
    for k in (1, 2, 3):
        whole = lax.dynamic_update_slice_in_dim(
            whole, exchange(mine, 2 * k, 0), (z ^ k) * quarter, 0
        )
    other = exchange(whole, 1, 0)
    is_odd = odd == 1
    return jnp.concatenate([pick(is_odd, other, whole), pick(is_odd, whole, other)], axis=0).astype(
        F32
    )


def reduce_small(slots, common):
    width = slots[0].shape[0]
    got = exchange(jnp.concatenate([slots[1], slots[3], common]), 0, 1)
    own, across = slots[0] + got[:width], slots[2] + got[width : 2 * width]
    common = common + got[2 * width :]
    got = exchange(jnp.concatenate([across, common]), 0, 2)
    total = jnp.concatenate([own, common]) + got
    bit = 1
    while bit < lax.axis_size("dp"):
        total = total + exchange(total, bit, 0)
        bit *= 2
    return total[:width], total[width:]


def on_device(
    layer_input,
    lengths,
    query_weight,
    query_bias,
    key_weight,
    value_weight,
    value_bias,
    out_weight,
    out_bias,
    first_gain,
    first_shift,
    inner_weight,
    inner_bias,
    outer_weight,
    outer_bias,
    second_gain,
    second_shift,
    cotangent,
):
    slots = lax.axis_size("tp")
    rows = layer_input.shape[0] // slots
    width = query_weight.shape[1]
    tp, dp = lax.axis_index("tp"), lax.axis_index("dp")
    odd, z = dp & 1, (dp >> 1) & 3
    is_odd = odd == 1
    inputs = lax.dynamic_slice_in_dim(layer_input, tp * rows, rows, 0)
    own_grad = lax.dynamic_slice_in_dim(cotangent, tp * rows, rows, 0).astype(F32)
    length = lax.dynamic_index_in_dim(lengths, tp, 0, keepdims=False)

    def gather(first, second):
        near = exchange(pick(is_odd, second, first), 0, 2)
        far = exchange(near, 1, 0)
        first2, second2 = pick(is_odd, far, near), pick(is_odd, near, far)
        return (
            [first, exchange(first, 0, 1), first2, exchange(first2, 0, 1)],
            [second, exchange(second, 0, 1), second2, exchange(second2, 0, 1)],
        )

    qk, vo = gather(
        jnp.concatenate([query_weight.T, key_weight.T]),
        jnp.concatenate([value_weight.T, out_weight]),
    )
    inner, outer = gather(inner_weight, outer_weight)
    biases = jnp.concatenate([query_bias, value_bias, inner_bias])
    bias1 = exchange(biases, 0, 1)
    bias23 = exchange(jnp.stack([biases, bias1]), 0, 2)
    bias = [biases, bias1, bias23[0], bias23[1]]

    inputs_full = inputs.astype(F32)
    kept = []
    first_sum = inputs_full + out_bias
    for pair in ((0, 1), (2, 3)):
        both = lambda blocks, low: jnp.concatenate(
            [blocks[s][low * width : (low + 1) * width] for s in pair]
        )
        wq, wk, wv, wo = both(qk, 0), both(qk, 1), both(vo, 0), both(vo, 1)
        bq = jnp.concatenate([bias[s][:width] for s in pair])
        bv = jnp.concatenate([bias[s][width : 2 * width] for s in pair])
        queries = (dot(inputs, wq, 1, 1) + bq).astype(BF16)
        keys = dot(inputs, wk, 1, 1).astype(BF16)
        values = (dot(inputs, wv, 1, 1) + bv).astype(BF16)
        context, log_total = attention_forward(queries, keys, values, length)
        first_sum = first_sum + dot(context, wo)
        kept.append((queries, keys, values, context, log_total, wq, wk, wv, wo))
    normed, first_rows, first_scale = norm_forward(first_sum, first_gain, first_shift)
    normed_low = normed.astype(BF16)

    second_sum = normed + outer_bias
    active, slope = [], []
    for s in range(slots):
        hidden = dot(normed_low, inner[s]) + bias[s][2 * width :]
        half_erf = 0.5 * (1.0 + lax.erf(hidden * 0.5**0.5))
        active.append((hidden * half_erf).astype(BF16))
        slope.append(
            (half_erf + hidden * jnp.exp(-0.5 * hidden * hidden) * 0.3989422804014327).astype(BF16)
        )
        second_sum = second_sum + dot(active[s], outer[s])
    output, second_rows, second_scale = norm_forward(second_sum, second_gain, second_shift)
    layer_output = output.astype(BF16)
    second_gain_grad = jnp.sum(own_grad * second_rows, axis=0)
    second_shift_grad = jnp.sum(own_grad, axis=0)
    second_grad = norm_backward(own_grad, second_rows, second_scale, second_gain)
    outer_bias_grad = jnp.sum(second_grad, axis=0)
    result_grad = second_grad.astype(BF16)

    order = (1, 3, 2, 0)
    outer_parts, inner_parts, hidden_grads = {}, {}, {}
    for s in order:
        outer_parts[s] = dot(active[s], result_grad, 0, 0).astype(BF16)
    normed_grad = second_grad
    for s in order:
        hidden_grads[s] = (dot(result_grad, outer[s], 1, 1) * slope[s]).astype(BF16)
        inner_parts[s] = dot(normed_low, hidden_grads[s], 0, 0).astype(BF16)
    for s in order:
        normed_grad = normed_grad + dot(hidden_grads[s], inner[s], 1, 1)
    first_gain_grad = jnp.sum(normed_grad * first_rows, axis=0)
    first_shift_grad = jnp.sum(normed_grad, axis=0)
    first_grad = norm_backward(normed_grad, first_rows, first_scale, first_gain)
    out_bias_grad = jnp.sum(first_grad, axis=0)
    branch_grad = first_grad.astype(BF16)

    input_grad = first_grad
    attention_parts = [None] * slots
    small = [None] * slots
    for p, pair in ((1, (2, 3)), (0, (0, 1))):
        queries, keys, values, context, log_total, wq, wk, wv, wo = kept[p]
        out_part = dot(context, branch_grad, 0, 0).astype(BF16)
        context_grad = dot(branch_grad, wo, 1, 1).astype(BF16)
        q_grad, k_grad, v_grad = attention_backward(
            queries, keys, values, context_grad, length, log_total
        )
        q_part, k_part, v_part = (
            dot(a, inputs, 0, 0).astype(BF16) for a in (q_grad, k_grad, v_grad)
        )
        input_grad = input_grad + dot(q_grad, wq) + dot(k_grad, wk) + dot(v_grad, wv)
        q_sum, v_sum = (jnp.sum(a.astype(F32), axis=0) for a in (q_grad, v_grad))
        for i, s in enumerate(pair):
            cut = lambda a: a[i * width : (i + 1) * width]
            attention_parts[s] = jnp.concatenate(
                [cut(q_part), cut(k_part), cut(v_part), cut(out_part)]
            )
            small[s] = jnp.concatenate(
                [cut(q_sum), cut(v_sum), jnp.sum(hidden_grads[s].astype(F32), axis=0)]
            )

    outer_weight_grad = reduce_grad(outer_parts, odd, z)
    inner_weight_grad = reduce_grad(inner_parts, odd, z)
    attention_grad = reduce_grad(attention_parts, odd, z)
    common = jnp.concatenate(
        [
            out_bias_grad,
            first_gain_grad,
            first_shift_grad,
            outer_bias_grad,
            second_gain_grad,
            second_shift_grad,
        ]
    )
    own, common = reduce_small(small, common)
    model = layer_input.shape[1]
    common = common.reshape(6, model)
    return (
        layer_output,
        input_grad,
        attention_grad[:width].T,
        own[:width],
        attention_grad[width : 2 * width].T,
        attention_grad[2 * width : 3 * width].T,
        own[width : 2 * width],
        attention_grad[3 * width :],
        common[0],
        common[1],
        common[2],
        inner_weight_grad,
        own[2 * width :],
        outer_weight_grad,
        common[3],
        common[4],
        common[5],
    )


def solution(mesh):
    in_specs = (
        P("dp", None),
        P("dp"),
        P(None, "tp"),
        P("tp"),
        P(None, "tp"),
        P(None, "tp"),
        P("tp"),
        P("tp", None),
        P(),
        P(),
        P(),
        P(None, "tp"),
        P("tp"),
        P("tp", None),
        P(),
        P(),
        P(),
        P("dp", None),
    )
    out_specs = (
        P(("dp", "tp"), None),
        P(("dp", "tp"), None),
        P(None, "tp"),
        P("tp"),
        P(None, "tp"),
        P(None, "tp"),
        P("tp"),
        P("tp", None),
        P(),
        P(),
        P(),
        P(None, "tp"),
        P("tp"),
        P("tp", None),
        P(),
        P(),
        P(),
    )
    return jax.shard_map(
        on_device, mesh=mesh, in_specs=in_specs, out_specs=out_specs, check_vma=False
    )
```

```python
import functools

import jax
import jax.numpy as jnp
from jax import lax
from jax.experimental import pallas as pl
from jax.experimental.pallas import tpu as pltpu
from jax.sharding import PartitionSpec as P

HD = 64
EPSILON = 1e-05
BF16 = jnp.bfloat16
F32 = jnp.float32
VMEM_BYTES = 50 * 2**20
STEP_ROWS = 32


def dot(left, right, left_dim=1, right_dim=0):
    return lax.dot_general(
        left, right, (((left_dim,), (right_dim,)), ((), ())), preferred_element_type=F32
    )


def run(body, outs, *args, scalars=0, flops=0, ties=()):
    count = len(args)

    def kernel(*refs):
        body(*refs[:count], *refs[count + len(ties) :])

    return pl.pallas_call(
        kernel,
        out_shape=[jax.ShapeDtypeStruct(shape, dtype) for shape, dtype in outs],
        in_specs=[pl.BlockSpec(memory_space=pltpu.SMEM)] * scalars
        + [pl.BlockSpec(memory_space=pltpu.VMEM)] * (count - scalars)
        + [pl.BlockSpec(memory_space=pl.ANY)] * len(ties),
        out_specs=[pl.BlockSpec(memory_space=pltpu.VMEM)] * len(outs),
        compiler_params=pltpu.CompilerParams(vmem_limit_bytes=VMEM_BYTES),
        cost_estimate=pl.CostEstimate(flops=int(flops), bytes_accessed=0, transcendentals=0),
    )(*args, *ties)


def exchange(array, dp_bits, tp_bits):
    dp_size, tp_size = lax.axis_size("dp"), lax.axis_size("tp")
    pairs = [
        (d * tp_size + t, (d ^ dp_bits) * tp_size + (t ^ tp_bits))
        for d in range(dp_size)
        for t in range(tp_size)
    ]
    return lax.ppermute(array, ("dp", "tp"), pairs)


def later_masks():
    masks, bit = [], 2
    while bit < lax.axis_size("dp"):
        masks.append(6 if bit == 4 else bit)
        bit *= 2
    return masks


def folded(rows):
    return jnp.sum(rows.reshape(rows.shape[0] // 8, 8, rows.shape[1]), axis=0)


def row_steps(rows, body, carry):
    return lax.fori_loop(
        0,
        rows // STEP_ROWS,
        lambda i, c: body(pl.ds(pl.multiple_of(i * STEP_ROWS, STEP_ROWS), STEP_ROWS), c),
        carry,
    )


def normalize(values):
    average = jnp.mean(values, axis=-1, keepdims=True)
    centered = values - average
    spread = jnp.mean(centered * centered, axis=-1, keepdims=True)
    scale = lax.rsqrt(spread + EPSILON)
    return centered * scale, scale


def norm_backward(e, rows, scale):
    first = jnp.mean(e, axis=-1, keepdims=True)
    second = jnp.mean(e * rows, axis=-1, keepdims=True)
    return scale * (e - first - rows * second)


def stacked(low, high, start, width):
    return jnp.concatenate([low[start : start + width], high[start : start + width]])


def pair_weights(qk_a, qk_b, vo_a, vo_b):
    width = qk_a.shape[0] // 2
    return jnp.concatenate(
        [stacked(qk_a, qk_b, 0, width), stacked(qk_a, qk_b, width, width), stacked(vo_a, vo_b, 0, width)]
    )


def lone_head(transposed, head):
    part = transposed[head * HD : (head + 1) * HD]
    zeros = jnp.zeros_like(part)
    return jnp.concatenate([part, zeros] if head % 2 == 0 else [zeros, part])


def tile(array, head):
    start = head // 2 * 2 * HD
    return array[:, start : start + 2 * HD]


def hidden_keys(rows, length):
    return jnp.where(lax.broadcasted_iota(jnp.int32, (rows, 1), 0) < length, 0.0, -1e30)


def visible_scores(keys, queries_t, head, hidden):
    return dot(tile(keys, head), lone_head(queries_t, head)) + hidden


def attend_forward(length, inputs, qk_a, qk_b, vo_a, vo_b, bias, before, qkv, context_t, log_total, after):
    rows = inputs.shape[0]
    width = qk_a.shape[0]
    heads = width // HD
    weights = pair_weights(qk_a, qk_b, vo_a, vo_b)
    qkv[...] = (dot(inputs[...], weights, 1, 1) + bias[...]).astype(BF16)
    queries_t = (qkv[:, :width] * HD**-0.5).astype(BF16).T
    values_t = qkv[:, 2 * width :].T
    hidden = hidden_keys(rows, length[0])
    for h in range(heads):
        scores = visible_scores(qkv[:, width : 2 * width], queries_t, h, hidden)
        top = jnp.max(scores, axis=0, keepdims=True)
        raised = jnp.exp(scores - top)
        total = jnp.sum(raised, axis=0, keepdims=True)
        log_total[h : h + 1] = top + jnp.log(total)
        sums = dot(values_t[h * HD : (h + 1) * HD], raised.astype(BF16))
        context_t[h * HD : (h + 1) * HD] = (sums / total).astype(BF16)
    after[...] = before[...] + dot(context_t[...], stacked(vo_a, vo_b, width // 2, width // 2), 0, 0)


def first_pair(length, inputs, qk_a, qk_b, vo_a, vo_b, bias, out_bias, qkv, context_t, log_total, after):
    after[...] = inputs[...].astype(F32) + out_bias[...]
    attend_forward(length, inputs, qk_a, qk_b, vo_a, vo_b, bias, after, qkv, context_t, log_total, after)


def second_pair(
    length, inputs, qk_a, qk_b, vo_a, vo_b, bias, before, gain, shift, qkv, context_t, log_total, after, normed, normed_low
):
    attend_forward(length, inputs, qk_a, qk_b, vo_a, vo_b, bias, before, qkv, context_t, log_total, after)

    def step(at, carry):
        out = normalize(after[at])[0] * gain[...] + shift[...]
        normed[at] = out
        normed_low[at] = out.astype(BF16)
        return carry

    row_steps(after.shape[0], step, 0)


def feed_slot(normed_low, inner, outer, bias, active, slope):
    columns = 256
    for c in range(0, inner.shape[1], columns):
        at = slice(c, c + columns)
        hidden = dot(normed_low[...], inner[:, at]) + bias[:, at]
        half_erf = 0.5 * (1.0 + lax.erf(hidden * 0.5**0.5))
        active[:, at] = (hidden * half_erf).astype(BF16)
        slope[:, at] = (
            half_erf + hidden * jnp.exp(-0.5 * hidden * hidden) * 0.3989422804014327
        ).astype(BF16)
    return dot(active[...], outer[...])


def feed_first(normed_low, normed, outer_bias, inner_a, inner_b, outer_a, outer_b, bias_a, bias_b,
               active_a, active_b, slope_a, slope_b, after):
    after[...] = normed[...] + outer_bias[...]
    after[...] += feed_slot(normed_low, inner_a, outer_a, bias_a, active_a, slope_a)
    after[...] += feed_slot(normed_low, inner_b, outer_b, bias_b, active_b, slope_b)


def feed_last(normed_low, before, inner_a, inner_b, outer_a, outer_b, bias_a, bias_b, gain, shift, cotangent,
              active_a, active_b, slope_a, slope_b, output, second_grad, result_grad, sums, total):
    total[...] = before[...] + feed_slot(normed_low, inner_a, outer_a, bias_a, active_a, slope_a)
    total[...] += feed_slot(normed_low, inner_b, outer_b, bias_b, active_b, slope_b)

    def step(at, carry):
        rows, scale = normalize(total[at])
        output[at] = (rows * gain[...] + shift[...]).astype(BF16)
        grad = cotangent[at].astype(F32)
        back = norm_backward(grad * gain[...], rows, scale)
        second_grad[at] = back
        result_grad[at] = back.astype(BF16)
        return tuple(c + folded(v) for c, v in zip(carry, (back, grad * rows, grad)))

    zeros = jnp.zeros((8, total.shape[1]), F32)
    parts = row_steps(total.shape[0], step, (zeros,) * 3)
    for i, part in enumerate(parts):
        sums[i : i + 1] = jnp.sum(part, axis=0, keepdims=True)


def outer_near(active_1, active_3, result_grad, parts):
    parts[0] = dot(active_1[...], result_grad[...], 0, 0).astype(BF16)
    parts[1] = dot(active_3[...], result_grad[...], 0, 0).astype(BF16)


def hidden_slot(result_grad, outer, slope, hidden_grad, bias_sum):
    grad = (dot(result_grad[...], outer[...], 1, 1) * slope[...].astype(F32)).astype(BF16)
    hidden_grad[...] = grad
    bias_sum[...] = jnp.sum(grad.astype(F32), axis=0, keepdims=True)


def inner_near(result_grad, normed_low, outer_1, outer_3, inner_1, inner_3, slope_1, slope_3, before,
               parts, sum_1, sum_3, after, hidden_grad):
    after[...] = before[...]
    for i, (outer, inner, slope, bias_sum) in enumerate(
        ((outer_1, inner_1, slope_1, sum_1), (outer_3, inner_3, slope_3, sum_3))
    ):
        hidden_slot(result_grad, outer, slope, hidden_grad, bias_sum)
        parts[i] = dot(normed_low[...], hidden_grad[...], 0, 0).astype(BF16)
        after[...] += dot(hidden_grad[...], inner[...], 1, 1)


def outer_far(active_2, active_0, result_grad, got, low, high, own):
    across = dot(active_2[...], result_grad[...], 0, 0) + got[1].astype(F32)
    half = low.shape[0]
    low[...] = across[:half].astype(BF16)
    high[...] = across[half:].astype(BF16)
    own[...] = (dot(active_0[...], result_grad[...], 0, 0) + got[0].astype(F32)).astype(BF16)


def inner_far(result_grad, normed_low, outer_2, outer_0, inner_2, inner_0, slope_2, slope_0, before, got, first_sum, gain,
              low, high, own, sum_2, sum_0, first_grad, branch_grad, sums, hidden_grad, total):
    half = low.shape[0]
    hidden_slot(result_grad, outer_2, slope_2, hidden_grad, sum_2)
    across = dot(normed_low[...], hidden_grad[...], 0, 0) + got[1].astype(F32)
    low[...] = across[:half].astype(BF16)
    high[...] = across[half:].astype(BF16)
    total[...] = before[...] + dot(hidden_grad[...], inner_2[...], 1, 1)
    hidden_slot(result_grad, outer_0, slope_0, hidden_grad, sum_0)
    own[...] = (dot(normed_low[...], hidden_grad[...], 0, 0) + got[0].astype(F32)).astype(BF16)
    total[...] += dot(hidden_grad[...], inner_0[...], 1, 1)

    def step(at, carry):
        rows, scale = normalize(first_sum[at])
        grad = total[at]
        back = norm_backward(grad * gain[...], rows, scale)
        first_grad[at] = back
        branch_grad[at] = back.astype(BF16)
        return tuple(c + folded(v) for c, v in zip(carry, (back, grad * rows, grad)))

    zeros = jnp.zeros((8, total.shape[1]), F32)
    parts = row_steps(total.shape[0], step, (zeros,) * 3)
    for i, part in enumerate(parts):
        sums[i : i + 1] = jnp.sum(part, axis=0, keepdims=True)


def attend_backward(length, inputs, qk_a, qk_b, vo_a, vo_b, qkv, context_t, log_total, branch_grad, before,
                    part_a, part_b, bias_sums, after, wide):
    rows = inputs.shape[0]
    width = qk_a.shape[0]
    heads = width // HD
    half = width // 2
    out_weights = stacked(vo_a, vo_b, half, half)
    out_part = dot(context_t[...], branch_grad[...]).astype(BF16)
    part_a[3 * half :] = out_part[:half]
    part_b[3 * half :] = out_part[half:]
    grads = dot(branch_grad[...], out_weights, 1, 1).astype(BF16)
    grads_t = grads.T
    queries, keys, values = (qkv[:, i * width : (i + 1) * width] for i in range(3))
    queries_t = (queries * HD**-0.5).astype(BF16).T
    keys_t = keys.T
    hidden = hidden_keys(rows, length[0])
    lane = lax.broadcasted_iota(jnp.int32, (rows, 2 * HD), 1)
    query_grads = []
    for t in range(heads // 2):
        pair = []
        for h in (2 * t, 2 * t + 1):
            scores = visible_scores(keys, queries_t, h, hidden)
            probs = jnp.exp(scores - log_total[h : h + 1])
            prob_grad = dot(tile(values, h), lone_head(grads_t, h))
            inner = jnp.sum(probs * prob_grad, axis=0, keepdims=True)
            score_grad = (probs * (prob_grad - inner)).astype(BF16)
            value_grad = dot(probs.astype(BF16), tile(grads, h))
            key_grad = dot(score_grad, tile(queries, h)) * HD**-0.5
            query_grads.append(dot(keys_t[h * HD : (h + 1) * HD], score_grad) * HD**-0.5)
            pair.append((key_grad, value_grad))
        for i in (0, 1):
            at = (i + 1) * width + 2 * HD * t
            wide[:, at : at + 2 * HD] = jnp.where(lane < HD, pair[0][i], pair[1][i]).astype(BF16)
    query_grads = jnp.concatenate(query_grads).astype(BF16)
    wide[:, :width] = query_grads.T
    bias_sums[0:1] = jnp.sum(wide[:, :width].astype(F32), axis=0, keepdims=True)
    bias_sums[1:2] = jnp.sum(wide[:, 2 * width :].astype(F32), axis=0, keepdims=True)
    for i in range(3):
        grad_t = query_grads if i == 0 else wide[:, i * width : (i + 1) * width].T
        block = dot(grad_t, inputs[...]).astype(BF16)
        part_a[i * half : (i + 1) * half] = block[:half]
        part_b[i * half : (i + 1) * half] = block[half:]
    after[...] = before[...] + dot(wide[...], pair_weights(qk_a, qk_b, vo_a, vo_b))


def add_two(first, second, out):
    out[...] = (first[...].astype(F32) + second[...].astype(F32)).astype(BF16)


def split_sum(odd, *refs):
    *terms, keep, send = refs
    half = keep.shape[0]
    for out, side in ((keep, odd[0]), (send, 1 - odd[0])):
        at = pl.ds(pl.multiple_of(side * half, half), half)
        total = terms[0][at].astype(F32)
        for term in terms[1:]:
            total = total + term[at].astype(F32)
        out[...] = total.astype(BF16)


def assemble(odd, *refs):
    *halves, out = refs
    rows = halves[0].shape[0]
    for c in range(0, len(halves), 2):
        for half, side in ((halves[c], odd[0]), (halves[c + 1], 1 - odd[0])):
            at = pl.ds(pl.multiple_of(c * rows + side * rows, rows), rows)
            out[at] = half[...].astype(F32)


def add_up(first, second):
    return run(add_two, [(first.shape, BF16)], first, second)[0]


def spread_grad(terms, got, odd):
    shape = (got.shape[0] // 2, got.shape[1])
    keep, send = run(split_sum, [(shape, BF16)] * 2, odd, *terms, got, scalars=1)
    mine = add_up(keep, exchange(send, 1, 0))
    for mask in later_masks():
        mine = add_up(mine, exchange(mine, mask, 0))
    return mine, exchange(mine, 1, 0)


def reduce_small(slots, common):
    width = slots[0].shape[0]
    got = exchange(jnp.concatenate([slots[1], slots[3], common]), 0, 1)
    own, across = slots[0] + got[:width], slots[2] + got[width : 2 * width]
    common = common + got[2 * width :]
    got = exchange(jnp.concatenate([across, common]), 0, 2)
    total = jnp.concatenate([own, common]) + got
    for mask in [1] + later_masks():
        total = total + exchange(total, mask, 0)
    return total[:width], total[width:]


def on_device(
    layer_input,
    lengths,
    query_weight,
    query_bias,
    key_weight,
    value_weight,
    value_bias,
    out_weight,
    out_bias,
    first_gain,
    first_shift,
    inner_weight,
    inner_bias,
    outer_weight,
    outer_bias,
    second_gain,
    second_shift,
    cotangent,
):
    slots = lax.axis_size("tp")
    rows = layer_input.shape[0] // slots
    model = layer_input.shape[1]
    width = query_weight.shape[1]
    hidden = inner_weight.shape[1]
    tp, dp = lax.axis_index("tp"), lax.axis_index("dp")
    is_odd = (dp & 1) == 1
    odd = (dp & 1).reshape(1)
    inputs = lax.dynamic_slice_in_dim(layer_input, tp * rows, rows, 0)
    own_grad = lax.dynamic_slice_in_dim(cotangent, tp * rows, rows, 0)
    length = lax.dynamic_slice_in_dim(lengths, tp, 1, 0)

    def gather(first, second):
        near = exchange(jnp.where(is_odd, second, first), 0, 2)
        far = exchange(near, 1, 0)
        first2, second2 = jnp.where(is_odd, far, near), jnp.where(is_odd, near, far)
        return (
            [first, exchange(first, 0, 1), first2, exchange(first2, 0, 1)],
            [second, exchange(second, 0, 1), second2, exchange(second2, 0, 1)],
        )

    qk, vo = gather(
        jnp.concatenate([query_weight.T, key_weight.T]),
        jnp.concatenate([value_weight.T, out_weight]),
    )
    biases = jnp.concatenate([query_bias, value_bias, inner_bias])
    bias1 = exchange(biases, 0, 1)
    bias23 = exchange(jnp.stack([biases, bias1]), 0, 2)
    bias = [biases, bias1, bias23[0], bias23[1]]
    inner, outer = gather(inner_weight, outer_weight)

    def pair_bias(a, b):
        zeros = jnp.zeros((2 * width,), F32)
        parts = [bias[s][i * width : (i + 1) * width] for i in (0, 1) for s in (a, b)]
        return jnp.concatenate(parts[:2] + [zeros] + parts[2:]).reshape(1, 6 * width)

    row = lambda vector: vector.reshape(1, -1)
    feed_bias = [row(b[2 * width :]) for b in bias]
    blocks = lambda a, b: (qk[a], qk[b], vo[a], vo[b])
    seen = [((rows, 6 * width), BF16), ((2 * width, rows), BF16), ((8, rows), F32)]
    full, low = ((rows, model), F32), ((rows, model), BF16)

    qkv0, context0, log0, partial = run(
        first_pair, seen + [full], length, inputs, *blocks(0, 1), pair_bias(0, 1), row(out_bias), scalars=1
    )
    qkv1, context1, log1, first_sum, normed, normed_low = run(
        second_pair, seen + [full, full, low],
        length, inputs, *blocks(2, 3), pair_bias(2, 3), partial, row(first_gain), row(first_shift), scalars=1,
    )

    wide = ((rows, hidden), BF16)
    active, slope = [None] * slots, [None] * slots
    active[0], active[1], slope[0], slope[1], partial = run(
        feed_first, [wide] * 4 + [full],
        normed_low, normed, row(outer_bias), inner[0], inner[1], outer[0], outer[1], feed_bias[0], feed_bias[1],
    )
    (
        active[2], active[3], slope[2], slope[3], layer_output, second_grad, result_grad, second_sums, _,
    ) = run(
        feed_last, [wide] * 4 + [low, full, low, ((8, model), F32), full],
        normed_low, partial, inner[2], inner[3], outer[2], outer[3], feed_bias[2], feed_bias[3],
        row(second_gain), row(second_shift), own_grad,
    )

    square = (hidden, model)
    half_square = ((hidden // 2, model), BF16)
    (outer_parts,) = run(outer_near, [((2,) + square, BF16)], active[1], active[3], result_grad)
    outer_got = exchange(outer_parts, 0, 1)
    bias_sum = ((1, hidden), F32)
    inner_parts, sum1, sum3, partial, _ = run(
        inner_near, [((2,) + square, BF16), bias_sum, bias_sum, full, wide],
        result_grad, normed_low, outer[1], outer[3], inner[1], inner[3], slope[1], slope[3], second_grad,
    )
    inner_got = exchange(inner_parts, 0, 1)
    outer_low, outer_high, outer_own = run(
        outer_far, [half_square] * 2 + [(square, BF16)], active[2], active[0], result_grad, outer_got
    )
    outer_got = [exchange(a, 0, 2) for a in (outer_low, outer_high)]
    inner_low, inner_high, inner_own, sum2, sum0, first_grad, branch_grad, first_sums, _, _ = run(
        inner_far, [half_square] * 2 + [(square, BF16), bias_sum, bias_sum, full, low, ((8, model), F32), wide, full],
        result_grad, normed_low, outer[2], outer[0], inner[2], inner[0], slope[2], slope[0], partial, inner_got,
        first_sum, row(first_gain),
    )
    inner_got = [exchange(a, 0, 2) for a in (inner_low, inner_high)]

    block = ((4 * width, model), BF16)
    grads_out = [block, block, ((8, 2 * width), F32), full, ((rows, 6 * width), BF16)]
    part2, part3, bias_sums1, partial, _ = run(
        attend_backward, grads_out,
        length, inputs, *blocks(2, 3), qkv1, context1, log1, branch_grad, first_grad, scalars=1,
    )
    got3 = exchange(part3, 0, 1)
    part0, part1, bias_sums0, input_grad, _ = run(
        attend_backward, grads_out,
        length, inputs, *blocks(0, 1), qkv0, context0, log0, branch_grad, partial, scalars=1,
    )
    got1 = exchange(part1, 0, 1)
    half = 2 * width
    across = add_up(part2, got3)
    attention_got = [exchange(across[c : c + half], 0, 2) for c in (0, half)]

    def finish(terms, got):
        rows = got[0].shape[0]
        parts = []
        for c in (0, 1):
            parts += spread_grad([t[c * rows : (c + 1) * rows] for t in terms], got[c], odd)
        return parts

    outer_weight_grad = run(assemble, [(square, F32)], odd, *finish([outer_own], outer_got), scalars=1)[0]
    inner_weight_grad = run(assemble, [(square, F32)], odd, *finish([inner_own], inner_got), scalars=1)[0]
    attention_grad = run(
        assemble, [((4 * width, model), F32)], odd, *finish([part0, got1], attention_got), scalars=1
    )[0]

    def small(s, sums, at, feed_sum):
        cut = slice(at * width, (at + 1) * width)
        return jnp.concatenate([sums[0, cut], sums[1, cut], feed_sum[0]])

    own, common = reduce_small(
        [small(0, bias_sums0, 0, sum0), small(1, bias_sums0, 1, sum1), small(2, bias_sums1, 0, sum2), small(3, bias_sums1, 1, sum3)],
        jnp.concatenate([first_sums[:3], second_sums[:3]]).reshape(-1),
    )
    common = common.reshape(6, model)
    return (
        layer_output,
        input_grad,
        attention_grad[:width].T,
        own[:width],
        attention_grad[width : 2 * width].T,
        attention_grad[2 * width : 3 * width].T,
        own[width : 2 * width],
        attention_grad[3 * width :],
        common[0],
        common[1],
        common[2],
        inner_weight_grad,
        own[2 * width :],
        outer_weight_grad,
        common[3],
        common[4],
        common[5],
    )


def solution(mesh):
    in_specs = (
        P("dp", None),
        P("dp"),
        P(None, "tp"),
        P("tp"),
        P(None, "tp"),
        P(None, "tp"),
        P("tp"),
        P("tp", None),
        P(),
        P(),
        P(),
        P(None, "tp"),
        P("tp"),
        P("tp", None),
        P(),
        P(),
        P(),
        P("dp", None),
    )
    out_specs = (
        P(("dp", "tp"), None),
        P(("dp", "tp"), None),
        P(None, "tp"),
        P("tp"),
        P(None, "tp"),
        P(None, "tp"),
        P("tp"),
        P("tp", None),
        P(),
        P(),
        P(),
        P(None, "tp"),
        P("tp"),
        P("tp", None),
        P(),
        P(),
        P(),
    )
    return jax.shard_map(
        on_device, mesh=mesh, in_specs=in_specs, out_specs=out_specs, check_vma=False
    )
```

```python
import dataclasses

import jax
import jax.numpy as jnp
from jax import lax
from jax.experimental import pallas as pl
from jax.experimental.pallas import tpu as pltpu
from jax.sharding import PartitionSpec as P

HD = 64
EPSILON = 1e-05
BF16 = jnp.bfloat16
F32 = jnp.float32
LARGE = 24 * 2**20
SMALL = 12 * 2**20
STEP_ROWS = 128
BIAS_ROWS = 16


def dot(left, right, left_dim=1, right_dim=0):
    return lax.dot_general(
        left, right, (((left_dim,), (right_dim,)), ((), ())), preferred_element_type=F32
    )


@dataclasses.dataclass(frozen=True)
class Afar:
    arrays: tuple
    way: str = "whole"
    rows: int = 0

    def shape(self):
        rows = self.rows or sum(a.shape[0] for a in self.arrays)
        return (rows,) + self.arrays[0].shape[1:]


def afar(*arrays):
    return Afar(arrays)


@dataclasses.dataclass(frozen=True)
class Out:
    shape: tuple
    dtype: jnp.dtype


class Traffic:
    def __init__(self, sems):
        self.sems, self.count = sems, 0
        self.coming, self.going, self.sent = {}, {}, []

    def copy(self, source, target):
        copy = pltpu.make_async_copy(source, target, self.sems.at[self.count])
        copy.start()
        self.count += 1
        return copy

    def need(self, *refs):
        for ref in refs:
            for copy in self.coming.pop(id(ref), ()):
                copy.wait()

    def send(self, *refs):
        for ref in refs:
            self.sent.append(self.copy(ref, self.going.pop(id(ref))))

    def end(self):
        for copies in self.coming.values():
            for copy in copies:
                copy.wait()
        for ref, target in list(self.rest):
            if id(ref) in self.going:
                self.send(ref)
        for copy in self.sent:
            copy.wait()


class Sequence:
    def __init__(self, **scalars):
        self.last, self.scalars = None, scalars

    def __call__(self, body, outs, *args, scalars=(), scratch=(), limit=LARGE):
        operands, sizes, fetched, copies = [self.scalars[name] for name in scalars], [], [], 0
        spaces = [pltpu.SMEM] * len(scalars)
        for arg in args:
            if isinstance(arg, Afar) and arg.way == "raw":
                operands += [pltpu.with_memory_space_constraint(a, pltpu.HBM) for a in arg.arrays]
                spaces += [pltpu.HBM] * len(arg.arrays)
                sizes.append(len(arg.arrays))
                copies += len(arg.arrays)
            elif isinstance(arg, Afar):
                operands += [pltpu.with_memory_space_constraint(a, pltpu.HBM) for a in arg.arrays]
                spaces += [pltpu.HBM] * len(arg.arrays)
                fetched.append(pltpu.VMEM(arg.shape(), arg.arrays[0].dtype))
                sizes.append(len(arg.arrays))
                copies += len(arg.arrays)
            else:
                operands.append(arg)
                spaces.append(pltpu.VMEM)
                sizes.append(1)
        ties = [] if self.last is None else [self.last]
        staged = [pltpu.VMEM(out.shape, out.dtype) for out in outs if isinstance(out, Out)]
        copies += len(staged)
        shapes = [
            pltpu.HBM(out.shape, out.dtype) if isinstance(out, Out) else pltpu.VMEM(*out) for out in outs
        ]

        def kernel(*refs):
            refs = list(refs)
            take = lambda n: [refs.pop(0) for _ in range(n)]
            info = {name: ref[0] for name, ref in zip(scalars, take(len(scalars)))}
            given = [take(n) for n in sizes]
            take(len(ties))
            results, buffers, stages, rest = take(len(outs)), take(len(fetched)), take(len(staged)), take(len(scratch))
            traffic = Traffic(refs[0] if refs else None)
            inputs = []
            for arg, sources in zip(args, given):
                if not isinstance(arg, Afar):
                    inputs += sources
                    continue
                if arg.way == "raw":
                    inputs.append(sources)
                    continue
                buffer = buffers.pop(0)
                inputs.append(buffer)
                parts, start = [], 0
                for i, source in enumerate(sources):
                    rows = source.shape[0]
                    if arg.way == "own":
                        source = source.at[pl.ds(pl.multiple_of(info["tp"] * arg.rows, arg.rows), arg.rows)]
                        target = buffer
                    elif arg.way == "tail":
                        source, target = source.at[pl.ds(rows - arg.rows, arg.rows)], buffer
                    elif len(sources) == 1:
                        target = buffer
                    elif arg.way == "pieces":
                        rows = arg.rows // len(sources)
                        source = source.at[pl.ds(0, rows)]
                        target = buffer.at[pl.ds(pl.multiple_of((info["place"] ^ i) * rows, rows), rows)]
                    else:
                        target = buffer.at[pl.ds(start, rows)]
                        start += rows
                    parts.append(traffic.copy(source, target))
                traffic.coming[id(buffer)] = parts
            for i, out in enumerate(outs):
                if isinstance(out, Out):
                    stage = stages.pop(0)
                    traffic.going[id(stage)] = results[i]
                    results[i] = stage
            traffic.rest = [(ref, None) for ref in results]
            body(traffic, info, *inputs, *results, *rest)
            traffic.end()

        results = pl.pallas_call(
            kernel,
            name=body.__name__,
            out_shape=shapes,
            in_specs=[pl.BlockSpec(memory_space=space) for space in spaces]
            + [pl.BlockSpec(memory_space=pl.ANY)] * len(ties),
            out_specs=[pl.BlockSpec(memory_space=pltpu.HBM if isinstance(o, Out) else pltpu.VMEM) for o in outs],
            scratch_shapes=fetched + staged + [pltpu.VMEM(shape, dtype) for shape, dtype in scratch]
            + ([pltpu.SemaphoreType.DMA((copies,))] if copies else []),
            compiler_params=pltpu.CompilerParams(vmem_limit_bytes=limit),
        )(*operands, *ties)
        self.last = results[-1]
        return results


def exchange(array, dp_bits, tp_bits):
    dp_size, tp_size = lax.axis_size("dp"), lax.axis_size("tp")
    pairs = [
        (d * tp_size + t, (d ^ dp_bits) * tp_size + (t ^ tp_bits))
        for d in range(dp_size)
        for t in range(tp_size)
    ]
    return lax.ppermute(array, ("dp", "tp"), pairs)


def later_masks():
    masks, bit = [], 2
    while bit < lax.axis_size("dp"):
        masks.append(6 if bit == 4 else bit)
        bit *= 2
    return masks


def folded(rows):
    return jnp.sum(rows.reshape(rows.shape[0] // 8, 8, rows.shape[1]), axis=0)


def normalize(values):
    average = jnp.mean(values, axis=-1, keepdims=True)
    centered = values - average
    spread = jnp.mean(centered * centered, axis=-1, keepdims=True)
    scale = lax.rsqrt(spread + EPSILON)
    return centered * scale, scale


def norm_backward(e, rows, scale):
    first = jnp.mean(e, axis=-1, keepdims=True)
    second = jnp.mean(e * rows, axis=-1, keepdims=True)
    return scale * (e - first - rows * second)


def row_steps(rows):
    return [slice(i, i + STEP_ROWS) for i in range(0, rows, STEP_ROWS)]


def as_row(ref):
    return ref[...].reshape(1, ref.shape[0])


def pick_attention(traffic, info, blocks, query_bias, value_bias, inner_bias, first, second, bias, values):
    rows = blocks[0].shape[0]
    targets = (first.at[pl.ds(0, rows)], second)
    for n, (target, mask) in enumerate(zip(targets, (0, 3))):
        for i, block in enumerate(blocks):
            @pl.when((info["place"] ^ mask) == i)
            def _():
                pltpu.make_async_copy(block, target, traffic.sems.at[n]).start()
    values[...] = jnp.zeros_like(values)
    for i, vector in enumerate((query_bias, value_bias, inner_bias)):
        values[i : i + 1, : vector.shape[0]] = as_row(vector)
    high = values[...].astype(BF16).astype(F32)
    packed = jnp.concatenate([high, values[...] - high]).astype(BF16)
    first[rows:] = packed
    bias[...] = packed
    for n, target in enumerate(targets):
        pltpu.make_async_copy(blocks[0], target, traffic.sems.at[n]).wait()
    traffic.count = 2


def unpacked(bias):
    rows = bias[...].astype(F32)
    return rows[: BIAS_ROWS // 2] + rows[BIAS_ROWS // 2 :]


def pair_bias(bias_a, bias_b, width):
    both = bias_a + pltpu.roll(bias_b, width, 1)
    return both[0:1, : 2 * width], both[1:2, : 2 * width]


def pick_feed(traffic, info, blocks, *targets):
    inner, outer = blocks[:2]
    copies = []
    for target, (block, mask) in zip(targets, ((inner, 0), (outer, 0), (inner, 3), (outer, 3))):
        rows = target.shape[0]
        at = pl.ds(pl.multiple_of((info["place"] ^ mask) * rows, rows), rows)
        copies.append(traffic.copy(block.at[at], target))
    for copy, target in zip(copies, targets):
        copy.wait()
        traffic.send(target)


def stacked(low, high, part):
    width = low.shape[0] // 4
    at = slice(part * width, (part + 1) * width)
    return jnp.concatenate([low[at], high[at]])


def pair_weights(block_a, block_b):
    return jnp.concatenate([stacked(block_a, block_b, i) for i in range(3)])


def lone_head(transposed, head):
    part = transposed[head * HD : (head + 1) * HD]
    zeros = jnp.zeros_like(part)
    return jnp.concatenate([part, zeros] if head % 2 == 0 else [zeros, part])


def tile(array, head):
    start = head // 2 * 2 * HD
    return array[:, start : start + 2 * HD]


def hidden_keys(rows, length):
    return jnp.where(lax.broadcasted_iota(jnp.int32, (rows, 1), 0) < length, 0.0, -1e30)


def visible_scores(keys, queries_t, head, hidden):
    return dot(tile(keys, head), lone_head(queries_t, head)) + hidden


def attend_forward(traffic, info, inputs, block_a, block_b, bias_a, bias_b, qkv, context_t, log_total):
    rows = inputs.shape[0]
    width = block_a.shape[0] // 2
    heads = width // HD
    traffic.need(inputs, block_a, block_b)
    weights = pair_weights(block_a, block_b)
    both = dot(inputs[...], weights, 1, 1)
    query_bias, value_bias = pair_bias(bias_a, bias_b, width // 2)
    qkv[:, :width] = (both[:, :width] + query_bias).astype(BF16)
    qkv[:, width : 2 * width] = both[:, width : 2 * width].astype(BF16)
    qkv[:, 2 * width :] = (both[:, 2 * width :] + value_bias).astype(BF16)
    traffic.send(qkv)
    queries_t = (qkv[:, :width] * HD**-0.5).astype(BF16).T
    values_t = qkv[:, 2 * width :].T
    hidden = hidden_keys(rows, info["length"])
    for h in range(heads):
        scores = visible_scores(qkv[:, width : 2 * width], queries_t, h, hidden)
        top = jnp.max(scores, axis=0, keepdims=True)
        raised = jnp.exp(scores - top)
        total = jnp.sum(raised, axis=0, keepdims=True)
        log_total[h : h + 1] = top + jnp.log(total)
        sums = dot(values_t[h * HD : (h + 1) * HD], raised.astype(BF16))
        context_t[h * HD : (h + 1) * HD] = (sums / total).astype(BF16)
    traffic.send(context_t)
    return dot(context_t[...], stacked(block_a, block_b, 3), 0, 0)


def near_pair(traffic, info, inputs, block_a, block_b, bias_a, bias_b, out_bias, qkv, context_t, log_total, after):
    biases = unpacked(bias_a), unpacked(bias_b)
    branch = attend_forward(traffic, info, inputs, block_a, block_b, *biases, qkv, context_t, log_total)
    after[...] = inputs[...].astype(F32) + as_row(out_bias) + branch


def far_pair(traffic, info, inputs, block_a, block_b, tail_a, tail_b, before, gain, shift,
             qkv, context_t, log_total, after, normed, normed_low, bias_a, bias_b):
    traffic.need(tail_a, tail_b)
    bias_a[...], bias_b[...] = tail_a[...], tail_b[...]
    biases = unpacked(bias_a), unpacked(bias_b)
    branch = attend_forward(traffic, info, inputs, block_a, block_b, *biases, qkv, context_t, log_total)
    traffic.need(before)
    after[...] = before[...] + branch
    traffic.send(after)
    for at in row_steps(after.shape[0]):
        out = normalize(after[at])[0] * as_row(gain) + as_row(shift)
        normed[at] = out
        normed_low[at] = out.astype(BF16)


def attend_backward(traffic, info, block_a, block_b, context_t, qkv, inputs, log_total, branch_grad, before,
                    part_a, query_b, key_b, value_b, out_b, bias_sums, after, wide):
    rows = inputs.shape[0]
    half = block_a.shape[0] // 4
    width = 2 * half
    heads = width // HD
    traffic.need(block_a, block_b)
    grads = dot(branch_grad[...], stacked(block_a, block_b, 3), 1, 1).astype(BF16)
    grads_t = grads.T
    traffic.need(context_t)
    out_part = dot(context_t[...], branch_grad[...]).astype(BF16)
    part_a[3 * half :] = out_part[:half]
    out_b[...] = out_part[half:]
    traffic.need(qkv)
    queries, keys, values = (qkv[:, i * width : (i + 1) * width] for i in range(3))
    queries_t = (queries * HD**-0.5).astype(BF16).T
    keys_t = keys.T
    hidden = hidden_keys(rows, info["length"])
    lane = lax.broadcasted_iota(jnp.int32, (rows, 2 * HD), 1)
    query_grads = []
    for t in range(heads // 2):
        pair = []
        for h in (2 * t, 2 * t + 1):
            scores = visible_scores(keys, queries_t, h, hidden)
            probs = jnp.exp(scores - log_total[h : h + 1])
            prob_grad = dot(tile(values, h), lone_head(grads_t, h))
            inner = jnp.sum(probs * prob_grad, axis=0, keepdims=True)
            score_grad = (probs * (prob_grad - inner)).astype(BF16)
            value_grad = dot(probs.astype(BF16), tile(grads, h))
            key_grad = dot(score_grad, tile(queries, h)) * HD**-0.5
            query_grads.append(dot(keys_t[h * HD : (h + 1) * HD], score_grad) * HD**-0.5)
            pair.append((key_grad, value_grad))
        for i in (0, 1):
            at = (i + 1) * width + 2 * HD * t
            wide[:, at : at + 2 * HD] = jnp.where(lane < HD, pair[0][i], pair[1][i]).astype(BF16)
    query_grads = jnp.concatenate(query_grads).astype(BF16)
    wide[:, :width] = query_grads.T
    bias_sums[0:1] = jnp.sum(wide[:, :width].astype(F32), axis=0, keepdims=True)
    bias_sums[1:2] = jnp.sum(wide[:, 2 * width :].astype(F32), axis=0, keepdims=True)
    traffic.need(inputs)
    for i, part_b in enumerate((query_b, key_b, value_b)):
        grad_t = query_grads if i == 0 else wide[:, i * width : (i + 1) * width].T
        block = dot(grad_t, inputs[...]).astype(BF16)
        part_a[i * half : (i + 1) * half] = block[:half]
        part_b[...] = block[half:]
    after[...] = before[...] + dot(wide[...], pair_weights(block_a, block_b))


def feed_slot(normed_low, inner, packed, active, slope):
    bias = unpacked(packed)[2:3]
    columns = 256
    for c in range(0, inner.shape[1], columns):
        at = slice(c, c + columns)
        hidden = dot(normed_low[...], inner[:, at]) + bias[:, at]
        half_erf = 0.5 * (1.0 + lax.erf(hidden * 0.5**0.5))
        active[:, at] = (hidden * half_erf).astype(BF16)
        slope[:, at] = (
            half_erf + hidden * jnp.exp(-0.5 * hidden * hidden) * 0.3989422804014327
        ).astype(BF16)


def feed_near(traffic, info, normed_low, normed, outer_bias, inner_a, inner_b, outer_a, outer_b, bias_a, bias_b,
              active_a, active_b, slope_a, slope_b, after):
    traffic.need(inner_a)
    feed_slot(normed_low, inner_a, bias_a, active_a, slope_a)
    traffic.need(inner_b)
    feed_slot(normed_low, inner_b, bias_b, active_b, slope_b)
    traffic.need(outer_a, outer_b)
    after[...] = (
        normed[...] + as_row(outer_bias) + dot(active_a[...], outer_a[...]) + dot(active_b[...], outer_b[...])
    )


def feed_far(traffic, info, normed_low, inner_a, inner_b, bias_a, bias_b, active_a, active_b, slope_a, slope_b):
    traffic.need(inner_a)
    feed_slot(normed_low, inner_a, bias_a, active_a, slope_a)
    traffic.need(inner_b)
    feed_slot(normed_low, inner_b, bias_b, active_b, slope_b)


def feed_out(traffic, info, active_a, active_b, outer_a, outer_b, before, gain, shift, cotangent,
             output, second_grad, result_grad, sums, total):
    traffic.need(outer_a, outer_b)
    total[...] = before[...] + dot(active_a[...], outer_a[...]) + dot(active_b[...], outer_b[...])
    traffic.need(cotangent)
    parts = [0.0] * 3
    for at in row_steps(total.shape[0]):
        rows, scale = normalize(total[at])
        output[at] = (rows * as_row(gain) + as_row(shift)).astype(BF16)
        grad = cotangent[at].astype(F32)
        back = norm_backward(grad * as_row(gain), rows, scale)
        second_grad[at] = back
        result_grad[at] = back.astype(BF16)
        parts = [c + folded(v) for c, v in zip(parts, (back, grad * rows, grad))]
    for i, part in enumerate(parts):
        sums[i : i + 1] = jnp.sum(part, axis=0, keepdims=True)


def near_grad(traffic, info, left, right, out):
    traffic.need(left)
    out[...] = dot(left[...], right[...], 0, 0).astype(BF16)


def far_grad(traffic, info, left, right, got, low, high):
    total = dot(left[...], right[...], 0, 0) + got[...].astype(F32)
    half = low.shape[0]
    low[...] = total[:half].astype(BF16)
    high[...] = total[half:].astype(BF16)


def hidden_pair(traffic, info, result_grad, outer_a, outer_b, slope_a, slope_b, grad_a, grad_b, sum_a, sum_b):
    for outer, slope, hidden_grad, bias_sum in (
        (outer_a, slope_a, grad_a, sum_a), (outer_b, slope_b, grad_b, sum_b)
    ):
        traffic.need(outer, slope)
        grad = (dot(result_grad[...], outer[...], 1, 1) * slope[...].astype(F32)).astype(BF16)
        hidden_grad[...] = grad
        bias_sum[...] = jnp.sum(grad.astype(F32), axis=0, keepdims=True)


def normed_back(traffic, info, before, g0, g1, g2, g3, w0, w1, w2, w3, first_sum, gain,
                first_grad, branch_grad, sums, total):
    traffic.need(before)
    total[...] = before[...]
    for g, w in ((g0, w0), (g1, w1), (g2, w2), (g3, w3)):
        traffic.need(w)
        total[...] += dot(g[...], w[...], 1, 1)
    traffic.need(first_sum)
    parts = [0.0] * 3
    for at in row_steps(total.shape[0]):
        rows, scale = normalize(first_sum[at])
        grad = total[at]
        back = norm_backward(grad * as_row(gain), rows, scale)
        first_grad[at] = back
        branch_grad[at] = back.astype(BF16)
        parts = [c + folded(v) for c, v in zip(parts, (back, grad * rows, grad))]
    for i, part in enumerate(parts):
        sums[i : i + 1] = jnp.sum(part, axis=0, keepdims=True)


def add_two(traffic, info, first, second, out):
    out[...] = (first[...].astype(F32) + second[...].astype(F32)).astype(BF16)


def add_far(traffic, info, first, query, key, value, out, low, high):
    rows = query.shape[0]
    for i, got in enumerate((query, key, value, out)):
        target = (low, high)[i // 2]
        total = first[i * rows : (i + 1) * rows].astype(F32) + got[...].astype(F32)
        target[i % 2 * rows : (i % 2 + 1) * rows] = total.astype(BF16)


def split_sum(start, info, *refs):
    *terms, got, keep, send = refs
    half = keep.shape[0]
    for out, side in ((keep, info["odd"]), (send, 1 - info["odd"])):
        total = got[pl.ds(pl.multiple_of(side * half, half), half)].astype(F32)
        for term in terms:
            total = total + term[pl.ds(pl.multiple_of(start + side * half, half), half)].astype(F32)
        out[...] = total.astype(BF16)


def split_pieces(start, info, own, first, second, got, keep, send):
    rows = keep.shape[0]
    for side, term in enumerate((first, second)):
        at, own_at = slice(side * rows, (side + 1) * rows), slice(start + side * rows, start + (side + 1) * rows)
        total = (own[own_at].astype(F32) + term[...].astype(F32) + got[at].astype(F32)).astype(BF16)
        for out, flag in ((keep, side), (send, 1 - side)):
            @pl.when(info["odd"] == flag)
            def _():
                out[...] = total


def place_block(traffic, info, *refs):
    *halves, out = refs
    rows = halves[0].shape[0]
    for c in range(0, len(halves), 2):
        for half, side in ((halves[c], info["odd"]), (halves[c + 1], 1 - info["odd"])):
            at = pl.ds(pl.multiple_of(c * rows + side * rows, rows), rows)
            out[at] = half[...].astype(F32)


def place_attention(traffic, info, mine_low, other_low, mine_high, other_high, query, key, value, out):
    for mine, other, first, second in ((mine_low, other_low, query, key), (mine_high, other_high, value, out)):
        for here, there, flag in ((first, second, 0), (second, first, 1)):
            @pl.when(info["odd"] == flag)
            def _():
                here[...] = mine[...].astype(F32)
                there[...] = other[...].astype(F32)


ORDER = (
    "pick_attention", "pick_feed", "near_pair", "ha0", "ha3", "hi0", "ha12", "ho0", "far_pair", "hi12", "hi3", "feed_near", "ho12", "ho3", "feed_far", "feed_out",
    "o3", "o1", "hidden31", "o2", "i3", "i1", "hidden20", "normed_back", "o0", "i0", "i2", "attend23", "go0_s", "attend01", "a2",
    "go1_s", "go0_0",
    "gi0_s", "go1_0", "go0_1",
    "gi1_s", "gi0_0", "go1_1", "go0_2",
    "ga0_s", "gi1_0", "gi0_1", "go1_2",
    "ga1_s", "ga0_0", "gi1_1", "gi0_2",
    "ga1_0", "ga0_1", "gi1_2", "o_end",
    "ga1_1", "ga0_2", "i_end",
    "ga1_2", "a_end",
)


class Plan:
    def __init__(self):
        self.tasks = {}

    def add(self, name, deps, work, transfer=False):
        self.tasks[name] = (tuple(deps), work, transfer)

    def execute(self):
        place = {name: i for i, name in enumerate(ORDER)}
        values, waiting = {}, dict(self.tasks)
        while waiting:
            ready = [n for n, (deps, _, _) in waiting.items() if all(d in values for d in deps)]
            name = min(ready, key=lambda n: -1 if waiting[n][2] else place.get(n, len(place)))
            deps, work, _ = waiting.pop(name)
            values[name] = work(*[values[d] for d in deps])
        return values


def hold(sequence, *arrays):
    def nothing(*refs):
        pass

    ties = [] if sequence.last is None else [sequence.last]
    anywhere = pl.BlockSpec(memory_space=pl.ANY)
    results = pl.pallas_call(
        nothing,
        name="hold",
        out_shape=[jax.ShapeDtypeStruct(a.shape, a.dtype) for a in arrays],
        in_specs=[anywhere] * (len(arrays) + len(ties)),
        out_specs=[anywhere] * len(arrays),
        input_output_aliases={i: i for i in range(len(arrays))},
    )(*arrays, *ties)
    sequence.last = results[0]
    return results


def reduce_small(slots, common):
    width = slots[0].shape[0]
    got = exchange(jnp.concatenate([slots[1], slots[3], common]), 0, 1)
    own, across = slots[0] + got[:width], slots[2] + got[width : 2 * width]
    common = common + got[2 * width :]
    got = exchange(jnp.concatenate([across, common]), 0, 2)
    total = jnp.concatenate([own, common]) + got
    for mask in [1] + later_masks():
        total = total + exchange(total, mask, 0)
    return total[:width], total[width:]


def on_device(
    layer_input,
    lengths,
    query_weight,
    query_bias,
    key_weight,
    value_weight,
    value_bias,
    out_weight,
    out_bias,
    first_gain,
    first_shift,
    inner_weight,
    inner_bias,
    outer_weight,
    outer_bias,
    second_gain,
    second_shift,
    cotangent,
):
    slots = lax.axis_size("tp")
    rows = layer_input.shape[0] // slots
    model = layer_input.shape[1]
    width = query_weight.shape[1]
    hidden = inner_weight.shape[1]
    tp, dp = lax.axis_index("tp"), lax.axis_index("dp")
    run = Sequence(
        tp=tp.reshape(1), place=(dp & 3).reshape(1), odd=(dp & 1).reshape(1),
        length=lax.dynamic_slice_in_dim(lengths, tp, 1, 0),
    )
    near_scalars, far_scalars = ["tp", "length"], ["tp", "place", "length"]
    plan = Plan()
    full, low = ((rows, model), F32), ((rows, model), BF16)
    piece, block = ((width, model), BF16), ((4 * width, model), BF16)
    square = ((hidden, model), BF16)
    half_square = ((hidden // 2, model), BF16)
    wide = ((rows, hidden), BF16)
    sums = ((8, model), F32)

    def transfer(name, dep, pick, dp_bits, tp_bits):
        plan.add(name, [dep], lambda v: exchange(pick(v), dp_bits, tp_bits), True)

    item = lambda i: lambda v: v[i]
    itself = lambda v: v

    own_weights = (query_weight.T, key_weight.T, value_weight.T, out_weight)
    own_block = Afar(own_weights)
    inputs, own_grad = Afar((layer_input,), "own", rows), Afar((cotangent,), "own", rows)
    quarter = ((hidden // 4, model), BF16)
    bias_block = ((BIAS_ROWS, model), BF16)
    plan.add("pick_attention", [], lambda: run(
        pick_attention, [Out((width + BIAS_ROWS, model), BF16), Out(*piece), bias_block], Afar(own_weights, "raw"),
        query_bias, value_bias, inner_bias, scalars=["place"], scratch=[((BIAS_ROWS // 2, model), F32)]))
    transfer("cb", "pick_attention", item(2), 0, 1)
    plan.add("pick_feed", [], lambda: run(
        pick_feed, [Out(*quarter)] * 4, Afar((inner_weight, outer_weight, inner_weight, outer_weight), "raw"), scalars=["place"]))
    for i, name in enumerate(("xa0", "xa3")):
        transfer(name, "pick_attention", item(i), 0, 2)
    for i, name in enumerate(("xi0", "xo0", "xi3", "xo3")):
        transfer(name, "pick_feed", item(i), 0, 2)
    plan.add("ca", [], lambda: Afar(tuple(exchange(w, 0, 1) for w in own_weights)), True)
    plan.add("ci", [], lambda: exchange(inner_weight, 0, 1), True)
    plan.add("co", [], lambda: exchange(outer_weight, 0, 1), True)
    for k, count in zip("aio", (4 * width, hidden, hidden)):
        plan.add(f"h{k}0", [f"x{k}0"], lambda a: hold(run, a))
        transfer(f"y{k}1", f"h{k}0", item(0), 1, 0)
        transfer(f"z{k}2", f"h{k}0", item(0), 2, 0)
        transfer(f"c{k}0", f"h{k}0", item(0), 0, 1)
        plan.add(f"h{k}3", [f"x{k}3"], lambda a: hold(run, a))
        transfer(f"c{k}3", f"h{k}3", item(0), 0, 1)
        plan.add(f"h{k}12", [f"y{k}1", f"z{k}2"], lambda a, b: hold(run, a, b))
        transfer(f"c{k}1", f"h{k}12", item(0), 0, 1)
        transfer(f"c{k}2", f"h{k}12", item(1), 0, 1)
        plan.add(f"f{k}2", [f"h{k}0", f"h{k}12", f"h{k}3"], lambda a, b, c, n=count: Afar((a[0], b[0], b[1], c[0]), "pieces", n), True)
        plan.add(f"f{k}3", [f"c{k}{i}" for i in range(4)], lambda *a, n=count: Afar(a, "pieces", n), True)

    after = Out(*full)
    seen = [Out((rows, 6 * width), BF16), Out((2 * width, rows), BF16), ((8, rows), F32)]
    plan.add("near_pair", ["pick_feed", "pick_attention", "cb", "ca"], lambda _, p, cb, ca: run(
        near_pair, seen + [after], inputs, own_block, ca, p[2], cb, out_bias, scalars=near_scalars))
    plan.add("far_pair", ["near_pair", "fa2", "fa3", "ha0", "ca0"], lambda n, a2, a3, h, c: run(
        far_pair, seen + [after, full, low] + [bias_block] * 2, inputs, a2, a3, Afar((h[0],), "tail", BIAS_ROWS),
        Afar((c,), "tail", BIAS_ROWS), afar(n[3]), first_gain,
        first_shift, scalars=far_scalars))
    plan.add("feed_near", ["far_pair", "ci", "co", "pick_attention", "cb"], lambda f, ci, co, p, cb: run(
        feed_near, [wide] * 4 + [full], f[5], f[4], outer_bias, afar(inner_weight), afar(ci),
        afar(outer_weight), afar(co), p[2], cb))
    plan.add("feed_far", ["far_pair", "fi2", "fi3"], lambda f, i2, i3: run(
        feed_far, [wide] * 4, f[5], i2, i3, f[6], f[7],
        scalars=["place"]))
    plan.add("feed_out", ["feed_near", "feed_far", "fo2", "fo3"], lambda n, f, o2, o3: run(
        feed_out, [Out(*low), after, low, sums], f[0], f[1], o2, o3, n[4], second_gain, second_shift, own_grad,
        scalars=["tp", "place"], scratch=[full]))

    near = lambda left, right: run(near_grad, [square], left, right)
    far = lambda left, right, got: run(far_grad, [half_square] * 2, left, right, got)
    plan.add("o3", ["feed_far", "feed_out"], lambda f, r: near(f[1], r[2]))
    plan.add("o1", ["feed_near", "feed_out"], lambda n, r: near(n[1], r[2]))
    for s in (3, 1):
        transfer(f"co{s}g", f"o{s}", item(0), 0, 1)
    hidden_out = [wide, wide] + [((1, hidden), F32)] * 2
    plan.add("hidden31", ["feed_out", "co", "fo3", "feed_far", "feed_near"], lambda r, co, o3, f, n: run(
        hidden_pair, hidden_out, r[2], o3, afar(co), f[3], n[3], scalars=["place"]))
    plan.add("o2", ["feed_far", "feed_out", "co3g"], lambda f, r, got: far(f[0], r[2], got))
    for i, half in enumerate(("low", "high")):
        transfer(f"xo{half}", "o2", item(i), 0, 2)
    for i, s in enumerate((3, 1)):
        plan.add(f"i{s}", ["far_pair", "hidden31"], lambda f, h, i=i: near(f[5], h[i]))
        transfer(f"ci{s}g", f"i{s}", item(0), 0, 1)
    plan.add("hidden20", ["feed_out", "fo2", "feed_far", "feed_near"], lambda r, o2, f, n: run(
        hidden_pair, hidden_out, r[2], o2, afar(outer_weight), f[2], n[2], scalars=["place"]))
    plan.add("i2", ["far_pair", "hidden20", "ci3g"], lambda f, h, got: far(f[5], h[0], got))
    for i, half in enumerate(("low", "high")):
        transfer(f"xi{half}", "i2", item(i), 0, 2)
    plan.add("normed_back", ["feed_out", "hidden20", "hidden31", "fi2", "fi3", "ci", "far_pair"],
             lambda r, h20, h31, i2, i3, ci, p: run(
                 normed_back, [full, low, sums], afar(r[1]), h20[1], h31[1], h20[0], h31[0],
                 afar(inner_weight), afar(ci), i2, i3, afar(p[3]), first_gain, scalars=["place"],
                 scratch=[full]))
    plan.add("o0", ["feed_near", "feed_out"], lambda n, r: near(n[0], r[2]))
    plan.add("i0", ["far_pair", "hidden20"], lambda f, h: near(f[5], h[1]))

    bias_out = ((8, 2 * width), F32)
    plan.add("attend23", ["fa2", "fa3", "far_pair", "normed_back"], lambda a2, a3, f, b: run(
        attend_backward, [block] + [piece] * 4 + [bias_out, full], a2, a3, afar(f[1]), afar(f[0]), inputs, f[2], b[1],
        b[0], scalars=far_scalars, scratch=[((rows, 6 * width), BF16)]))
    for i in range(4):
        transfer(f"ca3g{i}", "attend23", item(1 + i), 0, 1)
    plan.add("attend01", ["ca", "near_pair", "normed_back", "attend23"], lambda ca, n, b, a: run(
        attend_backward, [Out(*block)] + [piece] * 4 + [bias_out, after], own_block, ca, afar(n[1]), afar(n[0]), inputs,
        n[2], b[1], a[6], scalars=near_scalars, scratch=[((rows, 6 * width), BF16)]))
    for i in range(4):
        transfer(f"ca1g{i}", "attend01", item(1 + i), 0, 1)
    plan.add("a2", ["attend23"] + [f"ca3g{i}" for i in range(4)], lambda a, *got: run(
        add_far, [((2 * width, model), BF16)] * 2, a[0], *got, limit=SMALL))
    for i, half in enumerate(("low", "high")):
        transfer(f"xa{half}", "a2", item(i), 0, 2)

    def chain(name, deps, pick, start, got, rows, body=split_sum):
        quarter = ((rows // 2, model), BF16)

        def split(*values):
            terms = pick(*values[:-1])

            def split_rows(traffic, *refs):
                body(start, *refs)

            return run(split_rows, [quarter, quarter], *terms, values[-1], scalars=["odd"], limit=SMALL)

        add = lambda a, b: run(add_two, [quarter], a[0], b, limit=SMALL)
        plan.add(f"{name}_s", deps + [got], split)
        transfer(f"{name}_y", f"{name}_s", item(1), 1, 0)
        plan.add(f"{name}_0", [f"{name}_s", f"{name}_y"], add)
        last = f"{name}_0"
        for i, mask in enumerate(later_masks()):
            transfer(f"{name}_z{i}", last, item(0), mask, 0)
            plan.add(f"{name}_{i + 1}", [last, f"{name}_z{i}"], add)
            last = f"{name}_{i + 1}"
        transfer(f"{name}_a", last, item(0), 1, 0)
        return [last, f"{name}_a"]

    ends = {}
    for c, half in enumerate(("low", "high")):
        start = c * hidden // 2
        ends["o", c] = chain(f"go{c}", ["o0", "co1g"], lambda o, g: [o[0], g], start, f"xo{half}", hidden // 2)
        ends["i", c] = chain(f"gi{c}", ["i0", "ci1g"], lambda o, g: [o[0], g], start, f"xi{half}", hidden // 2)
        ends["a", c] = chain(
            f"ga{c}", ["attend01", f"ca1g{2 * c}", f"ca1g{2 * c + 1}"], lambda a, g, h: [a[0], g, h], c * 2 * width,
            f"xa{half}", 2 * width, split_pieces)
    for k in "oi":
        plan.add(f"{k}_end", ends[k, 0] + ends[k, 1], lambda a, b, c, d: run(
            place_block, [Out(square[0], F32)], a[0], b, c[0], d, scalars=["odd"], limit=SMALL))
    plan.add("a_end", ends["a", 0] + ends["a", 1], lambda a, b, c, d: run(
        place_attention, [Out((width, model), F32)] * 4, a[0], b, c[0], d, scalars=["odd"], limit=SMALL))

    values = plan.execute()
    bias_sums = {0: (values["attend01"][5], 0), 1: (values["attend01"][5], 1),
                 2: (values["attend23"][5], 0), 3: (values["attend23"][5], 1)}
    feed_sums = {0: values["hidden20"][3], 1: values["hidden31"][3], 2: values["hidden20"][2], 3: values["hidden31"][2]}

    def small(s):
        both_sums, at = bias_sums[s]
        cut = slice(at * width, (at + 1) * width)
        return jnp.concatenate([both_sums[0, cut], both_sums[1, cut], feed_sums[s][0]])

    own, common = reduce_small(
        [small(s) for s in range(slots)],
        jnp.concatenate([values["normed_back"][2][:3], values["feed_out"][3][:3]]).reshape(-1),
    )
    common = common.reshape(6, model)
    query_grad, key_grad, value_grad, out_grad = values["a_end"]
    return (
        values["feed_out"][0],
        values["attend01"][6],
        query_grad.T,
        own[:width],
        key_grad.T,
        value_grad.T,
        own[width : 2 * width],
        out_grad,
        common[0],
        common[1],
        common[2],
        values["i_end"][0],
        own[2 * width :],
        values["o_end"][0],
        common[3],
        common[4],
        common[5],
    )


def solution(mesh):
    in_specs = (
        P("dp", None),
        P("dp"),
        P(None, "tp"),
        P("tp"),
        P(None, "tp"),
        P(None, "tp"),
        P("tp"),
        P("tp", None),
        P(),
        P(),
        P(),
        P(None, "tp"),
        P("tp"),
        P("tp", None),
        P(),
        P(),
        P(),
        P("dp", None),
    )
    out_specs = (
        P(("dp", "tp"), None),
        P(("dp", "tp"), None),
        P(None, "tp"),
        P("tp"),
        P(None, "tp"),
        P(None, "tp"),
        P("tp"),
        P("tp", None),
        P(),
        P(),
        P(),
        P(None, "tp"),
        P("tp"),
        P("tp", None),
        P(),
        P(),
        P(),
    )
    return jax.shard_map(
        on_device, mesh=mesh, in_specs=in_specs, out_specs=out_specs, check_vma=False
    )
```

```python
import dataclasses

import jax
import jax.numpy as jnp
from jax import lax
from jax.experimental import pallas as pl
from jax.experimental.pallas import tpu as pltpu
from jax.sharding import PartitionSpec as P

HD = 64
EPSILON = 1e-05
BF16 = jnp.bfloat16
F32 = jnp.float32
LARGE = 24 * 2**20
STEP_ROWS = 128
BIAS_ROWS = 16
SMALL_ROWS = 8

TP, PLACE, ODD, UPPER, LENGTH = range(5)

ORDERED, PLACED, OWN, RAW = range(4)


def dot(left, right, left_dim=1, right_dim=0):
    return lax.dot_general(
        left, right, (((left_dim,), (right_dim,)), ((), ())), preferred_element_type=F32
    )


@dataclasses.dataclass(frozen=True)
class Afar:
    parts: tuple
    way: int = ORDERED

    def shape(self):
        return (sum(rows for _, _, rows in self.parts),) + self.parts[0][0].shape[1:]


def afar(*arrays, way=ORDERED):
    return Afar(tuple((a, 0, a.shape[0]) for a in arrays), way)


@dataclasses.dataclass(frozen=True)
class Out:
    shape: tuple
    dtype: jnp.dtype


class Traffic:
    def __init__(self, sems):
        self.sems, self.count = sems, 0
        self.coming, self.going, self.sent = {}, {}, []

    def copy(self, source, target):
        copy = pltpu.make_async_copy(source, target, self.sems.at[self.count])
        copy.start()
        self.count += 1
        return copy

    def need(self, *refs):
        for ref in refs:
            for copy in self.coming.pop(id(ref), ()):
                copy.wait()

    def send(self, *refs):
        for ref in refs:
            if id(ref) in self.going:
                self.sent.append(self.copy(ref, self.going.pop(id(ref))))

    def end(self):
        for copies in self.coming.values():
            for copy in copies:
                copy.wait()
        for ref in self.results:
            if id(ref) in self.going:
                self.send(ref)
        for copy in self.sent:
            copy.wait()


class Sequence:
    def __init__(self, scalars):
        self.last, self.scalars = None, scalars

    def ties(self):
        return [] if self.last is None else [pltpu.with_memory_space_constraint(*self.last)]

    def note(self, results, outs):
        smallest = min(range(len(outs)), key=lambda i: results[i].size)
        space = pltpu.HBM if isinstance(outs[smallest], Out) else pltpu.VMEM
        self.last = (results[smallest], space)

    def __call__(self, body, outs, *args, scalars=(), scratch=(), limit=LARGE):
        operands, sizes, fetched, copies = [self.scalars[i] for i in scalars], [], [], 0
        spaces = [pltpu.SMEM] * len(scalars)
        for arg in args:
            if isinstance(arg, Afar):
                operands += [pltpu.with_memory_space_constraint(a, pltpu.HBM) for a, _, _ in arg.parts]
                spaces += [pltpu.HBM] * len(arg.parts)
                sizes.append(len(arg.parts))
                copies += len(arg.parts)
                if arg.way != RAW:
                    fetched.append(pltpu.VMEM(arg.shape(), arg.parts[0][0].dtype))
            else:
                operands.append(arg)
                spaces.append(pltpu.VMEM)
                sizes.append(1)
        ties = self.ties()
        staged = [pltpu.VMEM(out.shape, out.dtype) for out in outs if isinstance(out, Out)]
        copies += len(staged)
        shapes = [
            pltpu.HBM(out.shape, out.dtype) if isinstance(out, Out) else pltpu.VMEM(*out) for out in outs
        ]

        def kernel(*refs):
            refs = list(refs)
            take = lambda n: [refs.pop(0) for _ in range(n)]
            info = {name: ref[0] for name, ref in zip(scalars, take(len(scalars)))}
            given = [take(n) for n in sizes]
            take(len(ties))
            results, buffers, stages, rest = take(len(outs)), take(len(fetched)), take(len(staged)), take(len(scratch))
            traffic = Traffic(refs[0] if refs else None)
            inputs = []
            for arg, sources in zip(args, given):
                if not isinstance(arg, Afar):
                    inputs += sources
                    continue
                if arg.way == RAW:
                    inputs.append(sources)
                    continue
                buffer = buffers.pop(0)
                inputs.append(buffer)
                copies, start = [], 0
                for i, (source, (_, first, rows)) in enumerate(zip(sources, arg.parts)):
                    if arg.way == OWN:
                        first = pl.multiple_of(info[TP] * rows, rows)
                    if arg.way == PLACED:
                        start = pl.multiple_of((info[PLACE] ^ i) * rows, rows)
                    copies.append(traffic.copy(source.at[pl.ds(first, rows)], buffer.at[pl.ds(start, rows)]))
                    start += rows
                traffic.coming[id(buffer)] = copies
            for i, out in enumerate(outs):
                if isinstance(out, Out):
                    stage = stages.pop(0)
                    traffic.going[id(stage)] = results[i]
                    results[i] = stage
            traffic.results = results
            body(traffic, info, *inputs, *results, *rest)
            traffic.end()

        results = pl.pallas_call(
            kernel,
            name=body.__name__,
            out_shape=shapes,
            in_specs=[pl.BlockSpec(memory_space=space) for space in spaces]
            + [pl.BlockSpec(memory_space=pl.ANY)] * len(ties),
            out_specs=[pl.BlockSpec(memory_space=pltpu.HBM if isinstance(o, Out) else pltpu.VMEM) for o in outs],
            scratch_shapes=fetched + staged + [pltpu.VMEM(shape, dtype) for shape, dtype in scratch]
            + ([pltpu.SemaphoreType.DMA((copies,))] if copies else []),
            compiler_params=pltpu.CompilerParams(vmem_limit_bytes=limit),
        )(*operands, *ties)
        self.note(results, outs)
        return results


def exchange(array, dp_bits, tp_bits):
    dp_size, tp_size = lax.axis_size("dp"), lax.axis_size("tp")
    pairs = [
        (d * tp_size + t, (d ^ dp_bits) * tp_size + (t ^ tp_bits))
        for d in range(dp_size)
        for t in range(tp_size)
    ]
    return lax.ppermute(array, ("dp", "tp"), pairs)


def later_masks():
    masks, bit = [], 4
    while bit < lax.axis_size("dp"):
        masks.append(6 if bit == 4 else bit)
        bit *= 2
    return masks


def folded(rows):
    return jnp.sum(rows.reshape(rows.shape[0] // 8, 8, rows.shape[1]), axis=0)


def normalize(values):
    average = jnp.mean(values, axis=-1, keepdims=True)
    centered = values - average
    spread = jnp.mean(centered * centered, axis=-1, keepdims=True)
    scale = lax.rsqrt(spread + EPSILON)
    return centered * scale, scale


def norm_backward(e, rows, scale):
    first = jnp.mean(e, axis=-1, keepdims=True)
    second = jnp.mean(e * rows, axis=-1, keepdims=True)
    return scale * (e - first - rows * second)


def row_steps(rows):
    return [slice(i, i + STEP_ROWS) for i in range(0, rows, STEP_ROWS)]


def as_row(ref):
    return ref[...].reshape(1, ref.shape[0])


def pick_attention(traffic, info, blocks, query_bias, value_bias, inner_bias, pieces, bias, values):
    rows = blocks[0].shape[0]
    targets = [pieces.at[pl.ds(n * rows, rows)] for n in (0, 1)]
    sems = [traffic.sems.at[traffic.count + n] for n in (0, 1)]
    traffic.count += 2
    for target, mask, sem in zip(targets, (0, 3), sems):
        for i, block in enumerate(blocks):
            @pl.when((info[PLACE] ^ mask) == i)
            def _():
                pltpu.make_async_copy(block, target, sem).start()
    traffic.need(query_bias, value_bias, inner_bias)
    values[...] = jnp.zeros_like(values)
    for i, vector in enumerate((query_bias, value_bias, inner_bias)):
        values[i : i + 1, : vector.shape[0]] = as_row(vector)
    high = values[...].astype(BF16).astype(F32)
    packed = jnp.concatenate([high, values[...] - high]).astype(BF16)
    pieces[2 * rows :] = packed
    bias[...] = packed
    for target, sem in zip(targets, sems):
        pltpu.make_async_copy(blocks[0], target, sem).wait()


def unpacked(bias):
    rows = bias[...].astype(F32)
    return rows[: BIAS_ROWS // 2] + rows[BIAS_ROWS // 2 :]


def pair_bias(bias_a, bias_b, width):
    both = bias_a + pltpu.roll(bias_b, width, 1)
    return both[0:1, : 2 * width], both[1:2, : 2 * width]


def pick_feed(traffic, info, blocks, *targets):
    copies = []
    for target, mask in zip(targets, (0, 3)):
        rows = target.shape[0] // 2
        for i, block in enumerate(blocks[:2]):
            at = pl.ds(pl.multiple_of((info[PLACE] ^ mask) * rows, rows), rows)
            copies.append(traffic.copy(block.at[at], target.at[pl.ds(i * rows, rows)]))
    for i, target in enumerate(targets):
        copies[2 * i].wait()
        copies[2 * i + 1].wait()
        traffic.send(target)


def stacked(low, high, part):
    width = low.shape[0] // 4
    at = slice(part * width, (part + 1) * width)
    return jnp.concatenate([low[at], high[at]])


def pair_weights(block_a, block_b):
    return jnp.concatenate([stacked(block_a, block_b, i) for i in range(3)])


def lone_head(transposed, head):
    part = transposed[head * HD : (head + 1) * HD]
    zeros = jnp.zeros_like(part)
    return jnp.concatenate([part, zeros] if head % 2 == 0 else [zeros, part])


def tile(array, head):
    start = head // 2 * 2 * HD
    return array[:, start : start + 2 * HD]


def hidden_keys(rows, length):
    return jnp.where(lax.broadcasted_iota(jnp.int32, (rows, 1), 0) < length, 0.0, -1e30)


def visible_scores(keys, queries_t, head, hidden):
    return dot(tile(keys, head), lone_head(queries_t, head)) + hidden


def attend_forward(traffic, info, inputs, block_a, block_b, bias_a, bias_b, qkv, context_t, log_total):
    rows = inputs.shape[0]
    width = block_a.shape[0] // 2
    heads = width // HD
    traffic.need(inputs, block_a, block_b)
    weights = pair_weights(block_a, block_b)
    both = dot(inputs[...], weights, 1, 1)
    query_bias, value_bias = pair_bias(bias_a, bias_b, width // 2)
    qkv[:, :width] = (both[:, :width] + query_bias).astype(BF16)
    qkv[:, width : 2 * width] = both[:, width : 2 * width].astype(BF16)
    qkv[:, 2 * width :] = (both[:, 2 * width :] + value_bias).astype(BF16)
    traffic.send(qkv)
    queries_t = (qkv[:, :width] * HD**-0.5).astype(BF16).T
    values_t = qkv[:, 2 * width :].T
    hidden = hidden_keys(rows, info[LENGTH])
    for h in range(heads):
        scores = visible_scores(qkv[:, width : 2 * width], queries_t, h, hidden)
        top = jnp.max(scores, axis=0, keepdims=True)
        raised = jnp.exp(scores - top)
        total = jnp.sum(raised, axis=0, keepdims=True)
        log_total[h : h + 1] = top + jnp.log(total)
        sums = dot(values_t[h * HD : (h + 1) * HD], raised.astype(BF16))
        context_t[h * HD : (h + 1) * HD] = (sums / total).astype(BF16)
    traffic.send(context_t)
    return dot(context_t[...], stacked(block_a, block_b, 3), 0, 0)


def near_pair(traffic, info, inputs, block_a, block_b, bias_a, bias_b, out_bias, qkv, context_t, log_total, after):
    biases = unpacked(bias_a), unpacked(bias_b)
    branch = attend_forward(traffic, info, inputs, block_a, block_b, *biases, qkv, context_t, log_total)
    after[...] = inputs[...].astype(F32) + as_row(out_bias) + branch


def far_pair(traffic, info, inputs, block_a, block_b, tail_a, tail_b, before, gain, shift,
             qkv, context_t, log_total, after, normed, normed_low, bias_a, bias_b):
    traffic.need(tail_a, tail_b)
    bias_a[...], bias_b[...] = tail_a[...], tail_b[...]
    biases = unpacked(bias_a), unpacked(bias_b)
    branch = attend_forward(traffic, info, inputs, block_a, block_b, *biases, qkv, context_t, log_total)
    traffic.need(before)
    after[...] = before[...] + branch
    traffic.send(after)
    for at in row_steps(after.shape[0]):
        out = normalize(after[at])[0] * as_row(gain) + as_row(shift)
        normed[at] = out
        normed_low[at] = out.astype(BF16)


def attend_backward(traffic, info, qkv, block_a, block_b, context_t, inputs, log_total, branch_grad, before,
                    part_a, query_b, key_b, value_b, out_b, sums_a, sums_b, after, wide, probs):
    rows = inputs.shape[0]
    half = block_a.shape[0] // 4
    width = 2 * half
    heads = width // HD
    traffic.need(qkv)
    queries, keys, values = (qkv[:, i * width : (i + 1) * width] for i in range(3))
    queries_t = (queries * HD**-0.5).astype(BF16).T
    keys_t = keys.T
    hidden = hidden_keys(rows, info[LENGTH])
    for h in range(heads):
        scores = visible_scores(keys, queries_t, h, hidden)
        probs[h] = jnp.exp(scores - log_total[h : h + 1])
    traffic.need(block_a, block_b)
    grads = dot(branch_grad[...], stacked(block_a, block_b, 3), 1, 1).astype(BF16)
    grads_t = grads.T
    lane = lax.broadcasted_iota(jnp.int32, (rows, 2 * HD), 1)
    query_grads = []
    for t in range(heads // 2):
        pair = []
        for h in (2 * t, 2 * t + 1):
            prob_grad = dot(tile(values, h), lone_head(grads_t, h))
            inner = jnp.sum(probs[h] * prob_grad, axis=0, keepdims=True)
            score_grad = (probs[h] * (prob_grad - inner)).astype(BF16)
            value_grad = dot(probs[h].astype(BF16), tile(grads, h))
            key_grad = dot(score_grad, tile(queries, h)) * HD**-0.5
            query_grads.append(dot(keys_t[h * HD : (h + 1) * HD], score_grad) * HD**-0.5)
            pair.append((key_grad, value_grad))
        for i in (0, 1):
            at = (i + 1) * width + 2 * HD * t
            wide[:, at : at + 2 * HD] = jnp.where(lane < HD, pair[0][i], pair[1][i]).astype(BF16)
    traffic.need(context_t)
    out_part = dot(context_t[...], branch_grad[...]).astype(BF16)
    part_a[3 * half :] = out_part[:half]
    out_b[...] = out_part[half:]
    query_grads = jnp.concatenate(query_grads).astype(BF16)
    wide[:, :width] = query_grads.T
    after[...] = before[...] + dot(wide[...], pair_weights(block_a, block_b))
    traffic.send(after)
    model = sums_a.shape[1]
    first = lax.broadcasted_iota(jnp.int32, sums_a.shape, 1) < half

    def summed(at):
        row = jnp.sum(wide[:, at : at + width].astype(F32), axis=0, keepdims=True)
        return jnp.broadcast_to(jnp.concatenate([row, jnp.zeros((1, model - width), F32)], axis=1), sums_a.shape)

    query_sum, value_sum = summed(0), summed(2 * width)
    for out, shift in ((sums_a, 0), (sums_b, model - half)):
        query, value = ((pltpu.roll(a, shift, 1) if shift else a) for a in (query_sum, value_sum))
        out[...] = jnp.where(first, query, 0.0) + pltpu.roll(jnp.where(first, value, 0.0), value_start(half), 1)
    traffic.need(inputs)
    for i, part_b in enumerate((query_b, key_b, value_b)):
        grad_t = query_grads if i == 0 else wide[:, i * width : (i + 1) * width].T
        block = dot(grad_t, inputs[...]).astype(BF16)
        part_a[i * half : (i + 1) * half] = block[:half]
        part_b[...] = block[half:]


def value_start(width):
    return -(-width // 128) * 128


def feed_slot(normed_low, inner, packed, active, slope):
    bias = unpacked(packed)[2:3]
    columns = 256
    for c in range(0, inner.shape[1], columns):
        at = slice(c, c + columns)
        hidden = dot(normed_low[...], inner[:, at]) + bias[:, at]
        half_erf = 0.5 * (1.0 + lax.erf(hidden * 0.5**0.5))
        active[:, at] = (hidden * half_erf).astype(BF16)
        slope[:, at] = (
            half_erf + hidden * jnp.exp(-0.5 * hidden * hidden) * 0.3989422804014327
        ).astype(BF16)


def feed_near(traffic, info, normed_low, normed, outer_bias, inner_a, inner_b, outer_a, outer_b, bias_a, bias_b,
              active_a, active_b, slope_a, slope_b, after):
    traffic.need(inner_a)
    feed_slot(normed_low, inner_a, bias_a, active_a, slope_a)
    traffic.need(inner_b)
    feed_slot(normed_low, inner_b, bias_b, active_b, slope_b)
    traffic.need(outer_a, outer_b)
    after[...] = (
        normed[...] + as_row(outer_bias) + dot(active_a[...], outer_a[...]) + dot(active_b[...], outer_b[...])
    )


def feed_far(traffic, info, normed_low, inner, bias, active, slope):
    traffic.need(inner)
    feed_slot(normed_low, inner, bias, active, slope)


def feed_out(traffic, info, active_a, active_b, outer_a, outer_b, before, gain, shift, cotangent,
             output, second_grad, result_grad, sums, total):
    traffic.need(outer_a, outer_b)
    total[...] = before[...] + dot(active_a[...], outer_a[...]) + dot(active_b[...], outer_b[...])
    traffic.need(cotangent)
    parts = [0.0] * 3
    for at in row_steps(total.shape[0]):
        rows, scale = normalize(total[at])
        output[at] = (rows * as_row(gain) + as_row(shift)).astype(BF16)
        grad = cotangent[at].astype(F32)
        back = norm_backward(grad * as_row(gain), rows, scale)
        second_grad[at] = back
        result_grad[at] = back.astype(BF16)
        parts = [c + folded(v) for c, v in zip(parts, (back, grad * rows, grad))]
    for i, part in enumerate(parts):
        sums[i : i + 1] = jnp.sum(part, axis=0, keepdims=True)


def near_grad(traffic, info, left, right, out):
    out[...] = dot(left[...], right[...], 0, 0).astype(BF16)


def far_grad(traffic, info, left, right, got, *chunks):
    total = dot(left[...], right[...], 0, 0) + got[...].astype(F32)
    rows = chunks[0].shape[0]
    for i, chunk in enumerate(chunks):
        chunk[...] = total[i * rows : (i + 1) * rows].astype(BF16)


def hidden_pair(traffic, info, result_grad, outer_a, outer_b, slope_a, slope_b, grad_a, grad_b, sum_a, sum_b):
    for outer, slope, hidden_grad, bias_sum in (
        (outer_a, slope_a, grad_a, sum_a), (outer_b, slope_b, grad_b, sum_b)
    ):
        traffic.need(outer)
        grad = (dot(result_grad[...], outer[...], 1, 1) * slope[...].astype(F32)).astype(BF16)
        hidden_grad[...] = grad
        bias_sum[...] = jnp.sum(grad.astype(F32), axis=0, keepdims=True)


def feed_back(traffic, info, result_grad, outer_2, outer_0, slope_2, slope_0, before, grad_3, grad_1,
              inner_3, inner_1, inner_2, inner_0, first_sum, gain,
              grad_2, grad_0, sum_2, sum_0, first_grad, branch_grad, sums, total):
    hidden_pair(traffic, info, result_grad, outer_2, outer_0, slope_2, slope_0, grad_2, grad_0, sum_2, sum_0)
    traffic.need(before)
    total[...] = before[...]
    for g, w in ((grad_3, inner_3), (grad_1, inner_1), (grad_2, inner_2), (grad_0, inner_0)):
        traffic.need(w)
        total[...] += dot(g[...], w[...], 1, 1)
    traffic.need(first_sum)
    parts = [0.0] * 3
    for at in row_steps(total.shape[0]):
        rows, scale = normalize(first_sum[at])
        grad = total[at]
        back = norm_backward(grad * as_row(gain), rows, scale)
        first_grad[at] = back
        branch_grad[at] = back.astype(BF16)
        parts = [c + folded(v) for c, v in zip(parts, (back, grad * rows, grad))]
    for i, part in enumerate(parts):
        sums[i : i + 1] = jnp.sum(part, axis=0, keepdims=True)


def add_far(traffic, info, first, query, key, value, out, *chunks):
    rows = query.shape[0]
    each = chunks[0].shape[0] // rows
    for i, got in enumerate((query, key, value, out)):
        total = first[i * rows : (i + 1) * rows].astype(F32) + got[...].astype(F32)
        chunks[i // each][i % each * rows : (i % each + 1) * rows] = total.astype(BF16)


def split_rows(start):
    def split(traffic, info, own, near, got, keep, send):
        half = keep.shape[0]
        for out, side in ((keep, info[ODD]), (send, 1 - info[ODD])):
            at = pl.ds(pl.multiple_of(start + side * half, half), half)
            total = got[pl.ds(pl.multiple_of(side * half, half), half)].astype(F32)
            out[...] = (total + own[at].astype(F32) + near[at].astype(F32)).astype(BF16)

    return split


def split_pieces(start):
    def split(traffic, info, own, first, second, got, *refs):
        keep, send = refs[-3:-1] if len(refs) == 5 else refs
        rows = keep.shape[0]
        for side, term in enumerate((first, second)):
            at, own_at = slice(side * rows, (side + 1) * rows), slice(start + side * rows, start + (side + 1) * rows)
            total = (own[own_at].astype(F32) + term[...].astype(F32) + got[at].astype(F32)).astype(BF16)
            for out, flag in ((keep, side), (send, 1 - side)):
                @pl.when(info[ODD] == flag)
                def _():
                    out[...] = total
        if len(refs) == 5:
            refs[-1][...] = refs[0][...] + refs[1][...]

    return split


def add_split(traffic, info, keep, got, *refs):
    mine, send = refs[-3:-1] if len(refs) == 5 else refs
    rows = mine.shape[0]
    for out, side in ((mine, info[UPPER]), (send, 1 - info[UPPER])):
        at = pl.ds(pl.multiple_of(side * rows, rows), rows)
        out[...] = (keep[at].astype(F32) + got[at].astype(F32)).astype(BF16)
    if len(refs) == 5:
        refs[-1][...] = refs[0][...] + refs[1][...]


def add_two(traffic, info, first, second, *refs):
    if len(refs) == 1:
        (out,) = refs
    else:
        small, got, out, small_out = refs
        small_out[...] = small[...] + got[...]
    out[...] = (first[...].astype(F32) + second[...].astype(F32)).astype(BF16)


def join(traffic, info, mine, got, whole):
    rows = mine.shape[0]
    for part, side in ((mine, info[UPPER]), (got, 1 - info[UPPER])):
        whole[pl.ds(pl.multiple_of(side * rows, rows), rows)] = part[...]


def place_block(traffic, info, *refs):
    *halves, out = refs
    rows = halves[0].shape[0]
    for c in range(0, len(halves), 2):
        for half, side in ((halves[c], info[ODD]), (halves[c + 1], 1 - info[ODD])):
            at = pl.ds(pl.multiple_of(c * rows + side * rows, rows), rows)
            out[at] = half[...].astype(F32)


def place_pieces(traffic, info, mine, other, first, second):
    for here, there, flag in ((first, second, 0), (second, first, 1)):
        @pl.when(info[ODD] == flag)
        def _():
            here[...] = mine[...].astype(F32)
            there[...] = other[...].astype(F32)


def collect_small(traffic, info, h0, h1, h2, h3, a0, a1, a2, a3, first_sums, second_sums, own, across, near):
    common = jnp.concatenate([first_sums[0:3], second_sums[0:3]])
    zeros = jnp.zeros_like(common)
    own[...] = jnp.concatenate([h0[...], a0[0:1], common])
    across[...] = jnp.concatenate([h2[...], a2[0:1], zeros])
    near[...] = jnp.concatenate([h1[...], a1[0:1], h3[...], a3[0:1], common, zeros])


def add_small(traffic, info, own, across, got, own_out, across_out):
    total = own[...] + jnp.concatenate([got[0:2], got[4:10]])
    own_out[...] = total
    across_out[...] = jnp.concatenate([across[0:2] + got[2:4], total[2:]])


def spread_small(traffic, info, small, inner, query, value, *common):
    inner[...] = small[0:1].reshape(inner.shape)
    width = query.shape[0]
    start = value_start(width)
    query[...] = small[1:2, :width].reshape(query.shape)
    value[...] = small[1:2, start : start + width].reshape(value.shape)
    for i, out in enumerate(common):
        out[...] = small[2 + i : 3 + i].reshape(out.shape)


OUTER_CHUNKS, INNER_CHUNKS = 1, 2
STEPS = (1, 0, 1, 2, 0, 1, 2, 3, 1, 2, 0, 3, 4, 1, 3, 2, 4, 0, 2, 3, 4)
LAST_STEPS = (3, 4, 4)


def hold(run, *arrays):
    def nothing(*refs):
        pass

    ties = run.ties()
    anywhere = pl.BlockSpec(memory_space=pl.ANY)
    return pl.pallas_call(
        nothing,
        name=nothing.__name__,
        out_shape=[jax.ShapeDtypeStruct(a.shape, a.dtype) for a in arrays],
        in_specs=[anywhere] * (len(arrays) + len(ties)),
        out_specs=[anywhere] * len(arrays),
        input_output_aliases={i: i for i in range(len(arrays))},
    )(*arrays, *ties)


def chain(run, split, small):
    keep, send, *small = split(small)
    shape, rows = (keep.shape[0] // 2, keep.shape[1]), keep.shape[0]
    small_out = [(s.shape, F32) for s in small]
    partners = lambda mask: [b for s in small for b in (s, exchange(s, mask, 0))]
    got, pairs = exchange(send, 1, 0), partners(1)
    yield
    mine, send, *small = run(add_split, [(shape, BF16)] * 2 + small_out, keep, got, *pairs, scalars=[UPPER])
    got, pairs = exchange(send, 2, 0), partners(2)
    yield
    for mask in later_masks():
        mine, *small = run(add_two, [(shape, BF16)] + small_out, mine, got, *pairs)
        got, pairs = exchange(mine, mask, 0), partners(mask)
        yield
    mine, *small = run(add_two, [(shape, BF16)] + small_out, mine, got, *pairs)
    got = exchange(mine, 2, 0)
    yield
    (whole,) = run(join, [((rows, shape[1]), BF16)], mine, got, scalars=[UPPER])
    got = exchange(whole, 1, 0)
    yield
    return (whole, got), small


def on_device(
    layer_input,
    lengths,
    query_weight,
    query_bias,
    key_weight,
    value_weight,
    value_bias,
    out_weight,
    out_bias,
    first_gain,
    first_shift,
    inner_weight,
    inner_bias,
    outer_weight,
    outer_bias,
    second_gain,
    second_shift,
    cotangent,
):
    rows = layer_input.shape[0] // lax.axis_size("tp")
    model = layer_input.shape[1]
    width = query_weight.shape[1]
    hidden = inner_weight.shape[1]
    tp, dp = lax.axis_index("tp"), lax.axis_index("dp")
    upper = (dp >> 1) ^ (dp >> 2)
    run = Sequence(
        [s.reshape(1) for s in (tp, dp & 3, dp & 1, upper & 1)] + [lax.dynamic_slice_in_dim(lengths, tp, 1, 0)]
    )
    to_core = lambda a: exchange(a, 0, 1)
    to_x = lambda a: exchange(a, 0, 2)
    to_y = lambda a: exchange(a, 1, 0)
    to_z = lambda a: exchange(a, 2, 0)

    full, low = ((rows, model), F32), ((rows, model), BF16)
    piece, block = ((width, model), BF16), ((4 * width, model), BF16)
    square, wide = ((hidden, model), BF16), ((rows, hidden), BF16)
    bias_block, sums, small = ((BIAS_ROWS, model), BF16), ((8, model), F32), ((SMALL_ROWS, model), F32)
    inputs, own_grad = (Afar(((a, 0, rows),), OWN) for a in (layer_input, cotangent))

    own_weights = (query_weight.T, key_weight.T, value_weight.T, out_weight)
    sent, own_bias = run(
        pick_attention, [Out((2 * width + BIAS_ROWS, model), BF16), bias_block], afar(*own_weights, way=RAW),
        afar(query_bias), afar(value_bias), afar(inner_bias), scalars=[PLACE], scratch=[small])
    came = to_x(sent)
    near_weights, near_bias = [to_core(w) for w in own_weights], to_core(own_bias)
    half_square = Out((hidden // 2, model), BF16)
    sent = run(
        pick_feed, [half_square] * 2, afar(inner_weight, outer_weight, inner_weight, outer_weight, way=RAW),
        scalars=[PLACE])
    feed_came, feed_last_came = to_x(sent[0]), to_x(sent[1])
    near_inner, near_outer = to_core(inner_weight), to_core(outer_weight)

    near_scalars, far_scalars = [TP, LENGTH], [TP, PLACE, LENGTH]
    seen = [Out((rows, 6 * width), BF16), Out((2 * width, rows), BF16), ((8, rows), F32)]
    own_block, near_block = afar(*own_weights), afar(*near_weights)
    near_qkv, near_context, near_log, partial = run(
        near_pair, seen + [Out(*full)], inputs, own_block, near_block, own_bias, near_bias, out_bias,
        scalars=near_scalars)
    (came,) = hold(run, came)
    spread = came[:width]
    from_y, from_z, came_near = to_y(spread), to_z(spread), to_core(came)
    from_y, from_z = hold(run, from_y, from_z)
    (feed_came,) = hold(run, feed_came)
    feed_y, feed_z, feed_near_0 = to_y(feed_came), to_z(feed_came), to_core(feed_came)
    attention_parts = lambda a, b, c: Afar(((a, 0, width), (b, 0, width), (c, 0, width), (a, width, width)), PLACED)
    tail = lambda a: Afar(((a, 2 * width, BIAS_ROWS),))
    far_blocks = (attention_parts(came, from_y, from_z), attention_parts(came_near, to_core(from_y), to_core(from_z)))
    far_qkv, far_context, far_log, first_sum, normed, normed_low, bias_2, bias_3 = run(
        far_pair, seen + [Out(*full), full, low] + [bias_block] * 2, inputs, *far_blocks, tail(came), tail(came_near),
        afar(partial), first_gain, first_shift, scalars=far_scalars)

    active_0, active_1, slope_0, slope_1, partial = run(
        feed_near, [wide] * 4 + [full], normed_low, normed, outer_bias, afar(inner_weight), afar(near_inner),
        afar(outer_weight), afar(near_outer), own_bias, near_bias)
    (feed_last_came,) = hold(run, feed_last_came)
    feed_y, feed_z = hold(run, feed_y, feed_z)
    far_feed = (feed_came, feed_y, feed_z, feed_last_came)
    near_feed = (feed_near_0, to_core(feed_y), to_core(feed_z), to_core(feed_last_came))
    quarter = hidden // 4
    inner_2, inner_3 = (Afar(tuple((a, 0, quarter) for a in f), PLACED) for f in (far_feed, near_feed))
    outer_2, outer_3 = (Afar(tuple((a, quarter, quarter) for a in f), PLACED) for f in (far_feed, near_feed))
    (active_2, slope_2), (active_3, slope_3) = (
        run(feed_far, [wide] * 2, normed_low, inner, bias, scalars=[PLACE])
        for inner, bias in ((inner_2, bias_2), (inner_3, bias_3))
    )
    layer_output, second_grad, result_grad, second_sums = run(
        feed_out, [Out(*low), Out(*full), low, sums], active_2, active_3, outer_2, outer_3, partial,
        second_gain, second_shift, own_grad, scalars=[TP, PLACE], scratch=[full])

    near = lambda left, right: run(near_grad, [square], left, right)[0]
    outer_sent = near(active_3, result_grad)
    outer_got_3 = to_core(outer_sent)
    outer_got_1 = to_core(near(active_1, result_grad))
    hidden_out = [wide, wide] + [((1, hidden), F32)] * 2
    hidden_3, hidden_1, sum_3, sum_1 = run(
        hidden_pair, hidden_out, result_grad, outer_3, afar(near_outer), slope_3, slope_1, scalars=[PLACE])
    far = lambda left, right, got, n: run(
        far_grad, [((hidden // n, model), BF16)] * n, left, right, got)
    outer_x = [to_x(a) for a in far(active_2, result_grad, outer_got_3, OUTER_CHUNKS)]
    inner_got_3 = to_core(near(normed_low, hidden_3))
    inner_got_1 = to_core(near(normed_low, hidden_1))
    hidden_2, hidden_0, sum_2, sum_0, first_grad, branch_grad, first_sums = run(
        feed_back, hidden_out + [full, low, sums], result_grad, outer_2, afar(outer_weight), slope_2, slope_0,
        afar(second_grad), hidden_3, hidden_1, inner_3, afar(near_inner), inner_2, afar(inner_weight), afar(first_sum),
        first_gain, scalars=[PLACE], scratch=[full])
    inner_x = [to_x(a) for a in far(normed_low, hidden_2, inner_got_3, INNER_CHUNKS)]
    outer_own, inner_own = near(active_0, result_grad), near(normed_low, hidden_0)

    rooms = [((rows, 6 * width), BF16), ((2 * width // HD, rows, rows), F32)]
    part_2, *part_3, sums_2, sums_3, partial = run(
        attend_backward, [block] + [piece] * 4 + [sums, sums, full], afar(far_qkv), *far_blocks, afar(far_context),
        inputs, far_log, branch_grad, first_grad, scalars=far_scalars, scratch=rooms)
    got_3 = [to_core(a) for a in part_3]

    def of_square(own, near, got, chunk, chunks):
        size = hidden // chunks

        def split(small):
            return run(
                split_rows(chunk * size), [((size // 2, model), BF16)] * 2, own, near, got, scalars=[ODD])

        return chain(run, split, ())

    outer_ways = [of_square(outer_own, outer_got_1, a, i, OUTER_CHUNKS) for i, a in enumerate(outer_x)]
    inner_ways = [of_square(inner_own, inner_got_1, a, i, INNER_CHUNKS) for i, a in enumerate(inner_x)]
    next(outer_ways[0])
    part_0, *part_1, sums_0, sums_1, input_grad = run(
        attend_backward, [block] + [piece] * 4 + [sums, sums, Out(*full)], afar(near_qkv), own_block, near_block,
        afar(near_context), inputs, near_log, branch_grad, partial, scalars=near_scalars, scratch=rooms)
    got_1 = [to_core(a) for a in part_1]
    attention_x = [to_x(a) for a in run(add_far, [((2 * width, model), BF16)] * 2, part_2, *got_3)]
    small_own, small_across, small_near = run(
        collect_small, [small, small, ((2 * SMALL_ROWS, model), F32)], sum_0, sum_1, sum_2, sum_3,
        sums_0, sums_1, sums_2, sums_3, first_sums, second_sums)
    small_near = to_core(small_near)

    def of_attention(chunk, small):
        def split(small):
            return run(
                split_pieces(chunk * 2 * width), [piece] * 2 + [(s.shape, F32) for s in small[:1]], part_0,
                got_1[2 * chunk], got_1[2 * chunk + 1], attention_x[chunk], *small, scalars=[ODD])

        return chain(run, split, small)

    small_own, small_across = run(add_small, [small, small], small_own, small_across, small_near)
    attention_ways = [of_attention(0, ()), of_attention(1, (small_own, to_x(small_across)))]
    ways = outer_ways + inner_ways + attention_ways
    for number in STEPS:
        next(ways[number])

    def finish(way):
        while True:
            try:
                next(way)
            except StopIteration as stop:
                return stop.value

    def place(ways):
        halves = [half for way in ways for half in finish(way)[0]]
        return run(place_block, [Out(square[0], F32)], *halves, scalars=[ODD])[0]

    outer_weight_grad, inner_weight_grad = place(outer_ways), place(inner_ways)
    for number in LAST_STEPS:
        next(ways[number])
    grad = Out(piece[0], F32)
    (pair, _), (last_pair, (last_small,)) = (finish(way) for way in attention_ways)
    inner_bias_grad, query_bias_grad, value_bias_grad, *common = run(
        spread_small, [Out((size,), F32) for size in (hidden, width, width) + (model,) * 6], last_small)
    query_grad, key_grad = run(place_pieces, [grad] * 2, *pair, scalars=[ODD])
    value_grad, out_grad = run(place_pieces, [grad] * 2, *last_pair, scalars=[ODD])
    return (
        layer_output,
        input_grad,
        query_grad.T,
        query_bias_grad,
        key_grad.T,
        value_grad.T,
        value_bias_grad,
        out_grad,
        *common[:3],
        inner_weight_grad,
        inner_bias_grad,
        outer_weight_grad,
        *common[3:],
    )


def solution(mesh):
    in_specs = (
        P("dp", None),
        P("dp"),
        P(None, "tp"),
        P("tp"),
        P(None, "tp"),
        P(None, "tp"),
        P("tp"),
        P("tp", None),
        P(),
        P(),
        P(),
        P(None, "tp"),
        P("tp"),
        P("tp", None),
        P(),
        P(),
        P(),
        P("dp", None),
    )
    out_specs = (
        P(("dp", "tp"), None),
        P(("dp", "tp"), None),
        P(None, "tp"),
        P("tp"),
        P(None, "tp"),
        P(None, "tp"),
        P("tp"),
        P("tp", None),
        P(),
        P(),
        P(),
        P(None, "tp"),
        P("tp"),
        P("tp", None),
        P(),
        P(),
        P(),
    )
    return jax.shard_map(
        on_device, mesh=mesh, in_specs=in_specs, out_specs=out_specs, check_vma=False
    )
```

```python
import dataclasses

import jax
import jax.numpy as jnp
from jax import lax
from jax.experimental import pallas as pl
from jax.experimental.pallas import tpu as pltpu
from jax.sharding import PartitionSpec as P

HD = 64
EPSILON = 1e-05
BF16 = jnp.bfloat16
F32 = jnp.float32
LARGE = 24 * 2**20
STEP_ROWS = 128
BIAS_ROWS = 16
SMALL_ROWS = 8

TP, PLACE, ODD, UPPER, LENGTH = range(5)

ORDERED, PLACED, OWN, RAW = range(4)


def dot(left, right, left_dim=1, right_dim=0):
    return lax.dot_general(
        left, right, (((left_dim,), (right_dim,)), ((), ())), preferred_element_type=F32
    )


@dataclasses.dataclass(frozen=True)
class Afar:
    parts: tuple
    way: int = ORDERED

    def shape(self):
        return (sum(rows for _, _, rows in self.parts),) + self.parts[0][0].shape[1:]


def afar(*arrays, way=ORDERED):
    return Afar(tuple((a, 0, a.shape[0]) for a in arrays), way)


@dataclasses.dataclass(frozen=True)
class Out:
    shape: tuple
    dtype: jnp.dtype


class Traffic:
    def __init__(self, sems):
        self.sems, self.count = sems, 0
        self.coming, self.going, self.sent = {}, {}, []

    def copy(self, source, target):
        copy = pltpu.make_async_copy(source, target, self.sems.at[self.count])
        copy.start()
        self.count += 1
        return copy

    def need(self, *refs):
        for ref in refs:
            for copy in self.coming.pop(id(ref), ()):
                copy.wait()

    def send(self, *refs):
        for ref in refs:
            if id(ref) in self.going:
                self.sent.append(self.copy(ref, self.going.pop(id(ref))))

    def end(self):
        for copies in self.coming.values():
            for copy in copies:
                copy.wait()
        for ref in self.results:
            if id(ref) in self.going:
                self.send(ref)
        for copy in self.sent:
            copy.wait()


class Sequence:
    def __init__(self, scalars):
        self.last, self.scalars = None, scalars

    def ties(self):
        return [] if self.last is None else [pltpu.with_memory_space_constraint(*self.last)]

    def note(self, results, outs):
        smallest = min(range(len(outs)), key=lambda i: results[i].size)
        space = pltpu.HBM if isinstance(outs[smallest], Out) else pltpu.VMEM
        self.last = (results[smallest], space)

    def __call__(self, body, outs, *args, scalars=(), scratch=(), limit=LARGE):
        operands, sizes, fetched, copies = [self.scalars[i] for i in scalars], [], [], 0
        spaces = [pltpu.SMEM] * len(scalars)
        for arg in args:
            if isinstance(arg, Afar):
                operands += [pltpu.with_memory_space_constraint(a, pltpu.HBM) for a, _, _ in arg.parts]
                spaces += [pltpu.HBM] * len(arg.parts)
                sizes.append(len(arg.parts))
                copies += len(arg.parts)
                if arg.way != RAW:
                    fetched.append(pltpu.VMEM(arg.shape(), arg.parts[0][0].dtype))
            else:
                operands.append(arg)
                spaces.append(pltpu.VMEM)
                sizes.append(1)
        ties = self.ties()
        staged = [pltpu.VMEM(out.shape, out.dtype) for out in outs if isinstance(out, Out)]
        copies += len(staged)
        shapes = [
            pltpu.HBM(out.shape, out.dtype) if isinstance(out, Out) else pltpu.VMEM(*out) for out in outs
        ]

        def kernel(*refs):
            refs = list(refs)
            take = lambda n: [refs.pop(0) for _ in range(n)]
            info = {name: ref[0] for name, ref in zip(scalars, take(len(scalars)))}
            given = [take(n) for n in sizes]
            take(len(ties))
            results, buffers, stages, rest = take(len(outs)), take(len(fetched)), take(len(staged)), take(len(scratch))
            traffic = Traffic(refs[0] if refs else None)
            inputs = []
            for arg, sources in zip(args, given):
                if not isinstance(arg, Afar):
                    inputs += sources
                    continue
                if arg.way == RAW:
                    inputs.append(sources)
                    continue
                buffer = buffers.pop(0)
                inputs.append(buffer)
                copies, start = [], 0
                for i, (source, (_, first, rows)) in enumerate(zip(sources, arg.parts)):
                    if arg.way == OWN:
                        first = pl.multiple_of(info[TP] * rows, rows)
                    if arg.way == PLACED:
                        start = pl.multiple_of((info[PLACE] ^ i) * rows, rows)
                    copies.append(traffic.copy(source.at[pl.ds(first, rows)], buffer.at[pl.ds(start, rows)]))
                    start += rows
                traffic.coming[id(buffer)] = copies
            for i, out in enumerate(outs):
                if isinstance(out, Out):
                    stage = stages.pop(0)
                    traffic.going[id(stage)] = results[i]
                    results[i] = stage
            traffic.results = results
            body(traffic, info, *inputs, *results, *rest)
            traffic.end()

        results = pl.pallas_call(
            kernel,
            name=body.__name__,
            out_shape=shapes,
            in_specs=[pl.BlockSpec(memory_space=space) for space in spaces]
            + [pl.BlockSpec(memory_space=pl.ANY)] * len(ties),
            out_specs=[pl.BlockSpec(memory_space=pltpu.HBM if isinstance(o, Out) else pltpu.VMEM) for o in outs],
            scratch_shapes=fetched + staged + [pltpu.VMEM(shape, dtype) for shape, dtype in scratch]
            + ([pltpu.SemaphoreType.DMA((copies,))] if copies else []),
            compiler_params=pltpu.CompilerParams(vmem_limit_bytes=limit),
        )(*operands, *ties)
        self.note(results, outs)
        return results


def exchange(array, dp_bits, tp_bits):
    dp_size, tp_size = lax.axis_size("dp"), lax.axis_size("tp")
    pairs = [
        (d * tp_size + t, (d ^ dp_bits) * tp_size + (t ^ tp_bits))
        for d in range(dp_size)
        for t in range(tp_size)
    ]
    return lax.ppermute(array, ("dp", "tp"), pairs)


def later_masks():
    masks, bit = [], 4
    while bit < lax.axis_size("dp"):
        masks.append(6 if bit == 4 else bit)
        bit *= 2
    return masks


def folded(rows):
    return jnp.sum(rows.reshape(rows.shape[0] // 8, 8, rows.shape[1]), axis=0)


def normalize(values):
    average = jnp.mean(values, axis=-1, keepdims=True)
    centered = values - average
    spread = jnp.mean(centered * centered, axis=-1, keepdims=True)
    scale = lax.rsqrt(spread + EPSILON)
    return centered * scale, scale


def norm_backward(e, rows, scale):
    first = jnp.mean(e, axis=-1, keepdims=True)
    second = jnp.mean(e * rows, axis=-1, keepdims=True)
    return scale * (e - first - rows * second)


def row_steps(rows):
    return [slice(i, i + STEP_ROWS) for i in range(0, rows, STEP_ROWS)]


def as_row(ref):
    return ref[...].reshape(1, ref.shape[0])


def pick_attention(traffic, info, blocks, query_bias, value_bias, inner_bias, pieces, bias, values):
    rows = blocks[0].shape[0]
    targets = [pieces.at[pl.ds(n * rows, rows)] for n in (0, 1)]
    sems = [traffic.sems.at[traffic.count + n] for n in (0, 1)]
    traffic.count += 2
    for target, mask, sem in zip(targets, (0, 3), sems):
        for i, block in enumerate(blocks):
            @pl.when((info[PLACE] ^ mask) == i)
            def _():
                pltpu.make_async_copy(block, target, sem).start()
    traffic.need(query_bias, value_bias, inner_bias)
    values[...] = jnp.zeros_like(values)
    for i, vector in enumerate((query_bias, value_bias, inner_bias)):
        values[i : i + 1, : vector.shape[0]] = as_row(vector)
    high = values[...].astype(BF16).astype(F32)
    packed = jnp.concatenate([high, values[...] - high]).astype(BF16)
    pieces[2 * rows :] = packed
    bias[...] = packed
    for target, sem in zip(targets, sems):
        pltpu.make_async_copy(blocks[0], target, sem).wait()


def pick_own(traffic, info, weights, bias, own):
    traffic.need(weights)
    own[: weights.shape[0]] = weights[...]
    own[weights.shape[0] :] = bias[...]


def unpacked(bias):
    rows = bias[...].astype(F32)
    return rows[: BIAS_ROWS // 2] + rows[BIAS_ROWS // 2 :]


def pair_bias(bias_a, bias_b, width):
    both = bias_a + pltpu.roll(bias_b, width, 1)
    return both[0:1, : 2 * width], both[1:2, : 2 * width]


def pick_feed(traffic, info, blocks, *targets):
    copies = []
    for target, mask in zip(targets, (0, 3)):
        rows = target.shape[0] // 2
        for i, block in enumerate(blocks[:2]):
            at = pl.ds(pl.multiple_of((info[PLACE] ^ mask) * rows, rows), rows)
            copies.append(traffic.copy(block.at[at], target.at[pl.ds(i * rows, rows)]))
    for i, target in enumerate(targets):
        copies[2 * i].wait()
        copies[2 * i + 1].wait()
        traffic.send(target)


def stacked(low, high, part):
    width = low.shape[0] // 4
    at = slice(part * width, (part + 1) * width)
    return jnp.concatenate([low[at], high[at]])


def pair_weights(block_a, block_b):
    return jnp.concatenate([stacked(block_a, block_b, i) for i in range(3)])


def lone_head(transposed, head):
    part = transposed[head * HD : (head + 1) * HD]
    zeros = jnp.zeros_like(part)
    return jnp.concatenate([part, zeros] if head % 2 == 0 else [zeros, part])


def tile(array, head):
    start = head // 2 * 2 * HD
    return array[:, start : start + 2 * HD]


def hidden_keys(rows, length):
    return jnp.where(lax.broadcasted_iota(jnp.int32, (rows, 1), 0) < length, 0.0, -1e30)


def visible_scores(keys, queries_t, head, hidden):
    return dot(tile(keys, head), lone_head(queries_t, head)) + hidden


def attend_forward(traffic, info, inputs, block_a, block_b, bias_a, bias_b, qkv, context_t, log_total):
    rows = inputs.shape[0]
    width = block_a.shape[0] // 2
    heads = width // HD
    traffic.need(inputs, block_a, block_b)
    weights = pair_weights(block_a, block_b)
    both = dot(inputs[...], weights, 1, 1)
    query_bias, value_bias = pair_bias(bias_a, bias_b, width // 2)
    qkv[:, :width] = (both[:, :width] + query_bias).astype(BF16)
    qkv[:, width : 2 * width] = both[:, width : 2 * width].astype(BF16)
    qkv[:, 2 * width :] = (both[:, 2 * width :] + value_bias).astype(BF16)
    traffic.send(qkv)
    queries_t = (qkv[:, :width] * HD**-0.5).astype(BF16).T
    values_t = qkv[:, 2 * width :].T
    hidden = hidden_keys(rows, info[LENGTH])
    for h in range(heads):
        scores = visible_scores(qkv[:, width : 2 * width], queries_t, h, hidden)
        top = jnp.max(scores, axis=0, keepdims=True)
        raised = jnp.exp(scores - top)
        total = jnp.sum(raised, axis=0, keepdims=True)
        log_total[h : h + 1] = top + jnp.log(total)
        sums = dot(values_t[h * HD : (h + 1) * HD], raised.astype(BF16))
        context_t[h * HD : (h + 1) * HD] = (sums / total).astype(BF16)
    traffic.send(context_t)
    return dot(context_t[...], stacked(block_a, block_b, 3), 0, 0)


def near_pair(traffic, info, inputs, own, near, out_bias, qkv, context_t, log_total, after, bias_a, bias_b):
    rows = own.shape[0] - BIAS_ROWS
    bias_a[...], bias_b[...] = own[rows:], near[rows:]
    biases = unpacked(bias_a), unpacked(bias_b)
    blocks = own.at[pl.ds(0, rows)], near.at[pl.ds(0, rows)]
    branch = attend_forward(traffic, info, inputs, *blocks, *biases, qkv, context_t, log_total)
    after[...] = inputs[...].astype(F32) + as_row(out_bias) + branch


def far_pair(traffic, info, inputs, block_a, block_b, tail_a, tail_b, before, gain, shift,
             qkv, context_t, log_total, after, normed, normed_low, bias_a, bias_b):
    traffic.need(tail_a, tail_b)
    bias_a[...], bias_b[...] = tail_a[...], tail_b[...]
    biases = unpacked(bias_a), unpacked(bias_b)
    branch = attend_forward(traffic, info, inputs, block_a, block_b, *biases, qkv, context_t, log_total)
    traffic.need(before)
    after[...] = before[...] + branch
    traffic.send(after)
    for at in row_steps(after.shape[0]):
        out = normalize(after[at])[0] * as_row(gain) + as_row(shift)
        normed[at] = out
        normed_low[at] = out.astype(BF16)


def attend_backward(traffic, info, qkv, block_a, block_b, context_t, inputs, log_total, branch_grad, before,
                    part_a, *refs):
    *part_b, sums_a, sums_b, after, wide, probs = refs
    rows = inputs.shape[0]
    half = block_a.shape[0] // 4
    width = 2 * half
    heads = width // HD
    traffic.need(qkv)
    queries, keys, values = (qkv[:, i * width : (i + 1) * width] for i in range(3))
    queries_t = (queries * HD**-0.5).astype(BF16).T
    keys_t = keys.T
    hidden = hidden_keys(rows, info[LENGTH])
    for h in range(heads):
        scores = visible_scores(keys, queries_t, h, hidden)
        probs[h] = jnp.exp(scores - log_total[h : h + 1])
    traffic.need(block_a, block_b)
    grads = dot(branch_grad[...], stacked(block_a, block_b, 3), 1, 1).astype(BF16)
    grads_t = grads.T
    lane = lax.broadcasted_iota(jnp.int32, (rows, 2 * HD), 1)
    query_grads = []
    for t in range(heads // 2):
        pair = []
        for h in (2 * t, 2 * t + 1):
            prob_grad = dot(tile(values, h), lone_head(grads_t, h))
            inner = jnp.sum(probs[h] * prob_grad, axis=0, keepdims=True)
            score_grad = (probs[h] * (prob_grad - inner)).astype(BF16)
            value_grad = dot(probs[h].astype(BF16), tile(grads, h))
            key_grad = dot(score_grad, tile(queries, h)) * HD**-0.5
            query_grads.append(dot(keys_t[h * HD : (h + 1) * HD], score_grad) * HD**-0.5)
            pair.append((key_grad, value_grad))
        for i in (0, 1):
            at = (i + 1) * width + 2 * HD * t
            wide[:, at : at + 2 * HD] = jnp.where(lane < HD, pair[0][i], pair[1][i]).astype(BF16)
    traffic.need(context_t)
    out_part = dot(context_t[...], branch_grad[...]).astype(BF16)
    part_a[3 * half :] = out_part[:half]
    blocks_b = [out_part[half:]]
    query_grads = jnp.concatenate(query_grads).astype(BF16)
    wide[:, :width] = query_grads.T
    after[...] = before[...] + dot(wide[...], pair_weights(block_a, block_b))
    traffic.send(after)
    model = sums_a.shape[1]
    first = lax.broadcasted_iota(jnp.int32, sums_a.shape, 1) < half

    def summed(at):
        row = jnp.sum(wide[:, at : at + width].astype(F32), axis=0, keepdims=True)
        return jnp.broadcast_to(jnp.concatenate([row, jnp.zeros((1, model - width), F32)], axis=1), sums_a.shape)

    query_sum, value_sum = summed(0), summed(2 * width)
    for out, shift in ((sums_a, 0), (sums_b, model - half)):
        query, value = ((pltpu.roll(a, shift, 1) if shift else a) for a in (query_sum, value_sum))
        out[...] = jnp.where(first, query, 0.0) + pltpu.roll(jnp.where(first, value, 0.0), value_start(half), 1)
    traffic.need(inputs)
    for i in range(3):
        grad_t = query_grads if i == 0 else wide[:, i * width : (i + 1) * width].T
        block = dot(grad_t, inputs[...]).astype(BF16)
        part_a[i * half : (i + 1) * half] = block[:half]
        blocks_b.insert(i, block[half:])
    block_b = jnp.concatenate(blocks_b)
    size = part_b[0].shape[0]
    for i, part in enumerate(part_b):
        part[...] = block_b[i * size : (i + 1) * size]


def value_start(width):
    return -(-width // 128) * 128


def feed_slot(normed_low, inner, packed, active, slope):
    bias = unpacked(packed)[2:3]
    columns = 256
    for c in range(0, inner.shape[1], columns):
        at = slice(c, c + columns)
        hidden = dot(normed_low[...], inner[:, at]) + bias[:, at]
        half_erf = 0.5 * (1.0 + lax.erf(hidden * 0.5**0.5))
        active[:, at] = (hidden * half_erf).astype(BF16)
        slope[:, at] = (
            half_erf + hidden * jnp.exp(-0.5 * hidden * hidden) * 0.3989422804014327
        ).astype(BF16)


def feed_near(traffic, info, normed_low, normed, outer_bias, inner_a, inner_b, outer_a, outer_b, bias_a, bias_b,
              active_a, active_b, slope_a, slope_b, after):
    traffic.need(inner_a)
    feed_slot(normed_low, inner_a, bias_a, active_a, slope_a)
    traffic.send(active_a, slope_a)
    traffic.need(inner_b)
    feed_slot(normed_low, inner_b, bias_b, active_b, slope_b)
    traffic.send(active_b, slope_b)
    traffic.need(outer_a, outer_b)
    after[...] = (
        normed[...] + as_row(outer_bias) + dot(active_a[...], outer_a[...]) + dot(active_b[...], outer_b[...])
    )


def feed_far(traffic, info, normed_low, inner, bias, active, slope):
    traffic.need(inner)
    feed_slot(normed_low, inner, bias, active, slope)


def feed_out(traffic, info, active_a, active_b, outer_a, outer_b, before, gain, shift, cotangent,
             output, second_grad, result_grad, sums, total):
    traffic.need(outer_a, outer_b)
    total[...] = before[...] + dot(active_a[...], outer_a[...]) + dot(active_b[...], outer_b[...])
    traffic.need(cotangent)
    parts = [0.0] * 3
    for at in row_steps(total.shape[0]):
        rows, scale = normalize(total[at])
        output[at] = (rows * as_row(gain) + as_row(shift)).astype(BF16)
        grad = cotangent[at].astype(F32)
        back = norm_backward(grad * as_row(gain), rows, scale)
        second_grad[at] = back
        result_grad[at] = back.astype(BF16)
        parts = [c + folded(v) for c, v in zip(parts, (back, grad * rows, grad))]
    for i, part in enumerate(parts):
        sums[i : i + 1] = jnp.sum(part, axis=0, keepdims=True)


def near_grad(traffic, info, left, right, *chunks):
    total = dot(left[...], right[...], 0, 0).astype(BF16)
    rows = chunks[0].shape[0]
    for i, chunk in enumerate(chunks):
        chunk[...] = total[i * rows : (i + 1) * rows]


def far_grad(parts):
    def grad(traffic, info, left, right, *refs):
        traffic.need(left)
        total = dot(left[...], right[...], 0, 0)
        size = refs[-1].shape[0]
        got = jnp.concatenate([ref[...].astype(F32) for ref in refs[:parts]])
        for i, chunk in enumerate(refs[parts:]):
            at = slice(i * size, (i + 1) * size)
            chunk[...] = (total[at] + got[at]).astype(BF16)

    return grad


def hidden_pair(traffic, info, result_grad, outer_a, outer_b, slope_a, slope_b, grad_a, grad_b, sum_a, sum_b):
    for outer, slope, hidden_grad, bias_sum in (
        (outer_a, slope_a, grad_a, sum_a), (outer_b, slope_b, grad_b, sum_b)
    ):
        traffic.need(outer, slope)
        grad = (dot(result_grad[...], outer[...], 1, 1) * slope[...].astype(F32)).astype(BF16)
        hidden_grad[...] = grad
        bias_sum[...] = jnp.sum(grad.astype(F32), axis=0, keepdims=True)


def feed_back(traffic, info, result_grad, outer_2, outer_0, slope_2, slope_0, before, grad_3, grad_1,
              inner_3, inner_1, inner_2, inner_0, first_sum, gain,
              grad_2, grad_0, sum_2, sum_0, first_grad, branch_grad, sums, total):
    hidden_pair(traffic, info, result_grad, outer_2, outer_0, slope_2, slope_0, grad_2, grad_0, sum_2, sum_0)
    traffic.need(before)
    total[...] = before[...]
    for g, w in ((grad_3, inner_3), (grad_1, inner_1), (grad_2, inner_2), (grad_0, inner_0)):
        traffic.need(w)
        total[...] += dot(g[...], w[...], 1, 1)
    traffic.need(first_sum)
    parts = [0.0] * 3
    for at in row_steps(total.shape[0]):
        rows, scale = normalize(first_sum[at])
        grad = total[at]
        back = norm_backward(grad * as_row(gain), rows, scale)
        first_grad[at] = back
        branch_grad[at] = back.astype(BF16)
        parts = [c + folded(v) for c, v in zip(parts, (back, grad * rows, grad))]
    for i, part in enumerate(parts):
        sums[i : i + 1] = jnp.sum(part, axis=0, keepdims=True)


def add_parts(parts):
    def add(traffic, info, first, *refs):
        second = jnp.concatenate([ref[...].astype(F32) for ref in refs[:parts]])
        rows = refs[-1].shape[0]
        for i, chunk in enumerate(refs[parts:]):
            at = slice(i * rows, (i + 1) * rows)
            chunk[...] = (first[at].astype(F32) + second[at]).astype(BF16)

    return add


def split_rows(start):
    def split(traffic, info, own, got, *refs):
        if len(refs) > 2:
            small, small_got, *refs, small_out = refs
            small_out[...] = small[...] + small_got[...]
        keep, send = refs
        half = keep.shape[0]
        for out, side in ((keep, info[ODD]), (send, 1 - info[ODD])):
            at = pl.ds(pl.multiple_of(start + side * half, half), half)
            total = got[pl.ds(pl.multiple_of(side * half, half), half)].astype(F32)
            out[...] = (total + own[at].astype(F32)).astype(BF16)

    return split


def add_split(traffic, info, keep, got, *refs):
    mine, send = refs[-3:-1] if len(refs) == 5 else refs
    rows = mine.shape[0]
    for out, side in ((mine, info[UPPER]), (send, 1 - info[UPPER])):
        at = pl.ds(pl.multiple_of(side * rows, rows), rows)
        out[...] = (keep[at].astype(F32) + got[at].astype(F32)).astype(BF16)
    if len(refs) == 5:
        refs[-1][...] = refs[0][...] + refs[1][...]


def add_two(traffic, info, first, second, *refs):
    if len(refs) == 1:
        (out,) = refs
    else:
        small, got, out, small_out = refs
        small_out[...] = small[...] + got[...]
    out[...] = (first[...].astype(F32) + second[...].astype(F32)).astype(BF16)


def join(traffic, info, mine, got, whole):
    rows = mine.shape[0]
    for part, side in ((mine, info[UPPER]), (got, 1 - info[UPPER])):
        whole[pl.ds(pl.multiple_of(side * rows, rows), rows)] = part[...]


def place_block(traffic, info, *refs):
    *halves, out = refs
    rows = halves[0].shape[0]
    for c in range(0, len(halves), 2):
        for half, side in ((halves[c], info[ODD]), (halves[c + 1], 1 - info[ODD])):
            at = pl.ds(pl.multiple_of(c * rows + side * rows, rows), rows)
            out[at] = half[...].astype(F32)


def place_pieces(traffic, info, mine, other, first, second):
    for here, there, flag in ((first, second, 0), (second, first, 1)):
        @pl.when(info[ODD] == flag)
        def _():
            here[...] = mine[...].astype(F32)
            there[...] = other[...].astype(F32)


def collect_small(traffic, info, h0, h1, h2, h3, a0, a1, a2, a3, first_sums, second_sums, own, across, near):
    common = jnp.concatenate([first_sums[0:3], second_sums[0:3]])
    zeros = jnp.zeros_like(common)
    own[...] = jnp.concatenate([h0[...], a0[0:1], common])
    across[...] = jnp.concatenate([h2[...], a2[0:1], zeros])
    near[...] = jnp.concatenate([h1[...], a1[0:1], h3[...], a3[0:1], common, zeros])


def add_small(traffic, info, own, across, got, own_out, across_out):
    total = own[...] + jnp.concatenate([got[0:2], got[4:10]])
    own_out[...] = total
    across_out[...] = jnp.concatenate([across[0:2] + got[2:4], total[2:]])


def spread_small(traffic, info, small, inner, query, value, *common):
    inner[...] = small[0:1].reshape(inner.shape)
    width = query.shape[0]
    start = value_start(width)
    query[...] = small[1:2, :width].reshape(query.shape)
    value[...] = small[1:2, start : start + width].reshape(value.shape)
    for i, out in enumerate(common):
        out[...] = small[2 + i : 3 + i].reshape(out.shape)


OUTER_CHUNKS, INNER_CHUNKS, ATTENTION_CHUNKS = 1, 1, 2
NEAR_PARTS, ATTENTION_PARTS = 2, 2
STEPS = (2, 0, 2, 1, 3, 2, 0, 3, 1, 3, 2, 1, 3, 2)
LAST_STEPS = (3,)


def hold(run, *arrays):
    def mark(*refs):
        refs[-1][...] = jnp.zeros_like(refs[-1])

    ties = run.ties()
    anywhere = pl.BlockSpec(memory_space=pl.ANY)
    *results, token = pl.pallas_call(
        mark,
        name=mark.__name__,
        out_shape=[jax.ShapeDtypeStruct(a.shape, a.dtype) for a in arrays] + [pltpu.VMEM((8, 128), F32)],
        in_specs=[anywhere] * (len(arrays) + len(ties)),
        out_specs=[anywhere] * len(arrays) + [pl.BlockSpec(memory_space=pltpu.VMEM)],
        input_output_aliases={i: i for i in range(len(arrays))},
    )(*arrays, *ties)
    run.last = (token, pltpu.VMEM)
    return results


def chain(run, split, small):
    keep, send, *small = split(small)
    shape, rows = (keep.shape[0] // 2, keep.shape[1]), keep.shape[0]
    small_out = [(s.shape, F32) for s in small]
    partners = lambda mask: [b for s in small for b in (s, exchange(s, mask, 0))]
    got, pairs = exchange(send, 1, 0), partners(1)
    yield
    mine, send, *small = run(add_split, [(shape, BF16)] * 2 + small_out, keep, got, *pairs, scalars=[UPPER])
    got, pairs = exchange(send, 2, 0), partners(2)
    yield
    for mask in later_masks():
        mine, *small = run(add_two, [(shape, BF16)] + small_out, mine, got, *pairs)
        got, pairs = exchange(mine, mask, 0), partners(mask)
        yield
    mine, *small = run(add_two, [(shape, BF16)] + small_out, mine, got, *pairs)
    got = exchange(mine, 2, 0)
    yield
    (whole,) = run(join, [((rows, shape[1]), BF16)], mine, got, scalars=[UPPER])
    got = exchange(whole, 1, 0)
    yield
    return (whole, got), small


def on_device(
    layer_input,
    lengths,
    query_weight,
    query_bias,
    key_weight,
    value_weight,
    value_bias,
    out_weight,
    out_bias,
    first_gain,
    first_shift,
    inner_weight,
    inner_bias,
    outer_weight,
    outer_bias,
    second_gain,
    second_shift,
    cotangent,
):
    rows = layer_input.shape[0] // lax.axis_size("tp")
    model = layer_input.shape[1]
    width = query_weight.shape[1]
    hidden = inner_weight.shape[1]
    tp, dp = lax.axis_index("tp"), lax.axis_index("dp")
    upper = (dp >> 1) ^ (dp >> 2)
    run = Sequence(
        [s.reshape(1) for s in (tp, dp & 3, dp & 1, upper & 1)] + [lax.dynamic_slice_in_dim(lengths, tp, 1, 0)]
    )
    to_core = lambda a: exchange(a, 0, 1)
    to_x = lambda a: exchange(a, 0, 2)
    to_y = lambda a: exchange(a, 1, 0)
    to_z = lambda a: exchange(a, 2, 0)

    full, low = ((rows, model), F32), ((rows, model), BF16)
    piece, block = ((width, model), BF16), ((4 * width, model), BF16)
    square, wide = ((hidden, model), BF16), ((rows, hidden), BF16)
    bias_block, sums, small = ((BIAS_ROWS, model), BF16), ((8, model), F32), ((SMALL_ROWS, model), F32)
    inputs, own_grad = (Afar(((a, 0, rows),), OWN) for a in (layer_input, cotangent))

    own_weights = (query_weight.T, key_weight.T, value_weight.T, out_weight)
    sent, own_bias = run(
        pick_attention, [Out((2 * width + BIAS_ROWS, model), BF16), bias_block], afar(*own_weights, way=RAW),
        afar(query_bias), afar(value_bias), afar(inner_bias), scalars=[PLACE], scratch=[small])
    came = to_x(sent)
    (own,) = run(pick_own, [((4 * width + BIAS_ROWS, model), BF16)], afar(*own_weights), own_bias)
    near_own = to_core(own)
    half_square = Out((hidden // 2, model), BF16)
    sent = run(
        pick_feed, [half_square] * 2, afar(inner_weight, outer_weight, inner_weight, outer_weight, way=RAW),
        scalars=[PLACE])
    feed_came, feed_last_came = to_x(sent[0]), to_x(sent[1])
    near_inner, near_outer = hold(run, to_core(inner_weight), to_core(outer_weight))

    near_scalars, far_scalars = [TP, LENGTH], [TP, PLACE, LENGTH]
    seen = [Out((rows, 6 * width), BF16), Out((2 * width, rows), BF16), ((8, rows), F32)]
    near_qkv, near_context, near_log, partial, own_bias, near_bias = run(
        near_pair, seen + [Out(*full)] + [bias_block] * 2, inputs, own, near_own, out_bias, scalars=near_scalars)
    (came,) = hold(run, came)
    spread = came[:width]
    from_y, from_z, came_near = to_y(spread), to_z(spread), to_core(came)
    from_y, from_z, came_near = hold(run, from_y, from_z, came_near)
    near_y, near_z = hold(run, to_core(from_y), to_core(from_z))
    (feed_came,) = hold(run, feed_came)
    feed_y, feed_z = to_y(feed_came), to_z(feed_came)
    own_block, near_block = afar(*own_weights), Afar(((near_own, 0, 4 * width),))
    attention_parts = lambda a, b, c: Afar(((a, 0, width), (b, 0, width), (c, 0, width), (a, width, width)), PLACED)
    tail = lambda a: Afar(((a, 2 * width, BIAS_ROWS),))
    far_blocks = (attention_parts(came, from_y, from_z), attention_parts(came_near, near_y, near_z))
    far_qkv, far_context, far_log, first_sum, normed, normed_low, bias_2, bias_3 = run(
        far_pair, seen + [Out(*full), full, low] + [bias_block] * 2, inputs, *far_blocks, tail(came), tail(came_near),
        afar(partial), first_gain, first_shift, scalars=far_scalars)

    active_0, active_1, slope_0, slope_1, partial = run(
        feed_near, [Out(*wide), wide, Out(*wide), Out(*wide), full], normed_low, normed, outer_bias, afar(inner_weight), afar(near_inner),
        afar(outer_weight), afar(near_outer), own_bias, near_bias)
    far_feed = hold(run, feed_came, feed_y, feed_z, feed_last_came)
    near_feed = tuple(to_core(a) for a in far_feed)
    quarter = hidden // 4
    inner_2, inner_3 = (Afar(tuple((a, 0, quarter) for a in f), PLACED) for f in (far_feed, near_feed))
    outer_2, outer_3 = (Afar(tuple((a, quarter, quarter) for a in f), PLACED) for f in (far_feed, near_feed))
    (active_2, slope_2), (active_3, slope_3) = (
        run(feed_far, [wide] * 2, normed_low, inner, bias, scalars=[PLACE])
        for inner, bias in ((inner_2, bias_2), (inner_3, bias_3))
    )
    layer_output, second_grad, result_grad, second_sums = run(
        feed_out, [Out(*low), Out(*full), low, sums], active_2, active_3, outer_2, outer_3, partial,
        second_gain, second_shift, own_grad, scalars=[TP, PLACE], scratch=[full])

    def near(left, right, n):
        chunks = run(near_grad, [((hidden // n, model), BF16)] * n, left, right)
        return [to_core(a) for a in chunks]

    outer_got_3 = near(active_3, result_grad, 1)
    outer_got_1 = near(active_1, result_grad, 1)
    hidden_out = [wide, wide] + [((1, hidden), F32)] * 2
    hidden_3, hidden_1, sum_3, sum_1 = run(
        hidden_pair, hidden_out, result_grad, outer_3, afar(near_outer), slope_3, afar(slope_1), scalars=[PLACE])
    far = lambda left, right, got, n: run(
        far_grad(len(got)), [((hidden // n, model), BF16)] * n, left, right, *got)
    outer_x = [to_x(a) for a in far(active_2, result_grad, outer_got_3, OUTER_CHUNKS)]
    (outer_own,) = far(afar(active_0), result_grad, outer_got_1, 1)
    inner_got_3 = near(normed_low, hidden_3, NEAR_PARTS)
    inner_got_1 = near(normed_low, hidden_1, NEAR_PARTS)
    hidden_2, hidden_0, sum_2, sum_0, first_grad, branch_grad, first_sums = run(
        feed_back, hidden_out + [full, low, sums], result_grad, outer_2, afar(outer_weight), slope_2, afar(slope_0),
        afar(second_grad), hidden_3, hidden_1, inner_3, afar(near_inner), inner_2, afar(inner_weight), afar(first_sum),
        first_gain, scalars=[PLACE], scratch=[full])
    inner_x = [to_x(a) for a in far(normed_low, hidden_2, inner_got_3, INNER_CHUNKS)]
    (inner_own,) = far(normed_low, hidden_0, inner_got_1, 1)

    rooms = [((rows, 6 * width), BF16), ((2 * width // HD, rows, rows), F32)]
    part = ((4 * width // ATTENTION_PARTS, model), BF16)
    part_2, *part_3, sums_2, sums_3, partial = run(
        attend_backward, [block] + [part] * ATTENTION_PARTS + [sums, sums, full], afar(far_qkv), *far_blocks, afar(far_context),
        inputs, far_log, branch_grad, first_grad, scalars=far_scalars, scratch=rooms)
    got_3 = [to_core(a) for a in part_3]

    def ways_of(own, got, small=()):
        size = got[0].shape[0]

        def split_of(chunk):
            return lambda small: run(
                split_rows(chunk * size), [((size // 2, model), BF16)] * 2 + [(s.shape, F32) for s in small[:1]], own,
                got[chunk], *small, scalars=[ODD])

        return [chain(run, split_of(i), small if i == len(got) - 1 else ()) for i in range(len(got))]

    outer_ways, inner_ways = ways_of(outer_own, outer_x), ways_of(inner_own, inner_x)
    next(outer_ways[0])
    part_0, part_1, sums_0, sums_1, input_grad = run(
        attend_backward, [block, block, sums, sums, Out(*full)], afar(near_qkv), own_block, near_block,
        afar(near_context), inputs, near_log, branch_grad, partial, scalars=near_scalars, scratch=rooms)
    got_1 = to_core(part_1)
    next(outer_ways[0])
    chunk = ((4 * width // ATTENTION_CHUNKS, model), BF16)
    attention_x = [to_x(a) for a in run(
        add_parts(ATTENTION_PARTS), [chunk] * ATTENTION_CHUNKS, part_2, *got_3)]
    next(inner_ways[0])
    next(outer_ways[0])
    next(inner_ways[0])
    small_own, small_across, small_near = run(
        collect_small, [small, small, ((2 * SMALL_ROWS, model), F32)], sum_0, sum_1, sum_2, sum_3,
        sums_0, sums_1, sums_2, sums_3, first_sums, second_sums)
    small_near = to_core(small_near)
    (attention_own,) = run(add_parts(1), [block], part_0, got_1)
    small_own, small_across = run(add_small, [small, small], small_own, small_across, small_near)
    attention_ways = ways_of(attention_own, attention_x, (small_own, to_x(small_across)))
    ways = outer_ways + inner_ways + attention_ways
    for number in STEPS:
        next(ways[number])

    def finish(way):
        while True:
            try:
                next(way)
            except StopIteration as stop:
                return stop.value

    def place(ways):
        halves = [half for way in ways for half in finish(way)[0]]
        return run(place_block, [Out(square[0], F32)], *halves, scalars=[ODD])[0]

    outer_weight_grad = place(outer_ways)
    for number in LAST_STEPS:
        next(ways[number])
    inner_weight_grad = place(inner_ways)
    grad = Out(piece[0], F32)
    (pair, _), (last_pair, (last_small,)) = (finish(way) for way in attention_ways)
    inner_bias_grad, query_bias_grad, value_bias_grad, *common = run(
        spread_small, [Out((size,), F32) for size in (hidden, width, width) + (model,) * 6], last_small)
    query_grad, key_grad = run(place_pieces, [grad] * 2, *pair, scalars=[ODD])
    value_grad, out_grad = run(place_pieces, [grad] * 2, *last_pair, scalars=[ODD])
    return (
        layer_output,
        input_grad,
        query_grad.T,
        query_bias_grad,
        key_grad.T,
        value_grad.T,
        value_bias_grad,
        out_grad,
        *common[:3],
        inner_weight_grad,
        inner_bias_grad,
        outer_weight_grad,
        *common[3:],
    )


def solution(mesh):
    in_specs = (
        P("dp", None),
        P("dp"),
        P(None, "tp"),
        P("tp"),
        P(None, "tp"),
        P(None, "tp"),
        P("tp"),
        P("tp", None),
        P(),
        P(),
        P(),
        P(None, "tp"),
        P("tp"),
        P("tp", None),
        P(),
        P(),
        P(),
        P("dp", None),
    )
    out_specs = (
        P(("dp", "tp"), None),
        P(("dp", "tp"), None),
        P(None, "tp"),
        P("tp"),
        P(None, "tp"),
        P(None, "tp"),
        P("tp"),
        P("tp", None),
        P(),
        P(),
        P(),
        P(None, "tp"),
        P("tp"),
        P("tp", None),
        P(),
        P(),
        P(),
    )
    return jax.shard_map(
        on_device, mesh=mesh, in_specs=in_specs, out_specs=out_specs, check_vma=False
    )
```

```python
import dataclasses

import jax
import jax.numpy as jnp
from jax import lax
from jax.experimental import pallas as pl
from jax.experimental.pallas import tpu as pltpu
from jax.sharding import PartitionSpec as P

HD = 64
EPSILON = 1e-05
BF16 = jnp.bfloat16
F32 = jnp.float32
LARGE = 24 * 2**20
STEP_ROWS = 128
BIAS_ROWS = 16
SMALL_ROWS = 8

TP, PLACE, ODD, UPPER, LENGTHS = range(5)

ORDERED, PLACED, OWN, RAW = range(4)


def dot(left, right, left_dim=1, right_dim=0):
    return lax.dot_general(
        left, right, (((left_dim,), (right_dim,)), ((), ())), preferred_element_type=F32
    )


@dataclasses.dataclass(frozen=True)
class Afar:
    parts: tuple
    way: int = ORDERED

    def shape(self):
        return (sum(rows for _, _, rows in self.parts),) + self.parts[0][0].shape[1:]


def afar(*arrays, way=ORDERED):
    return Afar(tuple((a, 0, a.shape[0]) for a in arrays), way)


@dataclasses.dataclass(frozen=True)
class Out:
    shape: tuple
    dtype: jnp.dtype


class Traffic:
    def __init__(self, sems):
        self.sems, self.count = sems, 0
        self.coming, self.going, self.sent = {}, {}, []

    def copy(self, source, target):
        copy = pltpu.make_async_copy(source, target, self.sems.at[self.count])
        copy.start()
        self.count += 1
        return copy

    def need(self, *refs):
        for ref in refs:
            for copy in self.coming.pop(id(ref), ()):
                copy.wait()

    def send(self, *refs):
        for ref in refs:
            if id(ref) in self.going:
                self.sent.append(self.copy(ref, self.going.pop(id(ref))))

    def end(self):
        for copies in self.coming.values():
            for copy in copies:
                copy.wait()
        for ref in self.results:
            if id(ref) in self.going:
                self.send(ref)
        for copy in self.sent:
            copy.wait()


class Sequence:
    def __init__(self, scalars):
        self.last, self.scalars = None, scalars

    def ties(self):
        return [] if self.last is None else [pltpu.with_memory_space_constraint(*self.last)]

    def note(self, results, outs):
        smallest = min(range(len(outs)), key=lambda i: results[i].size)
        space = pltpu.HBM if isinstance(outs[smallest], Out) else pltpu.VMEM
        self.last = (results[smallest], space)

    def __call__(self, body, outs, *args, scalars=(), scratch=(), limit=LARGE):
        operands, sizes, fetched, copies = [self.scalars[i] for i in scalars], [], [], 0
        spaces = [pltpu.SMEM] * len(scalars)
        for arg in args:
            if isinstance(arg, Afar):
                operands += [pltpu.with_memory_space_constraint(a, pltpu.HBM) for a, _, _ in arg.parts]
                spaces += [pltpu.HBM] * len(arg.parts)
                sizes.append(len(arg.parts))
                copies += len(arg.parts)
                if arg.way != RAW:
                    fetched.append(pltpu.VMEM(arg.shape(), arg.parts[0][0].dtype))
            else:
                operands.append(arg)
                spaces.append(pltpu.VMEM)
                sizes.append(1)
        ties = self.ties()
        staged = [pltpu.VMEM(out.shape, out.dtype) for out in outs if isinstance(out, Out)]
        copies += len(staged)
        shapes = [
            pltpu.HBM(out.shape, out.dtype) if isinstance(out, Out) else pltpu.VMEM(*out) for out in outs
        ]

        def kernel(*refs):
            refs = list(refs)
            take = lambda n: [refs.pop(0) for _ in range(n)]
            info = {n: ref if n == LENGTHS else ref[0] for n, ref in zip(scalars, take(len(scalars)))}
            given = [take(n) for n in sizes]
            take(len(ties))
            results, buffers, stages, rest = take(len(outs)), take(len(fetched)), take(len(staged)), take(len(scratch))
            traffic = Traffic(refs[0] if refs else None)
            inputs = []
            for arg, sources in zip(args, given):
                if not isinstance(arg, Afar):
                    inputs += sources
                    continue
                if arg.way == RAW:
                    inputs.append(sources)
                    continue
                buffer = buffers.pop(0)
                inputs.append(buffer)
                copies, start = [], 0
                for i, (source, (_, first, rows)) in enumerate(zip(sources, arg.parts)):
                    if arg.way == OWN:
                        first = pl.multiple_of((info[TP] ^ first) * rows, rows)
                    if arg.way == PLACED:
                        start = pl.multiple_of((info[PLACE] ^ i) * rows, rows)
                    copies.append(traffic.copy(source.at[pl.ds(first, rows)], buffer.at[pl.ds(start, rows)]))
                    start += rows
                traffic.coming[id(buffer)] = copies
            for i, out in enumerate(outs):
                if isinstance(out, Out):
                    stage = stages.pop(0)
                    traffic.going[id(stage)] = results[i]
                    results[i] = stage
            traffic.results = results
            body(traffic, info, *inputs, *results, *rest)
            traffic.end()

        results = pl.pallas_call(
            kernel,
            name=body.__name__,
            out_shape=shapes,
            in_specs=[pl.BlockSpec(memory_space=space) for space in spaces]
            + [pl.BlockSpec(memory_space=pl.ANY)] * len(ties),
            out_specs=[pl.BlockSpec(memory_space=pltpu.HBM if isinstance(o, Out) else pltpu.VMEM) for o in outs],
            scratch_shapes=fetched + staged + [pltpu.VMEM(shape, dtype) for shape, dtype in scratch]
            + ([pltpu.SemaphoreType.DMA((copies,))] if copies else []),
            compiler_params=pltpu.CompilerParams(vmem_limit_bytes=limit),
        )(*operands, *ties)
        self.note(results, outs)
        return results


def exchange(array, dp_bits, tp_bits):
    dp_size, tp_size = lax.axis_size("dp"), lax.axis_size("tp")
    pairs = [
        (d * tp_size + t, (d ^ dp_bits) * tp_size + (t ^ tp_bits))
        for d in range(dp_size)
        for t in range(tp_size)
    ]
    return lax.ppermute(array, ("dp", "tp"), pairs)


def later_masks():
    masks, bit = [], 4
    while bit < lax.axis_size("dp"):
        masks.append(6 if bit == 4 else bit)
        bit *= 2
    return masks


def folded(rows):
    return jnp.sum(rows.reshape(rows.shape[0] // 8, 8, rows.shape[1]), axis=0)


def normalize(values):
    average = jnp.mean(values, axis=-1, keepdims=True)
    centered = values - average
    spread = jnp.mean(centered * centered, axis=-1, keepdims=True)
    scale = lax.rsqrt(spread + EPSILON)
    return centered * scale, scale


def norm_backward(e, rows, scale):
    first = jnp.mean(e, axis=-1, keepdims=True)
    second = jnp.mean(e * rows, axis=-1, keepdims=True)
    return scale * (e - first - rows * second)


def row_steps(rows):
    return [slice(i, i + STEP_ROWS) for i in range(0, rows, STEP_ROWS)]


def as_row(ref):
    return ref[...].reshape(1, ref.shape[0])


def packed(values):
    high = values.astype(BF16).astype(F32)
    return jnp.concatenate([high, values - high]).astype(BF16)


def unpacked(pairs):
    rows = pairs[...].astype(F32)
    return rows[: BIAS_ROWS // 2] + rows[BIAS_ROWS // 2 :]


def folded_one(part):
    rows, columns = part.shape
    third = rows // 3
    last = part[2 * third :]
    side = jnp.concatenate([last[:, : columns // 2], last[:, columns // 2 :]])
    return jnp.concatenate([part[: 2 * third], side], axis=1)


def unfolded_one(block):
    rows = block.shape[0] // 2
    columns = block.shape[1] * 2 // 3
    last = jnp.concatenate([block[:rows, columns:], block[rows:, columns:]], axis=1)
    return jnp.concatenate([block[:, :columns], last])


def folded_two(first, second):
    half, third = second.shape[1] // 2, second.shape[0] // 3
    below = [second[i * third : (i + 1) * third, half:] for i in range(3)]
    return jnp.concatenate(
        [jnp.concatenate([first, second[:, :half]], axis=1), jnp.concatenate(below, axis=1)])


def unfolded_first(block):
    rows, columns = block.shape[0] * 3 // 4, block.shape[1] * 2 // 3
    return block[:rows, :columns]


def unfolded_second(block):
    rows, columns = block.shape[0] * 3 // 4, block.shape[1] * 2 // 3
    below = block[rows:]
    right = jnp.concatenate([below[:, i * columns // 2 : (i + 1) * columns // 2] for i in range(3)])
    return jnp.concatenate([block[:rows, columns:], right], axis=1)


def pick_out(traffic, info, out_weight, inner_bias, sent, values):
    traffic.need(out_weight, inner_bias)
    rows = out_weight.shape[0]
    values[...] = jnp.zeros_like(values)
    values[0:1] = as_row(inner_bias)
    sent[:rows] = out_weight[...]
    sent[rows:] = packed(values[...])


def pick_feed(traffic, info, blocks, target):
    rows = target.shape[0] // 2
    copies = []
    for i, block in enumerate(blocks):
        at = pl.ds(pl.multiple_of(info[PLACE] * rows, rows), rows)
        copies.append(traffic.copy(block.at[at], target.at[pl.ds(i * rows, rows)]))
    for copy in copies:
        copy.wait()


def pick_last_feed(traffic, info, blocks, target):
    pick_feed(traffic, {PLACE: info[PLACE] ^ 3}, blocks, target)


def lone_head(transposed, head):
    part = transposed[head * HD : (head + 1) * HD]
    if head // 2 * 2 + 1 >= transposed.shape[0] // HD:
        return part
    zeros = jnp.zeros_like(part)
    return jnp.concatenate([part, zeros] if head % 2 == 0 else [zeros, part])


def tile(array, head):
    start = head // 2 * 2 * HD
    return array[:, start : start + 2 * HD]


def hidden_keys(rows, length):
    return jnp.where(lax.broadcasted_iota(jnp.int32, (rows, 1), 0) < length, 0.0, -1e30)


def visible_scores(keys, queries_t, head, hidden):
    return dot(tile(keys, head), lone_head(queries_t, head)) + hidden


def heads_forward(masks):
    def forward(traffic, info, inputs, query_weight, key_weight, value_weight, query_bias, value_bias, sent, *refs):
        *own, qkv, log_total = refs
        width = query_weight.shape[0]
        rows = inputs.shape[0] // 2
        heads = width // HD
        contexts = []
        traffic.need(query_weight, key_weight, value_weight, query_bias, value_bias, inputs)
        for i, mask in enumerate(masks):
            x = inputs[i * rows : (i + 1) * rows]
            queries = (dot(x, query_weight[...], 1, 1) + as_row(query_bias)).astype(BF16)
            keys = dot(x, key_weight[...], 1, 1).astype(BF16)
            vals = (dot(x, value_weight[...], 1, 1) + as_row(value_bias)).astype(BF16)
            for j, part in enumerate((queries, keys, vals)):
                qkv[(3 * i + j) * rows : (3 * i + j + 1) * rows] = part
            queries_t = (queries * HD**-0.5).astype(BF16).T
            values_t = vals.T
            hidden = hidden_keys(rows, info[LENGTHS][info[TP] ^ mask])
            context = []
            for h in range(heads):
                scores = visible_scores(keys, queries_t, h, hidden)
                top = jnp.max(scores, axis=0, keepdims=True)
                raised = jnp.exp(scores - top)
                total = jnp.sum(raised, axis=0, keepdims=True)
                log_total[i * heads + h : i * heads + h + 1] = top + jnp.log(total)
                sums = dot(values_t[h * HD : (h + 1) * HD], raised.astype(BF16))
                context.append((sums / total).astype(BF16))
            contexts.append(jnp.concatenate(context))
        if own:
            own[0][...] = contexts[1]
            sent[...] = folded_one(contexts[0])
        else:
            sent[...] = folded_two(*contexts)

    return forward


def all_contexts(own, near, far, far_near):
    return jnp.concatenate([own[...], unfolded_one(near[...]), unfolded_first(far[...]), unfolded_second(far_near[...])])


def project(traffic, info, inputs, own_context, near, far, far_near, weights, tail_1, tail_2, tail_3, out_bias,
            gain, shift, first_sum, normed, normed_low, bias_1, bias_2, bias_3):
    traffic.need(near, far, far_near, weights)
    branch = dot(all_contexts(own_context, near, far, far_near), weights[...], 0, 0)
    traffic.need(inputs)
    first_sum[...] = inputs[...].astype(F32) + as_row(out_bias) + branch
    traffic.send(first_sum)
    for at in row_steps(first_sum.shape[0]):
        out = normalize(first_sum[at])[0] * as_row(gain) + as_row(shift)
        normed[at] = out
        normed_low[at] = out.astype(BF16)
    traffic.need(tail_1, tail_2, tail_3)
    for tail, bias in ((tail_1, bias_1), (tail_2, bias_2), (tail_3, bias_3)):
        bias[...] = unpacked(tail)


def context_back(traffic, info, branch_grad, weights, own_context, near, far, far_near, own_grad, grad_1, grad_2,
                 grad_3, near_parts, part_0, part_2):
    traffic.need(weights)
    grads = dot(weights[...], branch_grad[...], 1, 1).astype(BF16)
    width = grads.shape[0] // 4
    slot = lambda array, s: array[s * width : (s + 1) * width]
    own_grad[...] = slot(grads, 0)
    for i, sent in enumerate((grad_1, grad_2, grad_3)):
        sent[...] = folded_one(slot(grads, 1 + i))
    traffic.need(near, far, far_near)
    parts = dot(all_contexts(own_context, near, far, far_near), branch_grad[...]).astype(BF16)
    part_0[...], part_2[...] = slot(parts, 0), slot(parts, 2)
    near_parts[:width], near_parts[width:] = slot(parts, 1), slot(parts, 3)


def heads_backward(masks, unfold):
    def backward(traffic, info, qkv, context_a, context_b, inputs, query_weight, key_weight, value_weight, log_total, *refs):
        wide, probs = refs[-2:]
        first = len(refs) == 7
        before, (grad_a, grad_b, sums_out, *weight_sums) = (refs[:1], refs[1:-2]) if first else (refs[:2], refs[2:-2])
        rows = inputs.shape[0] // 2
        width = query_weight.shape[0]
        heads = width // HD
        traffic.need(qkv)
        take = lambda i, j: qkv[(3 * i + j) * rows : (3 * i + j + 1) * rows]
        for i, mask in enumerate(masks):
            queries_t = (take(i, 0) * HD**-0.5).astype(BF16).T
            hidden = hidden_keys(rows, info[LENGTHS][info[TP] ^ mask])
            for h in range(heads):
                n = i * heads + h
                probs[n] = jnp.exp(visible_scores(take(i, 1), queries_t, h, hidden) - log_total[n : n + 1])
        traffic.need(context_a, context_b)
        lane = lax.broadcasted_iota(jnp.int32, (rows, 2 * HD), 1)
        query_grads = []
        for i, context in enumerate((context_a, context_b)):
            grads_t = unfold[i](context[...])
            grads = grads_t.T
            queries, keys, vals = (take(i, j) for j in range(3))
            keys_t = keys.T
            query_parts, pairs = [], []
            for h in range(heads):
                n = i * heads + h
                prob_grad = dot(tile(vals, h), lone_head(grads_t, h))
                inner = jnp.sum(probs[n] * prob_grad, axis=0, keepdims=True)
                score_grad = (probs[n] * (prob_grad - inner)).astype(BF16)
                value_grad = dot(probs[n].astype(BF16), tile(grads, h))
                key_grad = dot(score_grad, tile(queries, h)) * HD**-0.5
                query_parts.append(dot(keys_t[h * HD : (h + 1) * HD], score_grad) * HD**-0.5)
                pairs.append((key_grad, value_grad))
            query_grads.append(jnp.concatenate(query_parts).astype(BF16))
            wide[3 * i] = query_grads[i].T
            for j in (0, 1):
                at = 3 * i + 1 + j
                for h in range(0, heads, 2):
                    if h + 1 < heads:
                        wide[at, :, h * HD : (h + 2) * HD] = jnp.where(
                            lane < HD, pairs[h][j], pairs[h + 1][j]).astype(BF16)
                    else:
                        wide[at, :, h * HD :] = pairs[h][j].astype(BF16)
        traffic.need(query_weight, key_weight, value_weight)
        for i, out in enumerate((grad_a, grad_b)):
            total = dot(wide[3 * i], query_weight[...]) + dot(wide[3 * i + 1], key_weight[...])
            total = total + dot(wide[3 * i + 2], value_weight[...])
            if out.dtype == F32:
                traffic.need(before[0])
                out[...] = before[0][...] + total
                traffic.send(out)
            else:
                out[...] = total.astype(BF16)
        model = sums_out.shape[1]

        def summed(j):
            row = sum(jnp.sum(wide[3 * i + j].astype(F32), axis=0, keepdims=True) for i in (0, 1))
            return jnp.concatenate([row, jnp.zeros((1, model - width), F32)], axis=1)

        eight = lambda row: jnp.broadcast_to(row, sums_out.shape)
        sums = eight(summed(0)) + pltpu.roll(eight(summed(2)), value_start(width), 1)
        traffic.need(inputs)
        x = inputs[...]
        for j in range(3):
            if j == 0:
                grad_t = jnp.concatenate(query_grads, axis=1)
            else:
                grad_t = jnp.concatenate([wide[j].T, wide[3 + j].T], axis=1)
            block = dot(grad_t, x)
            at = slice(j * width, (j + 1) * width)
            if first:
                weight_sums[0][at] = block
            else:
                weight_sums[0][at] = (before[0][at] + block).astype(BF16)
        sums_out[...] = sums if first else before[1][...] + sums

    return backward


def value_start(width):
    return -(-width // 128) * 128


def feed_slot(normed_low, inner, biases, active, slope):
    bias = biases[...].reshape(1, biases.shape[0]) if len(biases.shape) == 1 else biases[0:1]
    columns = 256
    for c in range(0, inner.shape[1], columns):
        at = slice(c, c + columns)
        hidden = dot(normed_low[...], inner[:, at]) + bias[:, at]
        half_erf = 0.5 * (1.0 + lax.erf(hidden * 0.5**0.5))
        active[:, at] = (hidden * half_erf).astype(BF16)
        slope[:, at] = (
            half_erf + hidden * jnp.exp(-0.5 * hidden * hidden) * 0.3989422804014327
        ).astype(BF16)


def feed_near(traffic, info, normed_low, normed, outer_bias, inner_a, inner_b, outer_a, outer_b, bias_a, bias_b,
              active_a, active_b, slope_a, slope_b, after):
    traffic.need(inner_a)
    feed_slot(normed_low, inner_a, bias_a, active_a, slope_a)
    traffic.send(active_a, slope_a)
    traffic.need(inner_b)
    feed_slot(normed_low, inner_b, bias_b, active_b, slope_b)
    traffic.send(active_b, slope_b)
    traffic.need(outer_a, outer_b)
    after[...] = (
        normed[...] + as_row(outer_bias) + dot(active_a[...], outer_a[...]) + dot(active_b[...], outer_b[...])
    )


def feed_far(traffic, info, normed_low, inner, bias, active, slope):
    traffic.need(inner)
    feed_slot(normed_low, inner, bias, active, slope)


def feed_out(traffic, info, active_a, active_b, outer_a, outer_b, before, gain, shift, cotangent,
             output, second_grad, result_grad, sums, total):
    traffic.need(outer_a, outer_b)
    total[...] = before[...] + dot(active_a[...], outer_a[...]) + dot(active_b[...], outer_b[...])
    traffic.need(cotangent)
    parts = [0.0] * 3
    for at in row_steps(total.shape[0]):
        rows, scale = normalize(total[at])
        output[at] = (rows * as_row(gain) + as_row(shift)).astype(BF16)
        grad = cotangent[at].astype(F32)
        back = norm_backward(grad * as_row(gain), rows, scale)
        second_grad[at] = back
        result_grad[at] = back.astype(BF16)
        parts = [c + folded(v) for c, v in zip(parts, (back, grad * rows, grad))]
    for i, part in enumerate(parts):
        sums[i : i + 1] = jnp.sum(part, axis=0, keepdims=True)


def near_grad(traffic, info, left, right, *chunks):
    traffic.need(left)
    total = dot(left[...], right[...], 0, 0).astype(BF16)
    rows = chunks[0].shape[0]
    for i, chunk in enumerate(chunks):
        chunk[...] = total[i * rows : (i + 1) * rows]


def far_grad(parts):
    def grad(traffic, info, left, right, *refs):
        traffic.need(left)
        total = dot(left[...], right[...], 0, 0)
        total = total + jnp.concatenate([ref[...].astype(F32) for ref in refs[:parts]])
        at = 0
        for chunk in refs[parts:]:
            rows = chunk.shape[0]
            chunk[...] = total[at : at + rows].astype(BF16)
            at += rows

    return grad


def hidden_pair(traffic, info, result_grad, outer_a, outer_b, slope_a, slope_b, grad_a, grad_b, sum_a, sum_b):
    for outer, slope, hidden_grad, bias_sum in (
        (outer_a, slope_a, grad_a, sum_a), (outer_b, slope_b, grad_b, sum_b)
    ):
        traffic.need(outer, slope)
        grad = (dot(result_grad[...], outer[...], 1, 1) * slope[...].astype(F32)).astype(BF16)
        hidden_grad[...] = grad
        bias_sum[...] = jnp.sum(grad.astype(F32), axis=0, keepdims=True)


def feed_back(traffic, info, result_grad, outer_2, outer_0, slope_2, slope_0, before, grad_3, grad_1,
              inner_3, inner_1, inner_2, inner_0, first_sum, gain,
              grad_2, grad_0, sum_2, sum_0, first_grad, branch_grad, sums, total):
    hidden_pair(traffic, info, result_grad, outer_2, outer_0, slope_2, slope_0, grad_2, grad_0, sum_2, sum_0)
    traffic.need(before)
    total[...] = before[...]
    for g, w in ((grad_3, inner_3), (grad_1, inner_1), (grad_2, inner_2), (grad_0, inner_0)):
        traffic.need(w)
        total[...] += dot(g[...], w[...], 1, 1)
    traffic.need(first_sum)
    parts = [0.0] * 3
    for at in row_steps(total.shape[0]):
        rows, scale = normalize(first_sum[at])
        grad = total[at]
        back = norm_backward(grad * as_row(gain), rows, scale)
        first_grad[at] = back
        branch_grad[at] = back.astype(BF16)
        parts = [c + folded(v) for c, v in zip(parts, (back, grad * rows, grad))]
    for i, part in enumerate(parts):
        sums[i : i + 1] = jnp.sum(part, axis=0, keepdims=True)


def add_out(traffic, info, part_0, part_2, got, own, across):
    rows = own.shape[0]
    own[...] = (part_0[...].astype(F32) + got[:rows].astype(F32)).astype(BF16)
    across[...] = (part_2[...].astype(F32) + got[rows:].astype(F32)).astype(BF16)


def add_rows(traffic, info, first, got, out):
    out[...] = (first[...].astype(F32) + got[...].astype(F32)).astype(BF16)


def add_input(traffic, info, partial, near, far, out):
    traffic.need(partial)
    out[...] = partial[...] + near[...].astype(F32) + far[...].astype(F32)


def pack_last(traffic, info, out_own, inner_own, out_across, inner_across, small, own, sent):
    rows, rest = out_own.shape[0], inner_across.shape[0]
    own[:rows] = out_own[...]
    own[rows:] = inner_own[inner_own.shape[0] - rest :]
    sent[:rows] = out_across[...]
    sent[rows : rows + rest] = inner_across[...]
    sent[rows + rest :] = packed(small[...])


def split_own(traffic, info, own, keep, send):
    half = keep.shape[0]
    for out, side in ((keep, info[ODD]), (send, 1 - info[ODD])):
        out[...] = own[pl.ds(pl.multiple_of(side * half, half), half)]


def add_below(small, got, small_out, send=None):
    total = small[...] + unpacked(got[got.shape[0] - BIAS_ROWS :])
    small_out[...] = total
    if send is not None:
        send[send.shape[0] - BIAS_ROWS :] = packed(total)


def split_rows(start):
    def split(traffic, info, own, got, *refs):
        *small, keep, send = refs
        if small:
            small, (keep, send, small_out) = small[0], refs[1:]
            add_below(small, got, small_out, send)
        half = keep.shape[0]
        for out, side in ((keep, info[ODD]), (send, 1 - info[ODD])):
            at = pl.ds(pl.multiple_of(start + side * half, half), half)
            total = got[pl.ds(pl.multiple_of(side * half, half), half)].astype(F32)
            out[:half] = (total + own[at].astype(F32)).astype(BF16)

    return split


def add_split(traffic, info, keep, got, *refs):
    if len(refs) == 2:
        mine, send = refs
    else:
        small, mine, send, small_out = refs
        add_below(small, got, small_out, send)
    rows = mine.shape[0]
    for out, side in ((mine, info[UPPER]), (send, 1 - info[UPPER])):
        at = pl.ds(pl.multiple_of(side * rows, rows), rows)
        out[:rows] = (keep[at].astype(F32) + got[at].astype(F32)).astype(BF16)


def add_two(traffic, info, first, second, *refs):
    out, *rest = refs
    if rest:
        small, out, *send, small_out = refs
        add_below(small, second, small_out, *send)
    else:
        send = ()
    rows = first.shape[0]
    total = (first[...].astype(F32) + second[:rows].astype(F32)).astype(BF16)
    for target in (out, *send):
        target[:rows] = total


def join(traffic, info, mine, got, whole):
    rows = mine.shape[0]
    for part, side in ((mine, info[UPPER]), (got, 1 - info[UPPER])):
        whole[pl.ds(pl.multiple_of(side * rows, rows), rows)] = part[...]


def place_rows(begins, segments):
    def place(traffic, info, *refs):
        halves, outs = refs[: 2 * len(begins)], refs[2 * len(begins) :]
        for flag in (0, 1):
            @pl.when(info[ODD] == flag)
            def _():
                for c, begin in enumerate(begins):
                    rows = halves[2 * c].shape[0]
                    for half, side in ((halves[2 * c], flag), (halves[2 * c + 1], 1 - flag)):
                        start = begin + side * rows
                        for first, count, out, row in segments:
                            low, high = max(start, first), min(start + rows, first + count)
                            if low < high:
                                outs[out][row + low - first : row + high - first] = half[
                                    low - start : high - start].astype(F32)

    return place


def collect_small(traffic, info, h0, h1, h2, h3, attention, first_sums, second_sums, own, across, near):
    common = jnp.concatenate([first_sums[0:3], second_sums[0:3]])
    zeros = jnp.zeros_like(common)
    none = jnp.zeros_like(h0)
    own[...] = jnp.concatenate([h0[...], attention[0:1], common])
    across[...] = jnp.concatenate([h2[...], none, zeros])
    near[...] = jnp.concatenate([h1[...], none, h3[...], none, common, zeros])


def add_small(traffic, info, own, across, got, own_out, across_out):
    total = own[...] + jnp.concatenate([got[0:2], got[4:10]])
    own_out[...] = total
    across_out[...] = jnp.concatenate([across[0:2] + got[2:4], total[2:]])


def spread_small(traffic, info, small, inner, query, value, *common):
    inner[...] = small[0:1].reshape(inner.shape)
    width = query.shape[0]
    start = value_start(width)
    query[...] = small[1:2, :width].reshape(query.shape)
    value[...] = small[1:2, start : start + width].reshape(value.shape)
    for i, out in enumerate(common):
        out[...] = small[2 + i : 3 + i].reshape(out.shape)


OUTER, ATTENTION, INNER, LAST, INPUT = range(5)
INNER_ROWS = 512
STEPS = (
    INNER, OUTER, ATTENTION, INNER, ATTENTION, LAST, OUTER, INNER, INPUT, LAST, OUTER, ATTENTION, LAST, INNER, ATTENTION)
LAST_STEPS = (INNER, LAST, LAST)


def hold(run, *arrays):
    def mark(*refs):
        refs[-1][...] = jnp.zeros_like(refs[-1])

    ties = run.ties()
    anywhere = pl.BlockSpec(memory_space=pl.ANY)
    *results, token = pl.pallas_call(
        mark,
        name=mark.__name__,
        out_shape=[jax.ShapeDtypeStruct(a.shape, a.dtype) for a in arrays] + [pltpu.VMEM((8, 128), F32)],
        in_specs=[anywhere] * (len(arrays) + len(ties)),
        out_specs=[anywhere] * len(arrays) + [pl.BlockSpec(memory_space=pltpu.VMEM)],
        input_output_aliases={i: i for i in range(len(arrays))},
    )(*arrays, *ties)
    run.last = (token, pltpu.VMEM)
    return results


def chain(run, split):
    keep, send, *small = split()
    (rows, columns), below = keep.shape, send.shape[0] - keep.shape[0]
    shape, sent = (rows // 2, columns), (rows // 2 + below, columns)
    small_out = [(s.shape, F32) for s in small]
    got = exchange(send, 1, 0)
    yield
    mine, send, *small = run(add_split, [(shape, BF16), (sent, BF16)] + small_out, keep, got, *small, scalars=[UPPER])
    got = exchange(send, 2, 0)
    yield
    for mask in later_masks():
        outs = [(shape, BF16)] + [(sent, BF16)] * len(small) + small_out
        mine, *rest = run(add_two, outs, mine, got, *small)
        send, small = (rest[0], rest[1:]) if rest else (mine, ())
        got = exchange(send, mask, 0)
        yield
    mine, *small = run(add_two, [(shape, BF16)] + small_out, mine, got, *small)
    got = exchange(mine, 2, 0)
    yield
    (whole,) = run(join, [((rows, columns), BF16)], mine, got, scalars=[UPPER])
    got = exchange(whole, 1, 0)
    yield
    return (whole, got), small


def on_device(
    layer_input,
    lengths,
    query_weight,
    query_bias,
    key_weight,
    value_weight,
    value_bias,
    out_weight,
    out_bias,
    first_gain,
    first_shift,
    inner_weight,
    inner_bias,
    outer_weight,
    outer_bias,
    second_gain,
    second_shift,
    cotangent,
):
    rows = layer_input.shape[0] // lax.axis_size("tp")
    model = layer_input.shape[1]
    width = query_weight.shape[1]
    hidden = inner_weight.shape[1]
    tp, dp = lax.axis_index("tp"), lax.axis_index("dp")
    upper = (dp >> 1) ^ (dp >> 2)
    run = Sequence([s.reshape(1) for s in (tp, dp & 3, dp & 1, upper & 1)] + [lengths])
    to_core = lambda a: exchange(a, 0, 1)
    to_x = lambda a: exchange(a, 0, 2)
    to_y = lambda a: exchange(a, 1, 0)
    to_z = lambda a: exchange(a, 2, 0)

    full, low = ((rows, model), F32), ((rows, model), BF16)
    square, wide = ((hidden, model), BF16), ((rows, hidden), BF16)
    sums, small = ((8, model), F32), ((SMALL_ROWS, model), F32)
    sequences = lambda *masks: Afar(tuple((layer_input, m, rows) for m in masks), OWN)
    inputs, own_grad = sequences(0), Afar(((cotangent, 0, rows),), OWN)

    near_inner, near_outer = to_core(inner_weight), to_core(outer_weight)
    head, slot = width + BIAS_ROWS, 2 * width // 3
    (sent,) = run(pick_out, [Out((head, model), BF16)], afar(out_weight), afar(inner_bias), scratch=[small])
    far_out, near_out = to_x(sent), to_core(sent)
    half_square = Out((hidden // 2, model), BF16)
    feed_weights = afar(inner_weight, outer_weight, way=RAW)
    feed_came = to_x(run(pick_feed, [half_square], feed_weights, scalars=[PLACE])[0])
    near_inner, near_outer = hold(run, near_inner, near_outer)

    own_weights = [afar(w) for w in (query_weight.T, key_weight.T, value_weight.T)]
    attention_scalars = [TP, LENGTHS]
    seen = [Out((6 * rows, width), BF16), ((8, rows), F32)]
    heads = lambda masks, outs: run(
        heads_forward(masks), outs + seen, sequences(*masks), *own_weights, afar(query_bias), afar(value_bias),
        scalars=attention_scalars)
    sent, far_qkv, far_log = heads((2, 3), [((2 * slot, model), BF16)])
    came = to_x(sent)
    sent, own_context, near_qkv, near_log = heads((1, 0), [((slot, model), BF16), ((width, rows), BF16)])
    near = to_core(sent)
    far_out, near_out = hold(run, far_out, near_out)
    far_near_out = to_core(far_out)
    (feed_came,) = hold(run, feed_came)
    feed_y, feed_z = to_y(feed_came), to_z(feed_came)
    feed_last_came = to_x(run(pick_last_feed, [half_square], feed_weights, scalars=[PLACE])[0])
    came, near = hold(run, came, near)
    contexts = [afar(a) for a in (near, came, to_core(came))]
    others = (near_out, far_out, far_near_out)
    out_weights = Afar(tuple((a, 0, width) for a in (out_weight,) + others))
    tails = [Afar(((a, width, BIAS_ROWS),)) for a in others]
    first_sum, normed, normed_low, bias_1, bias_2, bias_3 = run(
        project, [Out(*full), full, low] + [small] * 3, inputs, own_context, *contexts, out_weights, *tails, out_bias,
        first_gain, first_shift, scalars=[TP])

    active_0, active_1, slope_0, slope_1, partial = run(
        feed_near, [Out(*wide), wide, Out(*wide), Out(*wide), full], normed_low, normed, outer_bias, afar(inner_weight),
        afar(near_inner), afar(outer_weight), afar(near_outer), inner_bias, bias_1)
    far_feed = hold(run, feed_came, feed_y, feed_z, feed_last_came)
    near_feed = tuple(to_core(a) for a in far_feed)
    quarter = hidden // 4
    inner_2, inner_3 = (Afar(tuple((a, 0, quarter) for a in f), PLACED) for f in (far_feed, near_feed))
    outer_2, outer_3 = (Afar(tuple((a, quarter, quarter) for a in f), PLACED) for f in (far_feed, near_feed))
    (active_2, slope_2), (active_3, slope_3) = (
        run(feed_far, [wide] * 2, normed_low, inner, bias, scalars=[PLACE])
        for inner, bias in ((inner_2, bias_2), (inner_3, bias_3))
    )
    layer_output, second_grad, result_grad, second_sums = run(
        feed_out, [Out(*low), Out(*full), low, sums], active_2, active_3, outer_2, outer_3, partial,
        second_gain, second_shift, own_grad, scalars=[TP, PLACE], scratch=[full])

    near_part = lambda left, right, n: [
        to_core(a) for a in run(near_grad, [((hidden // n, model), BF16)] * n, left, right)]
    far_part = lambda left, right, got, *sizes: run(
        far_grad(len(got)), [((size, model), BF16) for size in sizes], left, right, *got)
    outer_got_3 = near_part(active_3, result_grad, 1)
    outer_got_1 = near_part(active_1, result_grad, 1)
    hidden_out = [wide, wide] + [((1, hidden), F32)] * 2
    hidden_3, hidden_1, sum_3, sum_1 = run(
        hidden_pair, hidden_out, result_grad, outer_3, afar(near_outer), slope_3, afar(slope_1), scalars=[PLACE])
    outer_x = to_x(far_part(active_2, result_grad, outer_got_3, hidden)[0])
    (outer_own,) = far_part(afar(active_0), result_grad, outer_got_1, hidden)
    inner_got_3, inner_got_1 = near_part(normed_low, hidden_3, 2), near_part(normed_low, hidden_1, 2)
    hidden_2, hidden_0, sum_2, sum_0, first_grad, branch_grad, first_sums = run(
        feed_back, hidden_out + [full, low, sums], result_grad, outer_2, afar(outer_weight), slope_2, afar(slope_0),
        afar(second_grad), hidden_3, hidden_1, inner_3, afar(near_inner), inner_2, afar(inner_weight), afar(first_sum),
        first_gain, scalars=[PLACE], scratch=[full])

    part = ((width, model), BF16)
    cut = INNER_ROWS * hidden // 768
    sent, last_inner = far_part(normed_low, hidden_2, inner_got_3, cut, hidden - cut)
    inner_x = to_x(sent)
    (inner_own,) = far_part(normed_low, hidden_0, inner_got_1, hidden)
    lent = ((slot, model), BF16)
    own_slot, *sent, near_parts, part_0, part_2 = run(
        context_back, [((width, rows), BF16), lent, lent, lent, ((2 * width, model), BF16), part, part],
        branch_grad, out_weights, own_context, *contexts)
    near, far, far_near = to_core(sent[0]), to_x(sent[1]), exchange(sent[2], 0, 3)
    near_parts = to_core(near_parts)
    rooms = [((6, rows, width), BF16), ((2 * width // HD, rows, rows), F32)]
    weight_rows = (3 * width, model)
    same = lambda block: block
    first_kernel = heads_backward((1, 0), (unfolded_one, same))
    near_input, partial, small_sums, weight_sums = run(
        first_kernel, [low, Out(*full), sums, (weight_rows, F32)], afar(near_qkv), afar(near), own_slot,
        sequences(1, 0), *own_weights, near_log, first_grad, scalars=attention_scalars, scratch=rooms)
    near_input = to_core(near_input)

    def way_of(own, start, rows, got, *small):
        below = BIAS_ROWS * len(small)
        outs = [((rows // 2, model), BF16), ((rows // 2 + below, model), BF16)] + [(s.shape, F32) for s in small]
        return chain(run, lambda: run(split_rows(start), outs, own, got, *small, scalars=[ODD]))

    outer_way = way_of(outer_own, 0, hidden, outer_x)
    far, far_near = hold(run, far, far_near)
    next(outer_way)
    out_own, out_across = run(add_out, [part, part], part_0, part_2, near_parts)
    second_kernel = heads_backward((2, 3), (unfolded_one, unfolded_one))
    far_input, sent, small_sums, attention_own = run(
        second_kernel, [low, low, sums, (weight_rows, BF16)], afar(far_qkv), afar(far), afar(far_near),
        sequences(2, 3), *own_weights, far_log, weight_sums, small_sums, scalars=attention_scalars, scratch=rooms)
    far_near_input = to_core(sent)
    half = ((3 * width // 2, model), BF16)
    attention_way = chain(run, lambda: run(split_own, [half, half], attention_own, scalars=[ODD]))
    next(attention_way)
    small_own, small_across, small_near = run(
        collect_small, [small, small, ((2 * SMALL_ROWS, model), F32)], sum_0, sum_1, sum_2, sum_3,
        small_sums, first_sums, second_sums)
    small_near = to_core(small_near)
    next(outer_way)
    small_own, small_across = run(add_small, [small, small], small_own, small_across, small_near)
    last_rows = width + hidden - cut
    last_own, sent = run(
        pack_last, [((last_rows, model), BF16), ((last_rows + BIAS_ROWS, model), BF16)], out_own, inner_own,
        out_across, last_inner, small_across)
    last_x = to_x(sent)

    def input_steps():
        (sent,) = run(add_rows, [low], far_input, far_near_input)
        got = to_x(sent)
        yield
        return run(add_input, [Out(*full)], afar(partial), near_input, got)[0]

    ways = {
        OUTER: outer_way, ATTENTION: attention_way, INNER: way_of(inner_own, 0, cut, inner_x),
        LAST: way_of(last_own, 0, last_rows, last_x, small_own), INPUT: input_steps(),
    }
    for number in STEPS:
        next(ways[number])

    def finish(way):
        while True:
            try:
                next(way)
            except StopIteration as stop:
                return stop.value

    finished = {}

    def results(number):
        if number not in finished:
            finished[number] = finish(ways[number])
        return finished[number]

    def place(numbers, begins, segments, *sizes):
        halves = [half for number in numbers for half in results(number)[0]]
        return run(place_rows(begins, segments), [Out((size, model), F32) for size in sizes], *halves, scalars=[ODD])

    (outer_weight_grad,) = place((OUTER,), (0,), ((0, hidden, 0, 0),), hidden)
    for number in LAST_STEPS:
        next(ways[number])
    input_grad = finish(ways[INPUT])
    query_grad, key_grad, value_grad = place(
        (ATTENTION,), (0,), [(i * width, width, i, 0) for i in range(3)], width, width, width)
    _, (last_small,) = results(LAST)
    inner_bias_grad, query_bias_grad, value_bias_grad, *common = run(
        spread_small, [Out((size,), F32) for size in (hidden, width, width) + (model,) * 6], last_small)
    inner_weight_grad, out_grad = place(
        (INNER, LAST), (0, cut),
        ((0, cut, 0, 0), (cut, width, 1, 0), (cut + width, hidden - cut, 0, cut)), hidden, width)
    return (
        layer_output,
        input_grad,
        query_grad.T,
        query_bias_grad,
        key_grad.T,
        value_grad.T,
        value_bias_grad,
        out_grad,
        *common[:3],
        inner_weight_grad,
        inner_bias_grad,
        outer_weight_grad,
        *common[3:],
    )


def solution(mesh):
    in_specs = (
        P("dp", None),
        P("dp"),
        P(None, "tp"),
        P("tp"),
        P(None, "tp"),
        P(None, "tp"),
        P("tp"),
        P("tp", None),
        P(),
        P(),
        P(),
        P(None, "tp"),
        P("tp"),
        P("tp", None),
        P(),
        P(),
        P(),
        P("dp", None),
    )
    out_specs = (
        P(("dp", "tp"), None),
        P(("dp", "tp"), None),
        P(None, "tp"),
        P("tp"),
        P(None, "tp"),
        P(None, "tp"),
        P("tp"),
        P("tp", None),
        P(),
        P(),
        P(),
        P(None, "tp"),
        P("tp"),
        P("tp", None),
        P(),
        P(),
        P(),
    )
    return jax.shard_map(
        on_device, mesh=mesh, in_specs=in_specs, out_specs=out_specs, check_vma=False
    )
```

```python
import dataclasses

import jax
import jax.numpy as jnp
from jax import lax
from jax.experimental import pallas as pl
from jax.experimental.pallas import tpu as pltpu
from jax.sharding import PartitionSpec as P

HD = 64
EPSILON = 1e-05
BF16 = jnp.bfloat16
F32 = jnp.float32
LARGE = 24 * 2**20
STEP_ROWS = 128
KEY_STEP = 160
BIAS_ROWS = 16
SMALL_ROWS = 8

TP, PLACE, ODD, UPPER, LENGTHS = range(5)

ORDERED, PLACED, OWN, RAW = range(4)


def dot(left, right, left_dim=1, right_dim=0):
    return lax.dot_general(
        left, right, (((left_dim,), (right_dim,)), ((), ())), preferred_element_type=F32
    )


@dataclasses.dataclass(frozen=True)
class Afar:
    parts: tuple
    way: int = ORDERED

    def shape(self):
        return (sum(rows for _, _, rows in self.parts),) + self.parts[0][0].shape[1:]


def afar(*arrays, way=ORDERED):
    return Afar(tuple((a, 0, a.shape[0]) for a in arrays), way)


@dataclasses.dataclass(frozen=True)
class Out:
    shape: tuple
    dtype: jnp.dtype


class Traffic:
    def __init__(self, sems):
        self.sems, self.count = sems, 0
        self.coming, self.going, self.sent = {}, {}, []

    def copy(self, source, target):
        copy = pltpu.make_async_copy(source, target, self.sems.at[self.count])
        copy.start()
        self.count += 1
        return copy

    def need(self, *refs):
        for ref in refs:
            for copy in self.coming.pop(id(ref), ()):
                copy.wait()

    def send(self, *refs):
        for ref in refs:
            if id(ref) in self.going:
                self.sent.append(self.copy(ref, self.going.pop(id(ref))))

    def end(self):
        for copies in self.coming.values():
            for copy in copies:
                copy.wait()
        for ref in self.results:
            if id(ref) in self.going:
                self.send(ref)
        for copy in self.sent:
            copy.wait()


class Sequence:
    def __init__(self, scalars):
        self.last, self.scalars = None, scalars

    def ties(self):
        return [] if self.last is None else [pltpu.with_memory_space_constraint(*self.last)]

    def note(self, results, outs):
        smallest = min(range(len(outs)), key=lambda i: results[i].size)
        space = pltpu.HBM if isinstance(outs[smallest], Out) else pltpu.VMEM
        self.last = (results[smallest], space)

    def __call__(self, body, outs, *args, scalars=(), scratch=(), limit=LARGE):
        operands, sizes, fetched, copies = [self.scalars[i] for i in scalars], [], [], 0
        spaces = [pltpu.SMEM] * len(scalars)
        for arg in args:
            if isinstance(arg, Afar):
                operands += [pltpu.with_memory_space_constraint(a, pltpu.HBM) for a, _, _ in arg.parts]
                spaces += [pltpu.HBM] * len(arg.parts)
                sizes.append(len(arg.parts))
                copies += len(arg.parts)
                if arg.way != RAW:
                    fetched.append(pltpu.VMEM(arg.shape(), arg.parts[0][0].dtype))
            else:
                operands.append(arg)
                spaces.append(pltpu.VMEM)
                sizes.append(1)
        ties = self.ties()
        staged = [pltpu.VMEM(out.shape, out.dtype) for out in outs if isinstance(out, Out)]
        copies += len(staged)
        shapes = [
            pltpu.HBM(out.shape, out.dtype) if isinstance(out, Out) else pltpu.VMEM(*out) for out in outs
        ]

        def kernel(*refs):
            refs = list(refs)
            take = lambda n: [refs.pop(0) for _ in range(n)]
            info = {n: ref if n == LENGTHS else ref[0] for n, ref in zip(scalars, take(len(scalars)))}
            given = [take(n) for n in sizes]
            take(len(ties))
            results, buffers, stages, rest = take(len(outs)), take(len(fetched)), take(len(staged)), take(len(scratch))
            traffic = Traffic(refs[0] if refs else None)
            inputs = []
            for arg, sources in zip(args, given):
                if not isinstance(arg, Afar):
                    inputs += sources
                    continue
                if arg.way == RAW:
                    inputs.append(sources)
                    continue
                buffer = buffers.pop(0)
                inputs.append(buffer)
                copies, start = [], 0
                for i, (source, (_, first, rows)) in enumerate(zip(sources, arg.parts)):
                    if arg.way == OWN:
                        first = pl.multiple_of((info[TP] ^ first) * rows, rows)
                    if arg.way == PLACED:
                        start = pl.multiple_of((info[PLACE] ^ i) * rows, rows)
                    copies.append(traffic.copy(source.at[pl.ds(first, rows)], buffer.at[pl.ds(start, rows)]))
                    start += rows
                traffic.coming[id(buffer)] = copies
            for i, out in enumerate(outs):
                if isinstance(out, Out):
                    stage = stages.pop(0)
                    traffic.going[id(stage)] = results[i]
                    results[i] = stage
            traffic.results = results
            body(traffic, info, *inputs, *results, *rest)
            traffic.end()

        results = pl.pallas_call(
            kernel,
            name=body.__name__,
            out_shape=shapes,
            in_specs=[pl.BlockSpec(memory_space=space) for space in spaces]
            + [pl.BlockSpec(memory_space=pl.ANY)] * len(ties),
            out_specs=[pl.BlockSpec(memory_space=pltpu.HBM if isinstance(o, Out) else pltpu.VMEM) for o in outs],
            scratch_shapes=fetched + staged + [pltpu.VMEM(shape, dtype) for shape, dtype in scratch]
            + ([pltpu.SemaphoreType.DMA((copies,))] if copies else []),
            compiler_params=pltpu.CompilerParams(vmem_limit_bytes=limit),
        )(*operands, *ties)
        self.note(results, outs)
        return results


def exchange(array, dp_bits, tp_bits):
    dp_size, tp_size = lax.axis_size("dp"), lax.axis_size("tp")
    pairs = [
        (d * tp_size + t, (d ^ dp_bits) * tp_size + (t ^ tp_bits))
        for d in range(dp_size)
        for t in range(tp_size)
    ]
    return lax.ppermute(array, ("dp", "tp"), pairs)


def along(array, moves):
    dp_size, tp_size = lax.axis_size("dp"), lax.axis_size("tp")
    pairs = [
        (d * tp_size + t, ((d & ~6) | (moves[(d >> 1) & 3] << 1)) * tp_size + t)
        for d in range(dp_size)
        for t in range(tp_size)
        if (d >> 1) & 3 in moves
    ]
    return lax.ppermute(array, ("dp", "tp"), pairs)


def later_masks():
    masks, bit = [], 8
    while bit < lax.axis_size("dp"):
        masks.append(bit)
        bit *= 2
    return masks


def folded(rows):
    return jnp.sum(rows.reshape(rows.shape[0] // 8, 8, rows.shape[1]), axis=0)


def normalize(values):
    average = jnp.mean(values, axis=-1, keepdims=True)
    centered = values - average
    spread = jnp.mean(centered * centered, axis=-1, keepdims=True)
    scale = lax.rsqrt(spread + EPSILON)
    return centered * scale, scale


def norm_backward(e, rows, scale):
    first = jnp.mean(e, axis=-1, keepdims=True)
    second = jnp.mean(e * rows, axis=-1, keepdims=True)
    return scale * (e - first - rows * second)


def row_steps(rows):
    return [slice(i, i + STEP_ROWS) for i in range(0, rows, STEP_ROWS)]


def as_row(ref):
    return ref[...].reshape(1, ref.shape[0])


def packed(values):
    high = values.astype(BF16).astype(F32)
    return jnp.concatenate([high, values - high]).astype(BF16)


def unpacked(pairs):
    rows = pairs[...].astype(F32)
    return rows[: BIAS_ROWS // 2] + rows[BIAS_ROWS // 2 :]


def folded_one(part):
    rows, columns = part.shape
    third = rows // 3
    last = part[2 * third :]
    side = jnp.concatenate([last[:, : columns // 2], last[:, columns // 2 :]])
    return jnp.concatenate([part[: 2 * third], side], axis=1)


def unfolded_one(block):
    rows = block.shape[0] // 2
    columns = block.shape[1] * 2 // 3
    last = jnp.concatenate([block[:rows, columns:], block[rows:, columns:]], axis=1)
    return jnp.concatenate([block[:, :columns], last])


def folded_two(first, second):
    half, third = second.shape[1] // 2, second.shape[0] // 3
    below = [second[i * third : (i + 1) * third, half:] for i in range(3)]
    return jnp.concatenate(
        [jnp.concatenate([first, second[:, :half]], axis=1), jnp.concatenate(below, axis=1)])


def unfolded_first(block):
    rows, columns = block.shape[0] * 3 // 4, block.shape[1] * 2 // 3
    return block[:rows, :columns]


def unfolded_second(block):
    rows, columns = block.shape[0] * 3 // 4, block.shape[1] * 2 // 3
    below = block[rows:]
    right = jnp.concatenate([below[:, i * columns // 2 : (i + 1) * columns // 2] for i in range(3)])
    return jnp.concatenate([block[:rows, columns:], right], axis=1)


def pick_out(traffic, info, out_weight, inner_bias, sent, values):
    traffic.need(out_weight, inner_bias)
    rows = out_weight.shape[0]
    values[...] = jnp.zeros_like(values)
    values[0:1] = as_row(inner_bias)
    sent[:rows] = out_weight[...]
    sent[rows:] = packed(values[...])


def pick_feed(traffic, info, blocks, target):
    rows = target.shape[0] // 2
    copies = []
    for i, block in enumerate(blocks):
        at = pl.ds(pl.multiple_of(info[PLACE] * rows, rows), rows)
        copies.append(traffic.copy(block.at[at], target.at[pl.ds(i * rows, rows)]))
    for copy in copies:
        copy.wait()


def pick_last_feed(traffic, info, blocks, target):
    pick_feed(traffic, {PLACE: info[PLACE] ^ 3}, blocks, target)


def lone_head(transposed, head):
    part = transposed[head * HD : (head + 1) * HD]
    if head // 2 * 2 + 1 >= transposed.shape[0] // HD:
        return part
    zeros = jnp.zeros_like(part)
    return jnp.concatenate([part, zeros] if head % 2 == 0 else [zeros, part])


def tile(array, head):
    start = head // 2 * 2 * HD
    return array[:, start : start + 2 * HD]


def hidden_keys(rows, length):
    return jnp.where(lax.broadcasted_iota(jnp.int32, (rows, 1), 0) < length, 0.0, -1e30)


def visible_scores(keys, queries_t, head, hidden):
    return dot(tile(keys, head), lone_head(queries_t, head)) + hidden


def heads_forward(masks):
    def forward(traffic, info, inputs, query_weight, key_weight, value_weight, query_bias, value_bias, sent, *refs):
        *own, qkv, log_total = refs
        width = query_weight.shape[0]
        rows = inputs.shape[0] // 2
        heads = width // HD
        contexts = []
        traffic.need(query_weight, key_weight, value_weight, query_bias, value_bias, inputs)
        for i, mask in enumerate(masks):
            x = inputs[i * rows : (i + 1) * rows]
            queries = (dot(x, query_weight[...], 1, 1) + as_row(query_bias)).astype(BF16)
            keys = dot(x, key_weight[...], 1, 1).astype(BF16)
            vals = (dot(x, value_weight[...], 1, 1) + as_row(value_bias)).astype(BF16)
            for j, part in enumerate((queries, keys, vals)):
                qkv[(3 * i + j) * rows : (3 * i + j + 1) * rows] = part
            queries_t = (queries * HD**-0.5).astype(BF16).T
            values_t = vals.T
            hidden = hidden_keys(rows, info[LENGTHS][info[TP] ^ mask])
            context = []
            for h in range(heads):
                scores = visible_scores(keys, queries_t, h, hidden)
                top = jnp.max(scores, axis=0, keepdims=True)
                raised = jnp.exp(scores - top)
                total = jnp.sum(raised, axis=0, keepdims=True)
                log_total[i * heads + h : i * heads + h + 1] = top + jnp.log(total)
                sums = dot(values_t[h * HD : (h + 1) * HD], raised.astype(BF16))
                context.append((sums / total).astype(BF16))
            contexts.append(jnp.concatenate(context))
        if own:
            own[0][...] = contexts[1]
            sent[...] = folded_one(contexts[0])
        else:
            sent[...] = folded_two(*contexts)

    return forward


def all_contexts(own, near, far, far_near):
    return jnp.concatenate([own[...], unfolded_one(near[...]), unfolded_first(far[...]), unfolded_second(far_near[...])])


def project(traffic, info, inputs, own_context, near, far, far_near, weights, tail_1, tail_2, tail_3, out_bias,
            gain, shift, first_sum, normed, normed_low, bias_1, bias_2, bias_3):
    traffic.need(near, far, far_near, weights)
    branch = dot(all_contexts(own_context, near, far, far_near), weights[...], 0, 0)
    traffic.need(inputs)
    first_sum[...] = inputs[...].astype(F32) + as_row(out_bias) + branch
    traffic.send(first_sum)
    for at in row_steps(first_sum.shape[0]):
        out = normalize(first_sum[at])[0] * as_row(gain) + as_row(shift)
        normed[at] = out
        normed_low[at] = out.astype(BF16)
    traffic.need(tail_1, tail_2, tail_3)
    for tail, bias in ((tail_1, bias_1), (tail_2, bias_2), (tail_3, bias_3)):
        bias[...] = unpacked(tail)


def context_back(traffic, info, branch_grad, weights, own_grad, *sent):
    traffic.need(weights)
    grads = dot(weights[...], branch_grad[...], 1, 1).astype(BF16)
    width = own_grad.shape[0]
    own_grad[...] = grads[:width]
    for i, part in enumerate(sent):
        part[...] = folded_one(grads[(1 + i) * width : (2 + i) * width])
        traffic.send(part)


def out_back(traffic, info, branch_grad, own_context, near, far, far_near, near_parts, part_0, part_2):
    traffic.need(near, far, far_near)
    parts = dot(all_contexts(own_context, near, far, far_near), branch_grad[...]).astype(BF16)
    width = part_0.shape[0]
    slot = lambda s: parts[s * width : (s + 1) * width]
    part_0[...], part_2[...] = slot(0), slot(2)
    near_parts[:width], near_parts[width:] = slot(1), slot(3)


def heads_backward(masks, unfold):
    def backward(traffic, info, qkv, context_a, context_b, inputs, query_weight, key_weight, value_weight, log_total, *refs):
        wide = refs[-1]
        first = len(refs) == 6
        before, (grad_a, grad_b, sums_out, *weight_sums) = (refs[:1], refs[1:-1]) if first else (refs[:2], refs[2:-1])
        rows = inputs.shape[0] // 2
        width = query_weight.shape[0]
        heads = width // HD
        lane = lambda count: lax.broadcasted_iota(jnp.int32, (count, 2 * HD), 1)
        traffic.need(qkv, log_total, context_a, context_b)

        def sequence(i, context, length, count):
            queries, keys, vals = (qkv[(3 * i + j) * rows : (3 * i + j) * rows + n] for j, n in enumerate((rows, count, count)))
            grads_t = unfold[i](context[...])
            grads = grads_t.T
            queries_t = (queries * HD**-0.5).astype(BF16).T
            keys_t = keys.T
            hidden = hidden_keys(count, length)
            query_parts, pairs = [], []
            for h in range(heads):
                n = i * heads + h
                probs = jnp.exp(visible_scores(keys, queries_t, h, hidden) - log_total[n : n + 1])
                prob_grad = dot(tile(vals, h), lone_head(grads_t, h))
                inner = jnp.sum(probs * prob_grad, axis=0, keepdims=True)
                score_grad = (probs * (prob_grad - inner)).astype(BF16)
                value_grad = dot(probs.astype(BF16), tile(grads, h))
                key_grad = dot(score_grad, tile(queries, h)) * HD**-0.5
                query_parts.append(dot(keys_t[h * HD : (h + 1) * HD], score_grad) * HD**-0.5)
                pairs.append((key_grad, value_grad))
            wide[3 * i] = jnp.concatenate(query_parts).astype(BF16).T
            for j in (0, 1):
                at = 3 * i + 1 + j
                for h in range(0, heads, 2):
                    if h + 1 < heads:
                        wide[at, :count, h * HD : (h + 2) * HD] = jnp.where(
                            lane(count) < HD, pairs[h][j], pairs[h + 1][j]).astype(BF16)
                    else:
                        wide[at, :count, h * HD :] = pairs[h][j].astype(BF16)
                if count < rows:
                    wide[at, count:] = jnp.zeros((rows - count, width), BF16)

        counts = [KEY_STEP, 2 * KEY_STEP, rows]
        for i, (mask, context) in enumerate(zip(masks, (context_a, context_b))):
            length = info[LENGTHS][info[TP] ^ mask]
            for low, count in zip([0] + counts, counts):
                @pl.when((length > low) & (length <= count))
                def _():
                    sequence(i, context, length, count)

        traffic.need(query_weight, key_weight, value_weight)
        for i, out in enumerate((grad_a, grad_b)):
            total = dot(wide[3 * i], query_weight[...]) + dot(wide[3 * i + 1], key_weight[...])
            total = total + dot(wide[3 * i + 2], value_weight[...])
            if out.dtype == F32:
                traffic.need(before[0])
                out[...] = before[0][...] + total
                traffic.send(out)
            else:
                out[...] = total.astype(BF16)
        model = sums_out.shape[1]

        def summed(j):
            row = sum(jnp.sum(wide[3 * i + j].astype(F32), axis=0, keepdims=True) for i in (0, 1))
            return jnp.concatenate([row, jnp.zeros((1, model - width), F32)], axis=1)

        eight = lambda row: jnp.broadcast_to(row, sums_out.shape)
        sums = eight(summed(0)) + pltpu.roll(eight(summed(2)), value_start(width), 1)
        traffic.need(inputs)
        x = inputs[...]
        for j in range(3):
            grad_t = jnp.concatenate([wide[j].T, wide[3 + j].T], axis=1)
            block = dot(grad_t, x)
            if not first:
                traffic.need(*before)
            at = slice(j * width, (j + 1) * width)
            if first:
                weight_sums[0][at] = block
            else:
                weight_sums[0][at] = (before[0][at] + block).astype(BF16)
        sums_out[...] = sums if first else before[1][...] + sums

    return backward


def value_start(width):
    return -(-width // 128) * 128


def feed_slot(normed_low, inner, biases, active, slope):
    bias = biases[...].reshape(1, biases.shape[0]) if len(biases.shape) == 1 else biases[0:1]
    columns = 256
    for c in range(0, inner.shape[1], columns):
        at = slice(c, c + columns)
        hidden = dot(normed_low[...], inner[:, at]) + bias[:, at]
        half_erf = 0.5 * (1.0 + lax.erf(hidden * 0.5**0.5))
        active[:, at] = (hidden * half_erf).astype(BF16)
        slope[:, at] = (
            half_erf + hidden * jnp.exp(-0.5 * hidden * hidden) * 0.3989422804014327
        ).astype(BF16)


def feed_near(traffic, info, normed_low, normed, outer_bias, inner_a, inner_b, outer_a, outer_b, bias_a, bias_b,
              active_a, active_b, slope_a, slope_b, after):
    traffic.need(inner_a)
    feed_slot(normed_low, inner_a, bias_a, active_a, slope_a)
    traffic.send(active_a, slope_a)
    traffic.need(inner_b)
    feed_slot(normed_low, inner_b, bias_b, active_b, slope_b)
    traffic.send(active_b, slope_b)
    traffic.need(outer_a, outer_b)
    after[...] = (
        normed[...] + as_row(outer_bias) + dot(active_a[...], outer_a[...]) + dot(active_b[...], outer_b[...])
    )


def feed_far(traffic, info, normed_low, inner, bias, active, slope):
    traffic.need(inner)
    feed_slot(normed_low, inner, bias, active, slope)


def feed_out(traffic, info, active_a, active_b, outer_a, outer_b, before, gain, shift, cotangent,
             output, second_grad, result_grad, sums, total):
    traffic.need(outer_a, outer_b)
    total[...] = before[...] + dot(active_a[...], outer_a[...]) + dot(active_b[...], outer_b[...])
    traffic.need(cotangent)
    parts = [0.0] * 3
    for at in row_steps(total.shape[0]):
        rows, scale = normalize(total[at])
        output[at] = (rows * as_row(gain) + as_row(shift)).astype(BF16)
        grad = cotangent[at].astype(F32)
        back = norm_backward(grad * as_row(gain), rows, scale)
        second_grad[at] = back
        result_grad[at] = back.astype(BF16)
        parts = [c + folded(v) for c, v in zip(parts, (back, grad * rows, grad))]
    for i, part in enumerate(parts):
        sums[i : i + 1] = jnp.sum(part, axis=0, keepdims=True)


def near_grad(traffic, info, left, right, *chunks):
    traffic.need(left)
    total = dot(left[...], right[...], 0, 0).astype(BF16)
    rows = chunks[0].shape[0]
    for i, chunk in enumerate(chunks):
        chunk[...] = total[i * rows : (i + 1) * rows]


def far_grad(parts):
    def grad(traffic, info, left, right, *refs):
        traffic.need(left)
        total = dot(left[...], right[...], 0, 0)
        total = total + jnp.concatenate([ref[...].astype(F32) for ref in refs[:parts]])
        at = 0
        for chunk in refs[parts:]:
            rows = chunk.shape[0]
            chunk[...] = total[at : at + rows].astype(BF16)
            at += rows

    return grad


def hidden_pair(traffic, info, result_grad, outer_a, outer_b, slope_a, slope_b, grad_a, grad_b, sum_a, sum_b):
    for outer, slope, hidden_grad, bias_sum in (
        (outer_a, slope_a, grad_a, sum_a), (outer_b, slope_b, grad_b, sum_b)
    ):
        traffic.need(outer, slope)
        grad = (dot(result_grad[...], outer[...], 1, 1) * slope[...].astype(F32)).astype(BF16)
        hidden_grad[...] = grad
        bias_sum[...] = jnp.sum(grad.astype(F32), axis=0, keepdims=True)


def feed_back(traffic, info, result_grad, outer_2, outer_0, slope_2, slope_0, before, grad_3, grad_1,
              inner_3, inner_1, inner_2, inner_0, first_sum, gain,
              grad_2, grad_0, sum_2, sum_0, first_grad, branch_grad, sums, total):
    hidden_pair(traffic, info, result_grad, outer_2, outer_0, slope_2, slope_0, grad_2, grad_0, sum_2, sum_0)
    traffic.need(before)
    total[...] = before[...]
    for g, w in ((grad_3, inner_3), (grad_1, inner_1), (grad_2, inner_2), (grad_0, inner_0)):
        traffic.need(w)
        total[...] += dot(g[...], w[...], 1, 1)
    traffic.need(first_sum)
    parts = [0.0] * 3
    for at in row_steps(total.shape[0]):
        rows, scale = normalize(first_sum[at])
        grad = total[at]
        back = norm_backward(grad * as_row(gain), rows, scale)
        first_grad[at] = back
        branch_grad[at] = back.astype(BF16)
        parts = [c + folded(v) for c, v in zip(parts, (back, grad * rows, grad))]
    for i, part in enumerate(parts):
        sums[i : i + 1] = jnp.sum(part, axis=0, keepdims=True)


def add_out(traffic, info, part_0, part_2, got, own, across):
    rows = own.shape[0]
    own[...] = (part_0[...].astype(F32) + got[:rows].astype(F32)).astype(BF16)
    across[...] = (part_2[...].astype(F32) + got[rows:].astype(F32)).astype(BF16)


def add_rows(traffic, info, first, got, out):
    out[...] = (first[...].astype(F32) + got[...].astype(F32)).astype(BF16)


def add_input(traffic, info, partial, near, far, out):
    traffic.need(partial)
    out[...] = partial[...] + near[...].astype(F32) + far[...].astype(F32)


def pack_last(traffic, info, out_own, inner_own, out_across, inner_across, small, own, sent):
    rows, rest = out_own.shape[0], inner_across.shape[0]
    own[:rows] = out_own[...]
    own[rows:] = inner_own[inner_own.shape[0] - rest :]
    sent[:rows] = out_across[...]
    sent[rows : rows + rest] = inner_across[...]
    sent[rows + rest :] = packed(small[...])


def split_own(traffic, info, own, keep, send):
    half = keep.shape[0]
    for out, side in ((keep, info[ODD]), (send, 1 - info[ODD])):
        out[...] = own[pl.ds(pl.multiple_of(side * half, half), half)]


def add_below(small, got, small_out, send=None):
    total = small[...] + unpacked(got[got.shape[0] - BIAS_ROWS :])
    small_out[...] = total
    if send is not None:
        send[send.shape[0] - BIAS_ROWS :] = packed(total)


def split_rows(start):
    def split(traffic, info, own, got, *refs):
        *small, keep, send = refs
        if small:
            small, (keep, send, small_out) = small[0], refs[1:]
            add_below(small, got, small_out, send)
        half = keep.shape[0]
        for out, side in ((keep, info[ODD]), (send, 1 - info[ODD])):
            at = pl.ds(pl.multiple_of(start + side * half, half), half)
            total = got[pl.ds(pl.multiple_of(side * half, half), half)].astype(F32)
            out[:half] = (total + own[at].astype(F32)).astype(BF16)

    return split


def add_two(traffic, info, first, second, *refs):
    *small, out = refs if len(refs) == 1 else refs[:2]
    if small:
        add_below(small[0], second, refs[2], out)
    rows = first.shape[0]
    out[:rows] = (first[...].astype(F32) + second[:rows].astype(F32)).astype(BF16)


def add_more(traffic, info, first, second, *refs):
    *small, out = refs if len(refs) == 1 else refs[:2]
    if small:
        add_below(small[0], second, refs[2], out)
        rows = first.shape[0] - BIAS_ROWS
    else:
        rows = first.shape[0]
    out[:rows] = (first[:rows].astype(F32) + second[:rows].astype(F32)).astype(BF16)


def choose(traffic, info, mine, got, *refs):
    *small, out = refs if len(refs) == 1 else refs[:2]
    rows = out.shape[0]

    @pl.when(info[UPPER] == 0)
    def _():
        out[...] = got[:rows]
        if small:
            refs[2][...] = unpacked(got[rows:])

    @pl.when(info[UPPER] != 0)
    def _():
        out[...] = mine[:rows]
        if small:
            refs[2][...] = small[0][...]


def place_rows(begins, segments):
    def place(traffic, info, *refs):
        halves, outs = refs[: 2 * len(begins)], refs[2 * len(begins) :]
        for flag in (0, 1):
            @pl.when(info[ODD] == flag)
            def _():
                for c, begin in enumerate(begins):
                    rows = halves[2 * c].shape[0]
                    for half, side in ((halves[2 * c], flag), (halves[2 * c + 1], 1 - flag)):
                        start = begin + side * rows
                        for first, count, out, row in segments:
                            low, high = max(start, first), min(start + rows, first + count)
                            if low < high:
                                outs[out][row + low - first : row + high - first] = half[
                                    low - start : high - start].astype(F32)

    return place


def collect_small(traffic, info, h0, h1, h2, h3, attention, first_sums, second_sums, own, across, near):
    common = jnp.concatenate([first_sums[0:3], second_sums[0:3]])
    zeros = jnp.zeros_like(common)
    none = jnp.zeros_like(h0)
    own[...] = jnp.concatenate([h0[...], attention[0:1], common])
    across[...] = jnp.concatenate([h2[...], none, zeros])
    near[...] = jnp.concatenate([h1[...], none, h3[...], none, common, zeros])


def add_small(traffic, info, own, across, got, own_out, across_out):
    total = own[...] + jnp.concatenate([got[0:2], got[4:10]])
    own_out[...] = total
    across_out[...] = jnp.concatenate([across[0:2] + got[2:4], total[2:]])


def spread_small(traffic, info, small, inner, query, value, *common):
    inner[...] = small[0:1].reshape(inner.shape)
    width = query.shape[0]
    start = value_start(width)
    query[...] = small[1:2, :width].reshape(query.shape)
    value[...] = small[1:2, start : start + width].reshape(value.shape)
    for i, out in enumerate(common):
        out[...] = small[2 + i : 3 + i].reshape(out.shape)


OUTER, ATTENTION, INNER, LAST, INPUT = range(5)
INNER_ROWS = 512
STEPS = (
    ATTENTION, OUTER, INPUT, INNER, ATTENTION, LAST, OUTER, INNER, ATTENTION, LAST, OUTER, INNER, LAST, ATTENTION, INNER, LAST)
LAST_STEPS = (LAST,)


def hold(run, *arrays):
    def mark(*refs):
        refs[-1][...] = jnp.zeros_like(refs[-1])

    ties = run.ties()
    afar_space = pl.BlockSpec(memory_space=pltpu.HBM)
    *results, token = pl.pallas_call(
        mark,
        name=mark.__name__,
        out_shape=[pltpu.HBM(a.shape, a.dtype) for a in arrays] + [pltpu.VMEM((8, 128), F32)],
        in_specs=[afar_space] * len(arrays) + [pl.BlockSpec(memory_space=pl.ANY)] * len(ties),
        out_specs=[afar_space] * len(arrays) + [pl.BlockSpec(memory_space=pltpu.VMEM)],
        input_output_aliases={i: i for i in range(len(arrays))},
    )(*[pltpu.with_memory_space_constraint(a, pltpu.HBM) for a in arrays], *ties)
    run.last = (token, pltpu.VMEM)
    return results


def chain(run, split):
    keep, send, *small = split()
    shape, sent = keep.shape, send.shape
    small_out = [(s.shape, F32) for s in small]
    got = exchange(send, 1, 0)
    yield
    total, *small = run(add_two, [(sent, BF16)] + small_out, keep, got, *small)
    got = along(total, {0: 1, 3: 2})
    yield
    moves = [lambda a: along(a, {1: 2, 2: 1})] + [lambda a, m=m: exchange(a, m, 0) for m in later_masks()]
    for move in moves + [lambda a: along(a, {1: 0, 2: 3})]:
        total, *small = run(add_more, [(sent, BF16)] + small_out, total, got, *small)
        got = move(total)
        yield
    whole, *small = run(choose, [(shape, BF16)] + small_out, total, got, *small, scalars=[UPPER])
    got = exchange(whole, 1, 0)
    yield
    return (whole, got), small


def on_device(
    layer_input,
    lengths,
    query_weight,
    query_bias,
    key_weight,
    value_weight,
    value_bias,
    out_weight,
    out_bias,
    first_gain,
    first_shift,
    inner_weight,
    inner_bias,
    outer_weight,
    outer_bias,
    second_gain,
    second_shift,
    cotangent,
):
    rows = layer_input.shape[0] // lax.axis_size("tp")
    model = layer_input.shape[1]
    width = query_weight.shape[1]
    hidden = inner_weight.shape[1]
    tp, dp = lax.axis_index("tp"), lax.axis_index("dp")
    upper = (dp >> 1) ^ (dp >> 2)
    run = Sequence([s.reshape(1) for s in (tp, dp & 3, dp & 1, upper & 1)] + [lengths])
    to_core = lambda a: exchange(a, 0, 1)
    to_x = lambda a: exchange(a, 0, 2)
    to_y = lambda a: exchange(a, 1, 0)
    to_z = lambda a: exchange(a, 2, 0)

    full, low = ((rows, model), F32), ((rows, model), BF16)
    square, wide = ((hidden, model), BF16), ((rows, hidden), BF16)
    sums, small = ((8, model), F32), ((SMALL_ROWS, model), F32)
    sequences = lambda *masks: Afar(tuple((layer_input, m, rows) for m in masks), OWN)
    inputs, own_grad = sequences(0), Afar(((cotangent, 0, rows),), OWN)

    near_inner, near_outer = to_core(inner_weight), to_core(outer_weight)
    head, slot = width + BIAS_ROWS, 2 * width // 3
    half_square = Out((hidden // 2, model), BF16)
    feed_weights = afar(inner_weight, outer_weight, way=RAW)
    feed_came = to_x(run(pick_feed, [half_square], feed_weights, scalars=[PLACE])[0])
    (sent,) = run(pick_out, [Out((head, model), BF16)], afar(out_weight), afar(inner_bias), scratch=[small])
    far_out, near_out = to_x(sent), to_core(sent)

    own_weights = [afar(w) for w in (query_weight.T, key_weight.T, value_weight.T)]
    attention_scalars = [TP, LENGTHS]
    seen = [Out((6 * rows, width), BF16), Out((8, rows), F32)]
    heads = lambda masks, outs: run(
        heads_forward(masks), outs + seen, sequences(*masks), *own_weights, afar(query_bias), afar(value_bias),
        scalars=attention_scalars)
    sent, far_qkv, far_log = heads((2, 3), [((2 * slot, model), BF16)])
    came = to_x(sent)
    near_inner, near_outer = hold(run, near_inner, near_outer)
    sent, own_context, near_qkv, near_log = heads((1, 0), [((slot, model), BF16), ((width, rows), BF16)])
    near = to_core(sent)
    far_out, near_out = hold(run, far_out, near_out)
    far_near_out = to_core(far_out)
    (feed_came,) = hold(run, feed_came)
    feed_y, feed_z = to_y(feed_came), to_z(feed_came)
    feed_last_came = to_x(run(pick_last_feed, [half_square], feed_weights, scalars=[PLACE])[0])
    came, near = hold(run, came, near)
    contexts = [afar(a) for a in (near, came, to_core(came))]
    others = (near_out, far_out, far_near_out)
    out_weights = Afar(tuple((a, 0, width) for a in (out_weight,) + others))
    tails = [Afar(((a, width, BIAS_ROWS),)) for a in others]
    first_sum, normed, normed_low, bias_1, bias_2, bias_3 = run(
        project, [Out(*full), full, low] + [small] * 3, inputs, own_context, *contexts, out_weights, *tails, out_bias,
        first_gain, first_shift, scalars=[TP])

    active_0, active_1, slope_0, slope_1, partial = run(
        feed_near, [Out(*wide), wide, Out(*wide), Out(*wide), full], normed_low, normed, outer_bias, afar(inner_weight),
        afar(near_inner), afar(outer_weight), afar(near_outer), inner_bias, bias_1)
    far_feed = hold(run, feed_came, feed_y, feed_z, feed_last_came)
    near_feed = tuple(to_core(a) for a in far_feed)
    quarter = hidden // 4
    inner_2, inner_3 = (Afar(tuple((a, 0, quarter) for a in f), PLACED) for f in (far_feed, near_feed))
    outer_2, outer_3 = (Afar(tuple((a, quarter, quarter) for a in f), PLACED) for f in (far_feed, near_feed))
    (active_2, slope_2), (active_3, slope_3) = (
        run(feed_far, [wide] * 2, normed_low, inner, bias, scalars=[PLACE])
        for inner, bias in ((inner_2, bias_2), (inner_3, bias_3))
    )
    layer_output, second_grad, result_grad, second_sums = run(
        feed_out, [Out(*low), Out(*full), low, sums], active_2, active_3, outer_2, outer_3, partial,
        second_gain, second_shift, own_grad, scalars=[TP, PLACE], scratch=[full])

    near_part = lambda left, right, n: [
        to_core(a) for a in run(near_grad, [((hidden // n, model), BF16)] * n, left, right)]
    far_part = lambda left, right, got, *sizes: run(
        far_grad(len(got)), [((size, model), BF16) for size in sizes], left, right, *got)
    outer_got_3 = near_part(active_3, result_grad, 1)
    outer_got_1 = near_part(active_1, result_grad, 1)
    hidden_out = [wide, wide] + [((1, hidden), F32)] * 2
    hidden_3, hidden_1, sum_3, sum_1 = run(
        hidden_pair, hidden_out, result_grad, outer_3, afar(near_outer), slope_3, afar(slope_1), scalars=[PLACE])
    outer_x = to_x(far_part(active_2, result_grad, outer_got_3, hidden)[0])
    (outer_own,) = far_part(afar(active_0), result_grad, outer_got_1, hidden)
    inner_got_3, inner_got_1 = near_part(normed_low, hidden_3, 2), near_part(normed_low, hidden_1, 2)
    hidden_2, hidden_0, sum_2, sum_0, first_grad, branch_grad, first_sums = run(
        feed_back, hidden_out + [Out(*full), low, sums], result_grad, outer_2, afar(outer_weight), slope_2, afar(slope_0),
        afar(second_grad), hidden_3, hidden_1, inner_3, afar(near_inner), inner_2, afar(inner_weight), afar(first_sum),
        first_gain, scalars=[PLACE], scratch=[full])

    part = ((width, model), BF16)
    cut = INNER_ROWS * hidden // 768
    sent, last_inner = far_part(normed_low, hidden_2, inner_got_3, cut, hidden - cut)
    inner_x = to_x(sent)
    (inner_own,) = far_part(normed_low, hidden_0, inner_got_1, hidden)
    lent = ((slot, model), BF16)
    own_slot, *sent = run(
        context_back, [((width, rows), BF16), lent, lent, lent], branch_grad, out_weights)
    near, far, far_near = to_core(sent[0]), to_x(sent[1]), exchange(sent[2], 0, 3)
    rooms = [((6, rows, width), BF16)]
    weight_rows = (3 * width, model)
    same = lambda block: block
    first_kernel = heads_backward((1, 0), (unfolded_one, same))
    near_input, partial, small_sums, weight_sums = run(
        first_kernel, [Out(*low), Out(*full), Out(*sums), Out(weight_rows, F32)], afar(near_qkv), afar(near), own_slot,
        sequences(1, 0), *own_weights, afar(near_log), afar(first_grad), scalars=attention_scalars, scratch=rooms)
    near_input = to_core(near_input)

    def way_of(own, start, rows, got, *small):
        below = BIAS_ROWS * len(small)
        outs = [((rows // 2, model), BF16), ((rows // 2 + below, model), BF16)] + [(s.shape, F32) for s in small]
        return chain(run, lambda: run(split_rows(start), outs, own, got, *small, scalars=[ODD]))

    outer_way = way_of(outer_own, 0, hidden, outer_x)
    near_parts, part_0, part_2 = run(
        out_back, [((2 * width, model), BF16), part, part], branch_grad, own_context, *contexts)
    near_parts = to_core(near_parts)
    far, far_near = hold(run, far, far_near)
    next(outer_way)
    second_kernel = heads_backward((2, 3), (unfolded_one, unfolded_one))
    far_input, sent, small_sums, attention_own = run(
        second_kernel, [low, low, sums, (weight_rows, BF16)], afar(far_qkv), afar(far), afar(far_near),
        sequences(2, 3), *own_weights, afar(far_log), afar(weight_sums), afar(small_sums), scalars=attention_scalars, scratch=rooms)
    far_near_input = to_core(sent)
    half = ((3 * width // 2, model), BF16)
    attention_way = chain(run, lambda: run(split_own, [half, half], attention_own, scalars=[ODD]))
    next(attention_way)
    small_own, small_across, small_near = run(
        collect_small, [small, small, ((2 * SMALL_ROWS, model), F32)], sum_0, sum_1, sum_2, sum_3,
        small_sums, first_sums, second_sums)
    small_near = to_core(small_near)
    out_own, out_across = run(add_out, [part, part], part_0, part_2, near_parts)
    next(outer_way)
    small_own, small_across = run(add_small, [small, small], small_own, small_across, small_near)
    last_rows = width + hidden - cut
    last_own, sent = run(
        pack_last, [((last_rows, model), BF16), ((last_rows + BIAS_ROWS, model), BF16)], out_own, inner_own,
        out_across, last_inner, small_across)
    last_x = to_x(sent)
    inner_way = way_of(inner_own, 0, cut, inner_x)
    next(inner_way)

    def input_steps():
        (sent,) = run(add_rows, [low], far_input, far_near_input)
        got = to_x(sent)
        yield
        return run(add_input, [Out(*full)], afar(partial), near_input, got)[0]

    ways = {
        OUTER: outer_way, ATTENTION: attention_way, INNER: inner_way,
        LAST: way_of(last_own, 0, last_rows, last_x, small_own), INPUT: input_steps(),
    }
    for number in STEPS:
        next(ways[number])

    def finish(way):
        while True:
            try:
                next(way)
            except StopIteration as stop:
                return stop.value

    finished = {}

    def results(number):
        if number not in finished:
            finished[number] = finish(ways[number])
        return finished[number]

    def place(numbers, begins, segments, *sizes):
        halves = [half for number in numbers for half in results(number)[0]]
        return run(place_rows(begins, segments), [Out((size, model), F32) for size in sizes], *halves, scalars=[ODD])

    (outer_weight_grad,) = place((OUTER,), (0,), ((0, hidden, 0, 0),), hidden)
    for number in LAST_STEPS:
        next(ways[number])
    input_grad = finish(ways[INPUT])
    query_grad, key_grad, value_grad = place(
        (ATTENTION,), (0,), [(i * width, width, i, 0) for i in range(3)], width, width, width)
    _, (last_small,) = results(LAST)
    inner_bias_grad, query_bias_grad, value_bias_grad, *common = run(
        spread_small, [Out((size,), F32) for size in (hidden, width, width) + (model,) * 6], last_small)
    inner_weight_grad, out_grad = place(
        (INNER, LAST), (0, cut),
        ((0, cut, 0, 0), (cut, width, 1, 0), (cut + width, hidden - cut, 0, cut)), hidden, width)
    return (
        layer_output,
        input_grad,
        query_grad.T,
        query_bias_grad,
        key_grad.T,
        value_grad.T,
        value_bias_grad,
        out_grad,
        *common[:3],
        inner_weight_grad,
        inner_bias_grad,
        outer_weight_grad,
        *common[3:],
    )


def solution(mesh):
    in_specs = (
        P("dp", None),
        P("dp"),
        P(None, "tp"),
        P("tp"),
        P(None, "tp"),
        P(None, "tp"),
        P("tp"),
        P("tp", None),
        P(),
        P(),
        P(),
        P(None, "tp"),
        P("tp"),
        P("tp", None),
        P(),
        P(),
        P(),
        P("dp", None),
    )
    out_specs = (
        P(("dp", "tp"), None),
        P(("dp", "tp"), None),
        P(None, "tp"),
        P("tp"),
        P(None, "tp"),
        P(None, "tp"),
        P("tp"),
        P("tp", None),
        P(),
        P(),
        P(),
        P(None, "tp"),
        P("tp"),
        P("tp", None),
        P(),
        P(),
        P(),
    )
    return jax.shard_map(
        on_device, mesh=mesh, in_specs=in_specs, out_specs=out_specs, check_vma=False
    )
```

```python
import dataclasses

import jax
import jax.numpy as jnp
from jax import lax
from jax.experimental import pallas as pl
from jax.experimental.pallas import tpu as pltpu
from jax.sharding import PartitionSpec as P

HD = 64
EPSILON = 1e-05
BF16 = jnp.bfloat16
F32 = jnp.float32
LARGE = 24 * 2**20
STEP_ROWS = 128
KEY_STEP = 160
BIAS_ROWS = 16
SMALL_ROWS = 8

TP, PLACE, ODD, UPPER, LENGTHS = range(5)

ORDERED, PLACED, OWN, RAW = range(4)


def dot(left, right, left_dim=1, right_dim=0):
    return lax.dot_general(
        left, right, (((left_dim,), (right_dim,)), ((), ())), preferred_element_type=F32
    )


@dataclasses.dataclass(frozen=True)
class Afar:
    parts: tuple
    way: int = ORDERED

    def shape(self):
        return (sum(rows for _, _, rows in self.parts),) + self.parts[0][0].shape[1:]


def afar(*arrays, way=ORDERED):
    return Afar(tuple((a, 0, a.shape[0]) for a in arrays), way)


@dataclasses.dataclass(frozen=True)
class Out:
    shape: tuple
    dtype: jnp.dtype


class Traffic:
    def __init__(self, sems):
        self.sems, self.count = sems, 0
        self.coming, self.going, self.sent = {}, {}, []

    def copy(self, source, target):
        copy = pltpu.make_async_copy(source, target, self.sems.at[self.count])
        copy.start()
        self.count += 1
        return copy

    def need(self, *refs):
        for ref in refs:
            for copy in self.coming.pop(id(ref), ()):
                copy.wait()

    def send(self, *refs):
        for ref in refs:
            if id(ref) in self.going:
                self.sent.append(self.copy(ref, self.going.pop(id(ref))))

    def end(self):
        for copies in self.coming.values():
            for copy in copies:
                copy.wait()
        for ref in self.results:
            if id(ref) in self.going:
                self.send(ref)
        for copy in self.sent:
            copy.wait()


class Sequence:
    def __init__(self, scalars):
        self.last, self.scalars = None, scalars

    def ties(self):
        return [] if self.last is None else [pltpu.with_memory_space_constraint(*self.last)]

    def note(self, results, outs):
        smallest = min(range(len(outs)), key=lambda i: results[i].size)
        space = pltpu.HBM if isinstance(outs[smallest], Out) else pltpu.VMEM
        self.last = (results[smallest], space)

    def __call__(self, body, outs, *args, scalars=(), scratch=(), limit=LARGE):
        operands, sizes, fetched, copies = [self.scalars[i] for i in scalars], [], [], 0
        spaces = [pltpu.SMEM] * len(scalars)
        for arg in args:
            if isinstance(arg, Afar):
                operands += [pltpu.with_memory_space_constraint(a, pltpu.HBM) for a, _, _ in arg.parts]
                spaces += [pltpu.HBM] * len(arg.parts)
                sizes.append(len(arg.parts))
                copies += len(arg.parts)
                if arg.way != RAW:
                    fetched.append(pltpu.VMEM(arg.shape(), arg.parts[0][0].dtype))
            else:
                operands.append(arg)
                spaces.append(pltpu.VMEM)
                sizes.append(1)
        ties = self.ties()
        staged = [pltpu.VMEM(out.shape, out.dtype) for out in outs if isinstance(out, Out)]
        copies += len(staged)
        shapes = [
            pltpu.HBM(out.shape, out.dtype) if isinstance(out, Out) else pltpu.VMEM(*out) for out in outs
        ]

        def kernel(*refs):
            refs = list(refs)
            take = lambda n: [refs.pop(0) for _ in range(n)]
            info = {n: ref if n == LENGTHS else ref[0] for n, ref in zip(scalars, take(len(scalars)))}
            given = [take(n) for n in sizes]
            take(len(ties))
            results, buffers, stages, rest = take(len(outs)), take(len(fetched)), take(len(staged)), take(len(scratch))
            traffic = Traffic(refs[0] if refs else None)
            inputs = []
            for arg, sources in zip(args, given):
                if not isinstance(arg, Afar):
                    inputs += sources
                    continue
                if arg.way == RAW:
                    inputs.append(sources)
                    continue
                buffer = buffers.pop(0)
                inputs.append(buffer)
                copies, start = [], 0
                for i, (source, (_, first, rows)) in enumerate(zip(sources, arg.parts)):
                    if arg.way == OWN:
                        first = pl.multiple_of((info[TP] ^ first) * rows, rows)
                    if arg.way == PLACED:
                        start = pl.multiple_of((info[PLACE] ^ i) * rows, rows)
                    copies.append(traffic.copy(source.at[pl.ds(first, rows)], buffer.at[pl.ds(start, rows)]))
                    start += rows
                traffic.coming[id(buffer)] = copies
            for i, out in enumerate(outs):
                if isinstance(out, Out):
                    stage = stages.pop(0)
                    traffic.going[id(stage)] = results[i]
                    results[i] = stage
            traffic.results = results
            body(traffic, info, *inputs, *results, *rest)
            traffic.end()

        results = pl.pallas_call(
            kernel,
            name=body.__name__,
            out_shape=shapes,
            in_specs=[pl.BlockSpec(memory_space=space) for space in spaces]
            + [pl.BlockSpec(memory_space=pl.ANY)] * len(ties),
            out_specs=[pl.BlockSpec(memory_space=pltpu.HBM if isinstance(o, Out) else pltpu.VMEM) for o in outs],
            scratch_shapes=fetched + staged + [pltpu.VMEM(shape, dtype) for shape, dtype in scratch]
            + ([pltpu.SemaphoreType.DMA((copies,))] if copies else []),
            compiler_params=pltpu.CompilerParams(vmem_limit_bytes=limit),
        )(*operands, *ties)
        self.note(results, outs)
        return results


def exchange(array, dp_bits, tp_bits):
    dp_size, tp_size = lax.axis_size("dp"), lax.axis_size("tp")
    pairs = [
        (d * tp_size + t, (d ^ dp_bits) * tp_size + (t ^ tp_bits))
        for d in range(dp_size)
        for t in range(tp_size)
    ]
    return lax.ppermute(array, ("dp", "tp"), pairs)


def along(array, moves):
    dp_size, tp_size = lax.axis_size("dp"), lax.axis_size("tp")
    pairs = [
        (d * tp_size + t, ((d & ~6) | (moves[(d >> 1) & 3] << 1)) * tp_size + t)
        for d in range(dp_size)
        for t in range(tp_size)
        if (d >> 1) & 3 in moves
    ]
    return lax.ppermute(array, ("dp", "tp"), pairs)


def later_masks():
    masks, bit = [], 8
    while bit < lax.axis_size("dp"):
        masks.append(bit)
        bit *= 2
    return masks


def folded(rows):
    return jnp.sum(rows.reshape(rows.shape[0] // 8, 8, rows.shape[1]), axis=0)


def normalize(values):
    average = jnp.mean(values, axis=-1, keepdims=True)
    centered = values - average
    spread = jnp.mean(centered * centered, axis=-1, keepdims=True)
    scale = lax.rsqrt(spread + EPSILON)
    return centered * scale, scale


def norm_backward(e, rows, scale):
    first = jnp.mean(e, axis=-1, keepdims=True)
    second = jnp.mean(e * rows, axis=-1, keepdims=True)
    return scale * (e - first - rows * second)


def row_steps(rows):
    return [slice(i, i + STEP_ROWS) for i in range(0, rows, STEP_ROWS)]


def as_row(ref):
    return ref[...].reshape(1, ref.shape[0])


def packed(values):
    high = values.astype(BF16).astype(F32)
    return jnp.concatenate([high, values - high]).astype(BF16)


def unpacked(pairs):
    rows = pairs[...].astype(F32)
    return rows[: BIAS_ROWS // 2] + rows[BIAS_ROWS // 2 :]


def folded_one(part):
    rows, columns = part.shape
    third = rows // 3
    last = part[2 * third :]
    side = jnp.concatenate([last[:, : columns // 2], last[:, columns // 2 :]])
    return jnp.concatenate([part[: 2 * third], side], axis=1)


def unfolded_one(block):
    rows = block.shape[0] // 2
    columns = block.shape[1] * 2 // 3
    last = jnp.concatenate([block[:rows, columns:], block[rows:, columns:]], axis=1)
    return jnp.concatenate([block[:, :columns], last])


def folded_two(first, second):
    half, third = second.shape[1] // 2, second.shape[0] // 3
    below = [second[i * third : (i + 1) * third, half:] for i in range(3)]
    return jnp.concatenate(
        [jnp.concatenate([first, second[:, :half]], axis=1), jnp.concatenate(below, axis=1)])


def unfolded_first(block):
    rows, columns = block.shape[0] * 3 // 4, block.shape[1] * 2 // 3
    return block[:rows, :columns]


def unfolded_second(block):
    rows, columns = block.shape[0] * 3 // 4, block.shape[1] * 2 // 3
    below = block[rows:]
    right = jnp.concatenate([below[:, i * columns // 2 : (i + 1) * columns // 2] for i in range(3)])
    return jnp.concatenate([block[:rows, columns:], right], axis=1)


def pick_out(traffic, info, out_weight, inner_bias, sent, values):
    traffic.need(out_weight, inner_bias)
    rows = out_weight.shape[0]
    values[...] = jnp.zeros_like(values)
    values[0:1] = as_row(inner_bias)
    sent[:rows] = out_weight[...]
    sent[rows:] = packed(values[...])


def pick_feed(traffic, info, blocks, target):
    rows = target.shape[0] // 2
    copies = []
    for i, block in enumerate(blocks):
        at = pl.ds(pl.multiple_of(info[PLACE] * rows, rows), rows)
        copies.append(traffic.copy(block.at[at], target.at[pl.ds(i * rows, rows)]))
    for copy in copies:
        copy.wait()


def pick_last_feed(traffic, info, blocks, target):
    pick_feed(traffic, {PLACE: info[PLACE] ^ 3}, blocks, target)


def lone_head(transposed, head):
    part = transposed[head * HD : (head + 1) * HD]
    if head // 2 * 2 + 1 >= transposed.shape[0] // HD:
        return part
    zeros = jnp.zeros_like(part)
    return jnp.concatenate([part, zeros] if head % 2 == 0 else [zeros, part])


def tile(array, head):
    start = head // 2 * 2 * HD
    return array[:, start : start + 2 * HD]


def hidden_keys(rows, length):
    return jnp.where(lax.broadcasted_iota(jnp.int32, (rows, 1), 0) < length, 0.0, -1e30)


def visible_scores(keys, queries_t, head, hidden):
    return dot(tile(keys, head), lone_head(queries_t, head)) + hidden


def heads_forward(masks):
    def forward(traffic, info, inputs, query_weight, key_weight, value_weight, query_bias, value_bias, sent, *refs):
        *own, qkv, log_total = refs
        width = query_weight.shape[0]
        rows = inputs.shape[0] // 2
        heads = width // HD
        contexts = []
        traffic.need(query_weight, key_weight, value_weight, query_bias, value_bias, inputs)
        for i, mask in enumerate(masks):
            x = inputs[i * rows : (i + 1) * rows]
            queries = (dot(x, query_weight[...], 1, 1) + as_row(query_bias)).astype(BF16)
            keys = dot(x, key_weight[...], 1, 1).astype(BF16)
            vals = (dot(x, value_weight[...], 1, 1) + as_row(value_bias)).astype(BF16)
            for j, part in enumerate((queries, keys, vals)):
                qkv[(3 * i + j) * rows : (3 * i + j + 1) * rows] = part
            queries_t = (queries * HD**-0.5).astype(BF16).T
            values_t = vals.T
            hidden = hidden_keys(rows, info[LENGTHS][info[TP] ^ mask])
            context = []
            for h in range(heads):
                scores = visible_scores(keys, queries_t, h, hidden)
                top = jnp.max(scores, axis=0, keepdims=True)
                raised = jnp.exp(scores - top)
                total = jnp.sum(raised, axis=0, keepdims=True)
                log_total[i * heads + h : i * heads + h + 1] = top + jnp.log(total)
                sums = dot(values_t[h * HD : (h + 1) * HD], raised.astype(BF16))
                context.append((sums / total).astype(BF16))
            contexts.append(jnp.concatenate(context))
        if own:
            own[0][...] = contexts[1]
            sent[...] = folded_one(contexts[0])
        else:
            sent[...] = folded_two(*contexts)

    return forward


def all_contexts(own, near, far, far_near):
    return jnp.concatenate([own[...], unfolded_one(near[...]), unfolded_first(far[...]), unfolded_second(far_near[...])])


def project(traffic, info, inputs, own_context, near, far, far_near, weights, tail_1, tail_2, tail_3, out_bias,
            gain, shift, first_sum, normed, normed_low, bias_1, bias_2, bias_3):
    traffic.need(near, far, far_near, weights)
    branch = dot(all_contexts(own_context, near, far, far_near), weights[...], 0, 0)
    traffic.need(inputs)
    first_sum[...] = inputs[...].astype(F32) + as_row(out_bias) + branch
    traffic.send(first_sum)
    for at in row_steps(first_sum.shape[0]):
        out = normalize(first_sum[at])[0] * as_row(gain) + as_row(shift)
        normed[at] = out
        normed_low[at] = out.astype(BF16)
    traffic.need(tail_1, tail_2, tail_3)
    for tail, bias in ((tail_1, bias_1), (tail_2, bias_2), (tail_3, bias_3)):
        bias[...] = unpacked(tail)


def context_back(traffic, info, branch_grad, weights, own_grad, *sent):
    traffic.need(weights)
    grads = dot(weights[...], branch_grad[...], 1, 1).astype(BF16)
    width = own_grad.shape[0]
    own_grad[...] = grads[:width]
    for i, part in enumerate(sent):
        part[...] = folded_one(grads[(1 + i) * width : (2 + i) * width])
        traffic.send(part)


def out_back(traffic, info, branch_grad, own_context, near, far, far_near, near_parts, part_0, part_2):
    traffic.need(near, far, far_near)
    parts = dot(all_contexts(own_context, near, far, far_near), branch_grad[...]).astype(BF16)
    width = part_0.shape[0]
    slot = lambda s: parts[s * width : (s + 1) * width]
    part_0[...], part_2[...] = slot(0), slot(2)
    near_parts[:width], near_parts[width:] = slot(1), slot(3)


def heads_backward(masks, unfold):
    def backward(traffic, info, qkv, context_a, context_b, inputs, query_weight, key_weight, value_weight, log_total, *refs):
        wide = refs[-1]
        first = len(refs) == 6
        before, (grad_a, grad_b, sums_out, *weight_sums) = (refs[:1], refs[1:-1]) if first else (refs[:2], refs[2:-1])
        rows = inputs.shape[0] // 2
        width = query_weight.shape[0]
        heads = width // HD
        lane = lambda count: lax.broadcasted_iota(jnp.int32, (count, 2 * HD), 1)
        traffic.need(qkv, log_total, context_a, context_b)

        def sequence(i, context, length, count):
            queries, keys, vals = (qkv[(3 * i + j) * rows : (3 * i + j) * rows + n] for j, n in enumerate((rows, count, count)))
            grads_t = unfold[i](context[...])
            grads = grads_t.T
            queries_t = (queries * HD**-0.5).astype(BF16).T
            keys_t = keys.T
            hidden = hidden_keys(count, length)
            query_parts, pairs = [], []
            for h in range(heads):
                n = i * heads + h
                probs = jnp.exp(visible_scores(keys, queries_t, h, hidden) - log_total[n : n + 1])
                prob_grad = dot(tile(vals, h), lone_head(grads_t, h))
                inner = jnp.sum(probs * prob_grad, axis=0, keepdims=True)
                score_grad = (probs * (prob_grad - inner)).astype(BF16)
                value_grad = dot(probs.astype(BF16), tile(grads, h))
                key_grad = dot(score_grad, tile(queries, h)) * HD**-0.5
                query_parts.append(dot(keys_t[h * HD : (h + 1) * HD], score_grad) * HD**-0.5)
                pairs.append((key_grad, value_grad))
            wide[3 * i] = jnp.concatenate(query_parts).astype(BF16).T
            for j in (0, 1):
                at = 3 * i + 1 + j
                for h in range(0, heads, 2):
                    if h + 1 < heads:
                        wide[at, :count, h * HD : (h + 2) * HD] = jnp.where(
                            lane(count) < HD, pairs[h][j], pairs[h + 1][j]).astype(BF16)
                    else:
                        wide[at, :count, h * HD :] = pairs[h][j].astype(BF16)
                if count < rows:
                    wide[at, count:] = jnp.zeros((rows - count, width), BF16)

        counts = [KEY_STEP, 2 * KEY_STEP, rows]
        for i, (mask, context) in enumerate(zip(masks, (context_a, context_b))):
            length = info[LENGTHS][info[TP] ^ mask]
            for low, count in zip([0] + counts, counts):
                @pl.when((length > low) & (length <= count))
                def _():
                    sequence(i, context, length, count)

        traffic.need(query_weight, key_weight, value_weight)
        for i, out in enumerate((grad_a, grad_b)):
            total = dot(wide[3 * i], query_weight[...]) + dot(wide[3 * i + 1], key_weight[...])
            total = total + dot(wide[3 * i + 2], value_weight[...])
            if out.dtype == F32:
                traffic.need(before[0])
                out[...] = before[0][...] + total
                traffic.send(out)
            else:
                out[...] = total.astype(BF16)
        model = sums_out.shape[1]

        def summed(j):
            row = sum(jnp.sum(wide[3 * i + j].astype(F32), axis=0, keepdims=True) for i in (0, 1))
            return jnp.concatenate([row, jnp.zeros((1, model - width), F32)], axis=1)

        eight = lambda row: jnp.broadcast_to(row, sums_out.shape)
        sums = eight(summed(0)) + pltpu.roll(eight(summed(2)), value_start(width), 1)
        traffic.need(inputs)
        x = inputs[...]
        for j in range(3):
            grad_t = jnp.concatenate([wide[j].T, wide[3 + j].T], axis=1)
            block = dot(grad_t, x)
            if not first:
                traffic.need(*before)
            at = slice(j * width, (j + 1) * width)
            if first:
                weight_sums[0][at] = block
            else:
                weight_sums[0][at] = (before[0][at] + block).astype(BF16)
        sums_out[...] = sums if first else before[1][...] + sums

    return backward


def value_start(width):
    return -(-width // 128) * 128


def feed_slot(normed_low, inner, biases, active, slope):
    bias = biases[...].reshape(1, biases.shape[0]) if len(biases.shape) == 1 else biases[0:1]
    columns = 256
    for c in range(0, inner.shape[1], columns):
        at = slice(c, c + columns)
        hidden = dot(normed_low[...], inner[:, at]) + bias[:, at]
        half_erf = 0.5 * (1.0 + lax.erf(hidden * 0.5**0.5))
        active[:, at] = (hidden * half_erf).astype(BF16)
        slope[:, at] = (
            half_erf + hidden * jnp.exp(-0.5 * hidden * hidden) * 0.3989422804014327
        ).astype(BF16)


def feed_near(traffic, info, normed_low, normed, outer_bias, inner_a, inner_b, outer_a, outer_b, bias_a, bias_b,
              active_a, active_b, slope_a, slope_b, after):
    traffic.need(inner_a)
    feed_slot(normed_low, inner_a, bias_a, active_a, slope_a)
    traffic.send(active_a, slope_a)
    traffic.need(inner_b)
    feed_slot(normed_low, inner_b, bias_b, active_b, slope_b)
    traffic.send(active_b, slope_b)
    traffic.need(outer_a, outer_b)
    after[...] = (
        normed[...] + as_row(outer_bias) + dot(active_a[...], outer_a[...]) + dot(active_b[...], outer_b[...])
    )


def feed_far(traffic, info, normed_low, inner, bias, active, slope):
    traffic.need(inner)
    feed_slot(normed_low, inner, bias, active, slope)


def feed_out(traffic, info, active_a, active_b, outer_a, outer_b, before, gain, shift, cotangent,
             output, second_grad, result_grad, sums, total):
    traffic.need(outer_a, outer_b)
    total[...] = before[...] + dot(active_a[...], outer_a[...]) + dot(active_b[...], outer_b[...])
    traffic.need(cotangent)
    parts = [0.0] * 3
    for at in row_steps(total.shape[0]):
        rows, scale = normalize(total[at])
        output[at] = (rows * as_row(gain) + as_row(shift)).astype(BF16)
        grad = cotangent[at].astype(F32)
        back = norm_backward(grad * as_row(gain), rows, scale)
        second_grad[at] = back
        result_grad[at] = back.astype(BF16)
        parts = [c + folded(v) for c, v in zip(parts, (back, grad * rows, grad))]
    for i, part in enumerate(parts):
        sums[i : i + 1] = jnp.sum(part, axis=0, keepdims=True)


def near_grad(traffic, info, left, right, *chunks):
    traffic.need(left)
    total = dot(left[...], right[...], 0, 0).astype(BF16)
    rows = chunks[0].shape[0]
    for i, chunk in enumerate(chunks):
        chunk[...] = total[i * rows : (i + 1) * rows]


def far_grad(parts):
    def grad(traffic, info, left, right, *refs):
        traffic.need(left)
        total = dot(left[...], right[...], 0, 0)
        total = total + jnp.concatenate([ref[...].astype(F32) for ref in refs[:parts]])
        at = 0
        for chunk in refs[parts:]:
            rows = chunk.shape[0]
            chunk[...] = total[at : at + rows].astype(BF16)
            at += rows

    return grad


def hidden_pair(traffic, info, result_grad, outer_a, outer_b, slope_a, slope_b, grad_a, grad_b, sum_a, sum_b):
    for outer, slope, hidden_grad, bias_sum in (
        (outer_a, slope_a, grad_a, sum_a), (outer_b, slope_b, grad_b, sum_b)
    ):
        traffic.need(outer, slope)
        grad = (dot(result_grad[...], outer[...], 1, 1) * slope[...].astype(F32)).astype(BF16)
        hidden_grad[...] = grad
        bias_sum[...] = jnp.sum(grad.astype(F32), axis=0, keepdims=True)


def feed_back(traffic, info, result_grad, outer_2, outer_0, slope_2, slope_0, before, grad_3, grad_1,
              inner_3, inner_1, inner_2, inner_0, first_sum, gain,
              grad_2, grad_0, sum_2, sum_0, first_grad, branch_grad, sums, total):
    hidden_pair(traffic, info, result_grad, outer_2, outer_0, slope_2, slope_0, grad_2, grad_0, sum_2, sum_0)
    traffic.need(before)
    total[...] = before[...]
    for g, w in ((grad_3, inner_3), (grad_1, inner_1), (grad_2, inner_2), (grad_0, inner_0)):
        traffic.need(w)
        total[...] += dot(g[...], w[...], 1, 1)
    traffic.need(first_sum)
    parts = [0.0] * 3
    for at in row_steps(total.shape[0]):
        rows, scale = normalize(first_sum[at])
        grad = total[at]
        back = norm_backward(grad * as_row(gain), rows, scale)
        first_grad[at] = back
        branch_grad[at] = back.astype(BF16)
        parts = [c + folded(v) for c, v in zip(parts, (back, grad * rows, grad))]
    for i, part in enumerate(parts):
        sums[i : i + 1] = jnp.sum(part, axis=0, keepdims=True)


def add_out(traffic, info, part_0, part_2, got, own, across):
    rows = own.shape[0]
    own[...] = (part_0[...].astype(F32) + got[:rows].astype(F32)).astype(BF16)
    across[...] = (part_2[...].astype(F32) + got[rows:].astype(F32)).astype(BF16)


def add_rows(traffic, info, first, got, out):
    out[...] = (first[...].astype(F32) + got[...].astype(F32)).astype(BF16)


def add_input(traffic, info, partial, near, far, out):
    traffic.need(partial)
    out[...] = partial[...] + near[...].astype(F32) + far[...].astype(F32)


def pack_last(traffic, info, out_own, inner_own, out_across, inner_across, small, own, sent):
    rows, rest = out_own.shape[0], inner_across.shape[0]
    own[:rows] = out_own[...]
    own[rows:] = inner_own[inner_own.shape[0] - rest :]
    sent[:rows] = out_across[...]
    sent[rows : rows + rest] = inner_across[...]
    sent[rows + rest :] = packed(small[...])


def split_own(traffic, info, own, keep, send):
    half = keep.shape[0]
    for out, side in ((keep, info[ODD]), (send, 1 - info[ODD])):
        out[...] = own[pl.ds(pl.multiple_of(side * half, half), half)]


def add_below(small, got, small_out, send=None):
    total = small[...] + unpacked(got[got.shape[0] - BIAS_ROWS :])
    small_out[...] = total
    if send is not None:
        send[send.shape[0] - BIAS_ROWS :] = packed(total)


def split_rows(start):
    def split(traffic, info, own, got, *refs):
        *small, keep, send = refs
        if small:
            small, (keep, send, small_out) = small[0], refs[1:]
            add_below(small, got, small_out, send)
        half = keep.shape[0]
        for out, side in ((keep, info[ODD]), (send, 1 - info[ODD])):
            at = pl.ds(pl.multiple_of(start + side * half, half), half)
            total = got[pl.ds(pl.multiple_of(side * half, half), half)].astype(F32)
            out[:half] = (total + own[at].astype(F32)).astype(BF16)

    return split


def add_two(traffic, info, first, second, *refs):
    *small, out = refs if len(refs) == 1 else refs[:2]
    if small:
        add_below(small[0], second, refs[2], out)
    rows = first.shape[0]
    out[:rows] = (first[...].astype(F32) + second[:rows].astype(F32)).astype(BF16)


def add_more(traffic, info, first, second, *refs):
    *small, out = refs if len(refs) == 1 else refs[:2]
    if small:
        add_below(small[0], second, refs[2], out)
        rows = first.shape[0] - BIAS_ROWS
    else:
        rows = first.shape[0]
    out[:rows] = (first[:rows].astype(F32) + second[:rows].astype(F32)).astype(BF16)


def choose(traffic, info, mine, got, *refs):
    *small, out = refs if len(refs) == 1 else refs[:2]
    rows = out.shape[0]

    @pl.when(info[UPPER] == 0)
    def _():
        out[...] = got[:rows]
        if small:
            refs[2][...] = unpacked(got[rows:])

    @pl.when(info[UPPER] != 0)
    def _():
        out[...] = mine[:rows]
        if small:
            refs[2][...] = small[0][...]


def place_rows(begins, segments):
    def place(traffic, info, *refs):
        halves, outs = refs[: 2 * len(begins)], refs[2 * len(begins) :]
        for flag in (0, 1):
            @pl.when(info[ODD] == flag)
            def _():
                for c, begin in enumerate(begins):
                    rows = halves[2 * c].shape[0]
                    for half, side in ((halves[2 * c], flag), (halves[2 * c + 1], 1 - flag)):
                        start = begin + side * rows
                        for first, count, out, row in segments:
                            low, high = max(start, first), min(start + rows, first + count)
                            if low < high:
                                outs[out][row + low - first : row + high - first] = half[
                                    low - start : high - start].astype(F32)

    return place


def collect_small(traffic, info, h0, h1, h2, h3, attention, first_sums, second_sums, own, across, near):
    common = jnp.concatenate([first_sums[0:3], second_sums[0:3]])
    zeros = jnp.zeros_like(common)
    none = jnp.zeros_like(h0)
    own[...] = jnp.concatenate([h0[...], attention[0:1], common])
    across[...] = jnp.concatenate([h2[...], none, zeros])
    near[...] = jnp.concatenate([h1[...], none, h3[...], none, common, zeros])


def add_small(traffic, info, own, across, got, own_out, across_out):
    total = own[...] + jnp.concatenate([got[0:2], got[4:10]])
    own_out[...] = total
    across_out[...] = jnp.concatenate([across[0:2] + got[2:4], total[2:]])


def spread_small(traffic, info, small, inner, query, value, *common):
    inner[...] = small[0:1].reshape(inner.shape)
    width = query.shape[0]
    start = value_start(width)
    query[...] = small[1:2, :width].reshape(query.shape)
    value[...] = small[1:2, start : start + width].reshape(value.shape)
    for i, out in enumerate(common):
        out[...] = small[2 + i : 3 + i].reshape(out.shape)


OUTER, ATTENTION, INNER, LAST, INPUT = range(5)
INNER_ROWS = 512
STEPS = (
    ATTENTION, OUTER, INPUT, INNER, ATTENTION, LAST, OUTER, INNER, ATTENTION, LAST, OUTER, INNER, LAST, ATTENTION, INNER, LAST)
LAST_STEPS = (LAST,)


def hold(run, *arrays):
    def mark(*refs):
        refs[-1][...] = jnp.zeros_like(refs[-1])

    ties = run.ties()
    afar_space = pl.BlockSpec(memory_space=pltpu.HBM)
    *results, token = pl.pallas_call(
        mark,
        name=mark.__name__,
        out_shape=[pltpu.HBM(a.shape, a.dtype) for a in arrays] + [pltpu.VMEM((8, 128), F32)],
        in_specs=[afar_space] * len(arrays) + [pl.BlockSpec(memory_space=pl.ANY)] * len(ties),
        out_specs=[afar_space] * len(arrays) + [pl.BlockSpec(memory_space=pltpu.VMEM)],
        input_output_aliases={i: i for i in range(len(arrays))},
    )(*[pltpu.with_memory_space_constraint(a, pltpu.HBM) for a in arrays], *ties)
    run.last = (token, pltpu.VMEM)
    return results


def place_last(run, most, cut, width, halves):
    rows, model = halves[0].shape
    rest = most.shape[0] - cut

    def last(odd, base, mine, other, *refs):
        inner, out, inner_stage, out_stage, sems = refs[-5:]
        for flag in (0, 1):
            @pl.when(odd[0] == flag)
            def _():
                for half, side in ((mine, flag), (other, 1 - flag)):
                    for stage, first, count in ((out_stage, 0, width), (inner_stage, width, rest)):
                        low, high = max(side * rows, first), min((side + 1) * rows, first + count)
                        if low < high:
                            stage[low - first : high - first] = half[low - side * rows : high - side * rows].astype(F32)
        copies = [
            pltpu.make_async_copy(inner_stage, inner.at[pl.ds(cut, rest)], sems.at[0]),
            pltpu.make_async_copy(out_stage, out, sems.at[1]),
        ]
        for copy in copies:
            copy.start()
        for copy in copies:
            copy.wait()

    ties = run.ties()
    afar_space, near_space = pl.BlockSpec(memory_space=pltpu.HBM), pl.BlockSpec(memory_space=pltpu.VMEM)
    return pl.pallas_call(
        last,
        name=last.__name__,
        out_shape=[pltpu.HBM(most.shape, F32), pltpu.HBM((width, model), F32)],
        in_specs=[pl.BlockSpec(memory_space=pltpu.SMEM), afar_space, near_space, near_space]
        + [pl.BlockSpec(memory_space=pl.ANY)] * len(ties),
        out_specs=[afar_space, afar_space],
        scratch_shapes=[pltpu.VMEM((rest, model), F32), pltpu.VMEM((width, model), F32), pltpu.SemaphoreType.DMA((2,))],
        input_output_aliases={1: 0},
        compiler_params=pltpu.CompilerParams(vmem_limit_bytes=LARGE),
    )(run.scalars[ODD], pltpu.with_memory_space_constraint(most, pltpu.HBM), *halves, *ties)


def chain(run, split):
    keep, send, *small = split()
    shape, sent = keep.shape, send.shape
    small_out = [(s.shape, F32) for s in small]
    got = exchange(send, 1, 0)
    yield
    total, *small = run(add_two, [(sent, BF16)] + small_out, keep, got, *small)
    got = along(total, {0: 1, 3: 2})
    yield
    moves = [lambda a: along(a, {1: 2, 2: 1})] + [lambda a, m=m: exchange(a, m, 0) for m in later_masks()]
    for move in moves + [lambda a: along(a, {1: 0, 2: 3})]:
        total, *small = run(add_more, [(sent, BF16)] + small_out, total, got, *small)
        got = move(total)
        yield
    whole, *small = run(choose, [(shape, BF16)] + small_out, total, got, *small, scalars=[UPPER])
    got = exchange(whole, 1, 0)
    yield
    return (whole, got), small


def on_device(
    layer_input,
    lengths,
    query_weight,
    query_bias,
    key_weight,
    value_weight,
    value_bias,
    out_weight,
    out_bias,
    first_gain,
    first_shift,
    inner_weight,
    inner_bias,
    outer_weight,
    outer_bias,
    second_gain,
    second_shift,
    cotangent,
):
    rows = layer_input.shape[0] // lax.axis_size("tp")
    model = layer_input.shape[1]
    width = query_weight.shape[1]
    hidden = inner_weight.shape[1]
    tp, dp = lax.axis_index("tp"), lax.axis_index("dp")
    upper = (dp >> 1) ^ (dp >> 2)
    run = Sequence([s.reshape(1) for s in (tp, dp & 3, dp & 1, upper & 1)] + [lengths])
    to_core = lambda a: exchange(a, 0, 1)
    to_x = lambda a: exchange(a, 0, 2)
    to_y = lambda a: exchange(a, 1, 0)
    to_z = lambda a: exchange(a, 2, 0)

    full, low = ((rows, model), F32), ((rows, model), BF16)
    square, wide = ((hidden, model), BF16), ((rows, hidden), BF16)
    sums, small = ((8, model), F32), ((SMALL_ROWS, model), F32)
    sequences = lambda *masks: Afar(tuple((layer_input, m, rows) for m in masks), OWN)
    inputs, own_grad = sequences(0), Afar(((cotangent, 0, rows),), OWN)

    near_inner, near_outer = to_core(inner_weight), to_core(outer_weight)
    head, slot = width + BIAS_ROWS, 2 * width // 3
    half_square = Out((hidden // 2, model), BF16)
    feed_weights = afar(inner_weight, outer_weight, way=RAW)
    feed_came = to_x(run(pick_feed, [half_square], feed_weights, scalars=[PLACE])[0])
    (sent,) = run(pick_out, [Out((head, model), BF16)], afar(out_weight), afar(inner_bias), scratch=[small])
    far_out, near_out = to_x(sent), to_core(sent)

    own_weights = [afar(w) for w in (query_weight.T, key_weight.T, value_weight.T)]
    attention_scalars = [TP, LENGTHS]
    seen = [Out((6 * rows, width), BF16), Out((8, rows), F32)]
    heads = lambda masks, outs: run(
        heads_forward(masks), outs + seen, sequences(*masks), *own_weights, afar(query_bias), afar(value_bias),
        scalars=attention_scalars)
    sent, far_qkv, far_log = heads((2, 3), [((2 * slot, model), BF16)])
    came = to_x(sent)
    near_inner, near_outer = hold(run, near_inner, near_outer)
    sent, own_context, near_qkv, near_log = heads((1, 0), [((slot, model), BF16), ((width, rows), BF16)])
    near = to_core(sent)
    far_out, near_out = hold(run, far_out, near_out)
    far_near_out = to_core(far_out)
    (feed_came,) = hold(run, feed_came)
    feed_y, feed_z = to_y(feed_came), to_z(feed_came)
    feed_last_came = to_x(run(pick_last_feed, [half_square], feed_weights, scalars=[PLACE])[0])
    came, near = hold(run, came, near)
    contexts = [afar(a) for a in (near, came, to_core(came))]
    others = (near_out, far_out, far_near_out)
    out_weights = Afar(tuple((a, 0, width) for a in (out_weight,) + others))
    tails = [Afar(((a, width, BIAS_ROWS),)) for a in others]
    first_sum, normed, normed_low, bias_1, bias_2, bias_3 = run(
        project, [Out(*full), full, low] + [small] * 3, inputs, own_context, *contexts, out_weights, *tails, out_bias,
        first_gain, first_shift, scalars=[TP])

    active_0, active_1, slope_0, slope_1, partial = run(
        feed_near, [Out(*wide), wide, Out(*wide), Out(*wide), full], normed_low, normed, outer_bias, afar(inner_weight),
        afar(near_inner), afar(outer_weight), afar(near_outer), inner_bias, bias_1)
    far_feed = hold(run, feed_came, feed_y, feed_z, feed_last_came)
    near_feed = tuple(to_core(a) for a in far_feed)
    quarter = hidden // 4
    inner_2, inner_3 = (Afar(tuple((a, 0, quarter) for a in f), PLACED) for f in (far_feed, near_feed))
    outer_2, outer_3 = (Afar(tuple((a, quarter, quarter) for a in f), PLACED) for f in (far_feed, near_feed))
    (active_2, slope_2), (active_3, slope_3) = (
        run(feed_far, [wide] * 2, normed_low, inner, bias, scalars=[PLACE])
        for inner, bias in ((inner_2, bias_2), (inner_3, bias_3))
    )
    layer_output, second_grad, result_grad, second_sums = run(
        feed_out, [Out(*low), Out(*full), low, sums], active_2, active_3, outer_2, outer_3, partial,
        second_gain, second_shift, own_grad, scalars=[TP, PLACE], scratch=[full])

    near_part = lambda left, right, n: [
        to_core(a) for a in run(near_grad, [((hidden // n, model), BF16)] * n, left, right)]
    far_part = lambda left, right, got, *sizes: run(
        far_grad(len(got)), [((size, model), BF16) for size in sizes], left, right, *got)
    outer_got_3 = near_part(active_3, result_grad, 1)
    outer_got_1 = near_part(active_1, result_grad, 1)
    hidden_out = [wide, wide] + [((1, hidden), F32)] * 2
    hidden_3, hidden_1, sum_3, sum_1 = run(
        hidden_pair, hidden_out, result_grad, outer_3, afar(near_outer), slope_3, afar(slope_1), scalars=[PLACE])
    outer_x = to_x(far_part(active_2, result_grad, outer_got_3, hidden)[0])
    (outer_own,) = far_part(afar(active_0), result_grad, outer_got_1, hidden)
    inner_got_3, inner_got_1 = near_part(normed_low, hidden_3, 2), near_part(normed_low, hidden_1, 2)
    hidden_2, hidden_0, sum_2, sum_0, first_grad, branch_grad, first_sums = run(
        feed_back, hidden_out + [Out(*full), low, sums], result_grad, outer_2, afar(outer_weight), slope_2, afar(slope_0),
        afar(second_grad), hidden_3, hidden_1, inner_3, afar(near_inner), inner_2, afar(inner_weight), afar(first_sum),
        first_gain, scalars=[PLACE], scratch=[full])

    part = ((width, model), BF16)
    cut = INNER_ROWS * hidden // 768
    sent, last_inner = far_part(normed_low, hidden_2, inner_got_3, cut, hidden - cut)
    inner_x = to_x(sent)
    (inner_own,) = far_part(normed_low, hidden_0, inner_got_1, hidden)
    lent = ((slot, model), BF16)
    own_slot, *sent = run(
        context_back, [((width, rows), BF16), lent, lent, lent], branch_grad, out_weights)
    near, far, far_near = to_core(sent[0]), to_x(sent[1]), exchange(sent[2], 0, 3)
    rooms = [((6, rows, width), BF16)]
    weight_rows = (3 * width, model)
    same = lambda block: block
    first_kernel = heads_backward((1, 0), (unfolded_one, same))
    near_input, partial, small_sums, weight_sums = run(
        first_kernel, [Out(*low), Out(*full), Out(*sums), Out(weight_rows, F32)], afar(near_qkv), afar(near), own_slot,
        sequences(1, 0), *own_weights, afar(near_log), afar(first_grad), scalars=attention_scalars, scratch=rooms)
    near_input = to_core(near_input)

    def way_of(own, start, rows, got, *small):
        below = BIAS_ROWS * len(small)
        outs = [((rows // 2, model), BF16), ((rows // 2 + below, model), BF16)] + [(s.shape, F32) for s in small]
        return chain(run, lambda: run(split_rows(start), outs, own, got, *small, scalars=[ODD]))

    outer_way = way_of(outer_own, 0, hidden, outer_x)
    near_parts, part_0, part_2 = run(
        out_back, [((2 * width, model), BF16), part, part], branch_grad, own_context, *contexts)
    near_parts = to_core(near_parts)
    far, far_near = hold(run, far, far_near)
    next(outer_way)
    second_kernel = heads_backward((2, 3), (unfolded_one, unfolded_one))
    far_input, sent, small_sums, attention_own = run(
        second_kernel, [low, low, sums, (weight_rows, BF16)], afar(far_qkv), afar(far), afar(far_near),
        sequences(2, 3), *own_weights, afar(far_log), afar(weight_sums), afar(small_sums), scalars=attention_scalars, scratch=rooms)
    far_near_input = to_core(sent)
    half = ((3 * width // 2, model), BF16)
    attention_way = chain(run, lambda: run(split_own, [half, half], attention_own, scalars=[ODD]))
    next(attention_way)
    small_own, small_across, small_near = run(
        collect_small, [small, small, ((2 * SMALL_ROWS, model), F32)], sum_0, sum_1, sum_2, sum_3,
        small_sums, first_sums, second_sums)
    small_near = to_core(small_near)
    out_own, out_across = run(add_out, [part, part], part_0, part_2, near_parts)
    next(outer_way)
    small_own, small_across = run(add_small, [small, small], small_own, small_across, small_near)
    last_rows = width + hidden - cut
    last_own, sent = run(
        pack_last, [((last_rows, model), BF16), ((last_rows + BIAS_ROWS, model), BF16)], out_own, inner_own,
        out_across, last_inner, small_across)
    last_x = to_x(sent)
    inner_way = way_of(inner_own, 0, cut, inner_x)
    next(inner_way)

    def input_steps():
        (sent,) = run(add_rows, [low], far_input, far_near_input)
        got = to_x(sent)
        yield
        return run(add_input, [Out(*full)], afar(partial), near_input, got)[0]

    ways = {
        OUTER: outer_way, ATTENTION: attention_way, INNER: inner_way,
        LAST: way_of(last_own, 0, last_rows, last_x, small_own), INPUT: input_steps(),
    }
    for number in STEPS:
        next(ways[number])

    def finish(way):
        while True:
            try:
                next(way)
            except StopIteration as stop:
                return stop.value

    finished = {}

    def results(number):
        if number not in finished:
            finished[number] = finish(ways[number])
        return finished[number]

    def place(numbers, begins, segments, *sizes):
        halves = [half for number in numbers for half in results(number)[0]]
        return run(place_rows(begins, segments), [Out((size, model), F32) for size in sizes], *halves, scalars=[ODD])

    (outer_weight_grad,) = place((OUTER,), (0,), ((0, hidden, 0, 0),), hidden)
    for number in LAST_STEPS:
        next(ways[number])
    input_grad = finish(ways[INPUT])
    query_grad, key_grad, value_grad = place(
        (ATTENTION,), (0,), [(i * width, width, i, 0) for i in range(3)], width, width, width)
    (most_inner,) = place((INNER,), (0,), ((0, cut, 0, 0),), hidden)
    _, (last_small,) = results(LAST)
    inner_bias_grad, query_bias_grad, value_bias_grad, *common = run(
        spread_small, [Out((size,), F32) for size in (hidden, width, width) + (model,) * 6], last_small)
    inner_weight_grad, out_grad = place_last(run, most_inner, cut, width, results(LAST)[0])
    return (
        layer_output,
        input_grad,
        query_grad.T,
        query_bias_grad,
        key_grad.T,
        value_grad.T,
        value_bias_grad,
        out_grad,
        *common[:3],
        inner_weight_grad,
        inner_bias_grad,
        outer_weight_grad,
        *common[3:],
    )


def solution(mesh):
    in_specs = (
        P("dp", None),
        P("dp"),
        P(None, "tp"),
        P("tp"),
        P(None, "tp"),
        P(None, "tp"),
        P("tp"),
        P("tp", None),
        P(),
        P(),
        P(),
        P(None, "tp"),
        P("tp"),
        P("tp", None),
        P(),
        P(),
        P(),
        P("dp", None),
    )
    out_specs = (
        P(("dp", "tp"), None),
        P(("dp", "tp"), None),
        P(None, "tp"),
        P("tp"),
        P(None, "tp"),
        P(None, "tp"),
        P("tp"),
        P("tp", None),
        P(),
        P(),
        P(),
        P(None, "tp"),
        P("tp"),
        P("tp", None),
        P(),
        P(),
        P(),
    )
    return jax.shard_map(
        on_device, mesh=mesh, in_specs=in_specs, out_specs=out_specs, check_vma=False
    )
```
